512 devices in a mesh: dp: 32 (over x, z), table: 16 (over y, core).
Axes of the slice: x: 4, y: 8, z: 8, core: 2. Of those that a mesh axis runs over, the one named last changes fastest.
Arguments:
- query_out: bfloat16 [65536, 256], P(('dp', 'table')), may hold values from -15 to 15
- item_out: bfloat16 [65536, 256], P(('dp', 'table')), may hold values from -12 to 12
- pooled_query: bfloat16 [65536, 128], P(('dp', 'table')), may hold values from -6 to 6
- pooled_item: bfloat16 [65536, 128], P(('dp', 'table')), may hold values from -6 to 6
- w_query: bfloat16 [128, 256], replicated, may hold values from -0.5 to 0.5
- w_item: bfloat16 [128, 256], replicated, may hold values from -0.5 to 0.5
- pair_weight: float32 [65536], P(('dp', 'table')), may hold values from 1 to 8
- slot_owner: int32 [65536, 16, 1], P(('dp', 'table')), may hold values from 0 to 15; in each aligned block of 2048 rows (0 to 2047, 2048 to 4095, ..., all dimensions but the last counted through in order) at most 256 rows name the same one
- slot_row: int32 [65536, 16, 1], P(('dp', 'table')), may hold values from 0 to 4095
Outputs:
- grad_table: float32 [65536, 128], P('table')
- grad_w_query: float32 [128, 256], replicated
- grad_w_item: float32 [128, 256], replicated
The draws below stay inside these ranges and needn't reach their ends.
Inputs may be any that keep to these rules, and one draw needn't show every extreme that they name: `slot_owner`: at most 256 of the 2048 slots of one device name the same owner, and some device has exactly 256 slots naming one owner.
All inputs are finite; a program needn't handle non-finite values.
Results may differ from the reference program's by a relative error of at most 0.023.
Values may be sent and summed in bfloat16 or wider, within the bound.
A program may use at most 64 MiB of HBM per device.

```python
import math
import jax
import jax.numpy as jnp
import numpy as np
from jax import lax

WIDTH = 256
EMB = 128
IDS_BAG = 8
B_DEV = 128
R_DEV = 4096
SLOTS_PAIR = 16
SLOTS_DEV = 2048
CAP = 256
GROUP = 4096
PAIRS = 65536
ROWS = 65536
N_DP = 32
N_TABLE = 16


def row_scales(key):
    return jnp.exp(jax.random.uniform(key, (PAIRS, 1), jnp.float32, math.log(0.3), math.log(1.5)))


def band_mask():
    return jnp.arange(WIDTH, dtype=jnp.int32) < WIDTH // 4


def common_vector(key, strength):
    dir_key, size_key = jax.random.split(key)
    flips = jax.random.bernoulli(dir_key, 0.5, (WIDTH,))
    common_sign = jnp.where(flips, 1.0, -1.0).astype(jnp.float32)
    common_size = jax.random.uniform(size_key, (WIDTH,), jnp.float32, 0.7, 1.3)
    return jnp.where(band_mask(), strength * common_sign * common_size, 0.0)


def draw_query_out(key, part):
    key = jax.random.fold_in(key, 11)
    base_key, scale_key, common_key = jax.random.split(key, 3)
    scales = row_scales(scale_key)
    common = common_vector(common_key, 2.0)
    values = jnp.clip(jax.random.normal(base_key, (PAIRS, WIDTH), jnp.float32), -4.0, 4.0) * scales + common[None, :]
    return values.astype(jnp.bfloat16)


def draw_item_out(key, part):
    key = jax.random.fold_in(key, 13)
    base_key, scale_key = jax.random.split(key)
    scales = row_scales(scale_key)
    damping = jnp.where(band_mask(), 0.1, 1.0).astype(jnp.float32)
    values = jnp.clip(jax.random.normal(base_key, (PAIRS, WIDTH), jnp.float32), -4.0, 4.0) * scales * damping[None, :]
    return values.astype(jnp.bfloat16)


def plant(drawn, stream_key, least, high):
    extent = drawn.shape
    spot = [jax.random.randint(jax.random.fold_in(stream_key, axis), (), 0, extent[axis]) for axis in range(len(extent))]
    drawn = drawn.at[tuple(spot)].set(least)
    longest = extent.index(max(extent))
    spot[longest] = (spot[longest] + 1) % extent[longest]
    return drawn.at[tuple(spot)].set(high)


def steps_of(key, extent, shards, smallest, high):
    gain, own = 1.0, jax.random.fold_in(key, 6)
    for dim, blocks in shards:
        draws = jnp.exp(jax.random.uniform(jax.random.fold_in(own, dim), (blocks,), jnp.float32, smallest / len(shards), high / len(shards)))
        gain = gain * jnp.repeat(draws, extent[dim] // blocks).reshape([-1 if axis == dim else 1 for axis in range(len(extent))])
    return gain


def shared_out(stream_key, own, number, rows, number_of, top, most, skew):
    ranking = jax.random.permutation(stream_key, number_of)
    heavy_load, usual = load_shares(number_of, rows * top, most, skew, True), load_shares(number_of, rows * top, most, skew, False)
    places = jnp.arange(number_of)

    def named(tallies, offset_by):
        used = int((tallies > 0).sum())
        fixed = max(1, used // 4)
        passed = fixed + (places - fixed + offset_by * (used - fixed)) % max(1, number_of - fixed)
        return jnp.zeros((number_of,), jnp.int32).at[ranking[jnp.where(places < fixed, places, passed)]].set(jnp.asarray(tallies, jnp.int32))

    tallies = jnp.where(number % 4 == 0, named(heavy_load, number // 4), named(usual, number - number // 4 - 1))
    mixed = jax.random.permutation(jax.random.fold_in(own, 3), number_of)
    giver, receiver = mixed[0:number_of // 2 * 2:2], mixed[1:number_of // 2 * 2:2]
    slack = jnp.minimum(tallies[giver] - 1, most - tallies[receiver]) // 2
    slack = jnp.where((giver == ranking[0]) | (receiver == ranking[0]) | (tallies[receiver] == 0), 0, jnp.maximum(slack, 0))
    passed = jax.random.randint(jax.random.fold_in(own, 4), (number_of // 2,), 0, 1 << 20) % (slack + 1)
    tallies = tallies.at[giver].add(-passed).at[receiver].add(passed)
    members = jnp.searchsorted(jnp.cumsum(tallies), jnp.arange(rows * top), side="right").astype(jnp.int32)
    grid = members.reshape(top, rows).T
    grid = grid[jax.random.permutation(jax.random.fold_in(own, 1), rows)]
    offset_by = jax.random.randint(jax.random.fold_in(own, 2), (rows, 1), 0, top)
    return jnp.take_along_axis(grid, (jnp.arange(top)[None, :] + offset_by) % top, axis=1)


def load_shares(amount, total, most, slope, full):
    portions = [(1 << 20) // math.isqrt(grade ** slope) + 1 for grade in range(1, amount + 1)]
    largest = most if full else min(most, max(-(-total // amount), total * portions[0] // sum(portions)))
    least = 1 if total - largest >= amount - 1 else 0
    holding, rest = [largest] + [least] * (amount - 1), total - largest - least * (amount - 1)
    while rest > 0:
        free = [i for i in range(1, amount) if holding[i] < largest] or [i for i in range(1, amount) if holding[i] < most]
        whole, remaining = sum([portions[i] for i in free]), rest
        for i in free:
            more = min(most - holding[i], max(1, remaining * portions[i] // whole), rest)
            holding[i] = holding[i] + more
            rest = rest - more
    return np.array(holding)


def normal_values(rng, extent, deviation, bound, cuts=(), held_as=jnp.bfloat16):
    factor_of = steps_of(rng, extent, cuts, -0.22, 0.18) if cuts else 1.0
    drawn = jax.random.normal(rng, extent, jnp.float32) * deviation * factor_of
    return jnp.minimum(jnp.maximum(drawn, -bound), bound).astype(held_as)


def setup_inputs(seed: int = 0) -> dict:
    seeds = jax.random.split(jax.random.key(seed), 10)
    query_out = draw_query_out(jax.random.fold_in(seeds[9], 71), 0)
    item_out = draw_item_out(jax.random.fold_in(seeds[9], 71), 0)
    pooled_query = normal_values(seeds[2], (PAIRS, EMB), 1.0, 6.0, ((0, 512),))
    pooled_item = normal_values(seeds[3], (PAIRS, EMB), 1.0, 6.0, ((0, 512),))
    w_query = normal_values(seeds[4], (EMB, WIDTH), EMB ** -0.5, 0.5)
    w_item = normal_values(seeds[5], (EMB, WIDTH), EMB ** -0.5, 0.5)
    pair_weight = jnp.clip(jnp.exp(math.log(8.0) - 2.0794415 * jax.random.uniform(seeds[6], (PAIRS,), jnp.float32) ** steps_of(seeds[6], (PAIRS,), ((0, 512),), -0.2, 0.2)), 1.0, 8.0)
    slot_owner_keys = jax.random.split(jax.random.fold_in(seeds[7], 1), PAIRS * SLOTS_PAIR // SLOTS_DEV)
    slot_owner_turns = jax.random.permutation(jax.random.fold_in(seeds[7], 3), PAIRS * SLOTS_PAIR // SLOTS_DEV)
    slot_owner = jax.vmap(lambda own, number: shared_out(jax.random.fold_in(seeds[7], 2), own, number, SLOTS_DEV, N_TABLE, 1, CAP, 2))(slot_owner_keys, slot_owner_turns).reshape((PAIRS, SLOTS_PAIR, 1))
    slot_row = plant(jax.random.randint(seeds[8], (PAIRS, SLOTS_PAIR, 1), 0, R_DEV), jax.random.fold_in(seeds[8], 1), 0, R_DEV - 1).astype(jnp.int32)
    return {"query_out": query_out, "item_out": item_out, "pooled_query": pooled_query, "pooled_item": pooled_item, "w_query": w_query, "w_item": w_item, "pair_weight": pair_weight, "slot_owner": slot_owner, "slot_row": slot_row}


def group_grads(operands):
    query_group, item_group, weight_group = operands
    logit_scale = 1.0 / math.sqrt(WIDTH)
    item_flat = item_group.reshape(GROUP, WIDTH)
    col_index = jnp.arange(GROUP, dtype=jnp.int32)

    def one_block(carry, inputs):
        query_block, weight_block, block_index = inputs
        logits = logit_scale * jnp.dot(query_block, item_flat.T, preferred_element_type=jnp.float32)
        row_max = lax.optimization_barrier(jnp.max(logits, axis=1))
        shifted = jnp.exp(logits - row_max[:, None])
        row_total = lax.optimization_barrier(jnp.sum(shifted, axis=1))
        positive = block_index * B_DEV + jnp.arange(B_DEV, dtype=jnp.int32)
        is_positive = (col_index[None, :] == positive[:, None]).astype(jnp.float32)
        grad_weights = (weight_block[:, None] * (shifted / row_total[:, None] - is_positive)).astype(jnp.bfloat16)
        query_grad = (logit_scale * jnp.dot(grad_weights, item_flat, preferred_element_type=jnp.float32)).astype(jnp.bfloat16)
        part_sum = (logit_scale * jnp.dot(grad_weights.T, query_block, preferred_element_type=jnp.float32)).astype(jnp.bfloat16)
        part_sum = lax.optimization_barrier(part_sum)
        return (carry + part_sum.astype(jnp.float32), query_grad)
    init = jnp.zeros((GROUP, WIDTH), jnp.float32)
    item_sum, query_grads = lax.scan(one_block, init, (query_group, weight_group, jnp.arange(N_DP, dtype=jnp.int32)))
    return (query_grads, item_sum.astype(jnp.bfloat16).reshape(N_DP, B_DEV, WIDTH))

def reference(query_out, item_out, pooled_query, pooled_item, w_query, w_item, pair_weight, slot_owner, slot_row):
    query_groups = query_out.reshape(N_DP, N_TABLE, B_DEV, WIDTH).transpose(1, 0, 2, 3)
    item_groups = item_out.reshape(N_DP, N_TABLE, B_DEV, WIDTH).transpose(1, 0, 2, 3)
    weight_groups = pair_weight.reshape(N_DP, N_TABLE, B_DEV).transpose(1, 0, 2)
    query_grads, item_grads = lax.map(group_grads, (query_groups, item_groups, weight_groups))
    query_grad = query_grads.transpose(1, 0, 2, 3).reshape(PAIRS, WIDTH)
    item_grad = item_grads.transpose(1, 0, 2, 3).reshape(PAIRS, WIDTH)
    query_pooled = jnp.dot(query_grad, w_query.T, preferred_element_type=jnp.float32).astype(jnp.bfloat16)
    item_pooled = jnp.dot(item_grad, w_item.T, preferred_element_type=jnp.float32).astype(jnp.bfloat16)
    grad_w_query = jnp.dot(pooled_query.T, query_grad, preferred_element_type=jnp.float32)
    grad_w_item = jnp.dot(pooled_item.T, item_grad, preferred_element_type=jnp.float32)
    table_ids = slot_owner[:, :, 0] * R_DEV + slot_row[:, :, 0]
    query_rows = query_pooled.astype(jnp.float32)
    item_rows = item_pooled.astype(jnp.float32)
    grad_table = jnp.zeros((ROWS, EMB), jnp.float32)
    for slot_index in range(SLOTS_PAIR):
        source = query_rows if slot_index < IDS_BAG else item_rows
        grad_table = grad_table.at[table_ids[:, slot_index]].add(source)
    return (grad_table, grad_w_query, grad_w_item)
```

```python
import math

import jax
import jax.numpy as jnp
from jax import lax
from jax.experimental import pallas as pl
from jax.experimental.pallas import tpu as pltpu
from jax.sharding import PartitionSpec as P

MESH = pl.DeviceIdType.MESH
F32, BF16, I32 = jnp.float32, jnp.bfloat16, jnp.int32
NX, NZ, NY = 4, 8, 8
B, W, E = 128, 256, 128
NT = 2 * NY
CAP = 256
SCALE = 1.0 / math.sqrt(W)
N_COPIES = 176

NN = (((1,), (0,)), ((), ()))
NT_DIMS = (((1,), (1,)), ((), ()))
TN = (((0,), (0,)), ((), ()))


def dot(a, b, dims=NN):
    return lax.dot_general(a, b, dims, preferred_element_type=F32)


def iota(shape, dim):
    return lax.broadcasted_iota(I32, shape, dim)


ARRIVE = (0, 2, 6, 1, 7, 3, 5, 4)
POS = {d: p for p, d in enumerate(ARRIVE)}
OWN = (0, 1, 2, 3, 4, 10, 11, 12)
SIB = (5, 6, 7, 8, 9, 13, 14, 15)
FIRST = 10 * CAP


def kernel(
    q_ref, it_ref, pq_ref, pi_ref, wq_ref, wi_ref, pw_ref, ow_ref, rw_ref,
    table_ref, gw_ref,
    pq, pi, wq, wi, pw, ow, rw,
    ibuf, qbuf, ebuf, gbuf, tops, totals, st_send, st_recv,
    gi_send, gi_relay, gi_half, gi_recv, gi_own, gq_send, gq_recv, gq_own,
    taken, slots_a, slots_b, list_send, list_recv, lists, low_row, onehot, select, factor, pooled, values,
    w_part, wx_recv, wz_send, wz_recv, wy_recv,
    t_own, t_send, tx_half, tx_relay, tx_recv, tz_own, tz_send, tz_recv, t_back,
    load_sem, send_sem, recv_sem,
):
    dp, tb = lax.axis_index("dp"), lax.axis_index("table")
    x, z = lax.div(dp, NZ), lax.rem(dp, NZ)
    y, core = lax.div(tb, 2), lax.rem(tb, 2)

    def at_x(d):
        return (lax.rem(x + d + NX, NX) * NZ + z, tb)

    def at_z(d):
        return (x * NZ + lax.rem(z + d + NZ, NZ), tb)

    def at_y(d):
        return (dp, lax.rem(y + d + NY, NY) * 2 + core)

    sibling = (dp, tb + 1 - 2 * core)
    partners = (
        [at_x(d) for d in range(1, NX)]
        + [at_z(d) for d in range(1, NZ)]
        + [at_y(d) for d in range(1, NY)]
        + [sibling]
    )
    barrier = pltpu.get_barrier_semaphore()
    for partner in partners:
        pl.semaphore_signal(barrier, inc=1, device_id=partner, device_id_type=MESH)
    loads = [
        pltpu.make_async_copy(src, dst, load_sem.at[i])
        for i, (src, dst) in enumerate((
            (it_ref, ibuf.at[pl.ds(0, B), :]),
            (q_ref, qbuf.at[pl.ds(0, B), :]),
            (ow_ref, ow),
            (rw_ref, rw),
            (pw_ref, pw),
            (pq_ref, pq),
            (pi_ref, pi),
            (wq_ref, wq),
            (wi_ref, wi),
        ))
    ]
    for load in loads:
        load.start()
    pl.semaphore_wait(barrier, len(partners))

    copies, drained = [], [0]

    def remote(index, src, dst, device):
        return pltpu.make_async_remote_copy(
            src_ref=src,
            dst_ref=dst,
            send_sem=send_sem.at[index],
            recv_sem=recv_sem.at[index],
            device_id=device,
            device_id_type=MESH,
        )

    def send(src, dst, device):
        copy = remote(len(copies), src, dst, device)
        copy.start()
        copies.append(copy)
        return copy

    def drain():
        for copy in copies[drained[0]:]:
            copy.wait_send()
        drained[0] = len(copies)

    def gather_start(slot, at, source=None):
        source = slot(0, None) if source is None else source
        return {d: send(source, slot(d % 8, None), at(d)) for d in (2, -2, 1, -1)}

    def gather_pass(got, slot, at):
        got[2].wait_recv()
        got[3] = send(slot(2, None), slot(3, None), at(1))
        got[4] = send(slot(2, 0), slot(4, 0), at(2))
        got[-2].wait_recv()
        got[-3] = send(slot(6, None), slot(5, None), at(-1))
        got[-4] = send(slot(6, 1), slot(4, 1), at(-2))

    def wait_for(got, *names):
        for name in names:
            got[name].wait_recv()

    def item_slot(d, half):
        if half is None:
            return ibuf.at[pl.ds(POS[d] * B, B), :]
        return ibuf.at[pl.ds(POS[d] * B + half * 64, 64), :]

    item_in = gather_start(item_slot, at_z, it_ref)
    query_in = {}
    for d in (1, 3, 2):
        query_in[d] = send(q_ref, qbuf.at[pl.ds(d * B, B), :], at_x(d))

    for load in loads:
        load.wait()
    owner_row = iota((NT, B), 0)
    hits = jnp.concatenate([(ow[k:k + 1, :] == owner_row).astype(F32) for k in range(16)], axis=0)
    before = (iota((B, 2 * B), 0) < iota((B, 2 * B), 1)).astype(BF16)
    counts = dot(hits.astype(BF16), before)
    at_row, at_col = iota((256, 256), 0), iota((256, 256), 1)
    earlier = jnp.logical_and(
        lax.bitwise_and(at_row, 15) == lax.bitwise_and(at_col, 15),
        lax.shift_right_logical(at_col, 4) < lax.shift_right_logical(at_row, 4),
    ).astype(BF16)
    taken[...] = (counts[:, 0:B] + dot(earlier, counts[:, B:].astype(BF16))) * hits
    list_row = iota((B, B), 0)
    list_owner, piece = lax.shift_right_logical(list_row, 3), lax.bitwise_and(list_row, 7)
    pair = iota((1, B), 1)
    place = iota((CAP, B), 0)

    def list_slot(k, _):
        lanes = pl.ds(pl.multiple_of(k * B, B), B)
        ranks = taken[pl.ds(pl.multiple_of(k * NT, NT), NT), :]
        rank = jnp.sum(ranks, axis=0, keepdims=True).astype(I32)
        slots_b[:, lanes] = (place == rank).astype(BF16)
        owner, row = ow[pl.ds(k, 1), :], rw[pl.ds(k, 1), :]
        part = jnp.where(
            piece == 0,
            pair + lax.div(k, 8) * B,
            jnp.where(
                piece == 1,
                lax.shift_right_logical(row, 8) + 1,
                jnp.where(piece == 2, lax.bitwise_and(row, 255), 0),
            ),
        )
        slots_a[:, lanes] = jnp.where(list_owner == owner, part, 0).astype(F32).astype(BF16)
        return 0

    lax.fori_loop(0, 16, list_slot, 0)
    list_send[...] = dot(slots_a[...], slots_b[...], NT_DIMS)
    list_in = {}
    for d in ARRIVE[1:]:
        to_y = lax.rem(y + d, NY)
        list_in[d] = send(
            list_send.at[pl.ds(pl.multiple_of(to_y * 16, 16), 16), :], list_recv.at[POS[d]], at_y(d)
        )
    list_recv[0] = list_send[pl.ds(pl.multiple_of(y * 16, 16), 16), :]

    gather_pass(item_in, item_slot, at_z)

    wait_for(query_in, 1, 3, 2)

    def logits(p, _):
        rows = pl.ds(pl.multiple_of(p * B, B), B)
        block = SCALE * dot(ibuf[rows, :], qbuf[...], NT_DIMS)
        top = jnp.max(block, axis=0, keepdims=True)
        block = jnp.exp(block - top)
        ebuf[rows, :] = block
        tops[pl.ds(p, 1), :] = top
        totals[pl.ds(p, 1), :] = jnp.sum(block, axis=0, keepdims=True)
        return 0

    wait_for(item_in, 1, -1)
    lax.fori_loop(0, 5, logits, 0)

    mine = pl.ds(pl.multiple_of(core * 8, 8), 8)
    other = pl.ds(pl.multiple_of((1 - core) * 8, 8), 8)
    for d in ARRIVE[1:]:
        list_in[d].wait_recv()
    list_sib = []
    for low, high in ((0, 5), (5, 8)):
        list_sib.append(send(
            list_recv.at[pl.ds(low, high - low), other, :],
            lists.at[pl.ds(SIB[low], high - low)],
            sibling,
        ))
        for p in range(low, high):
            lists[OWN[p]] = list_recv[p, mine, :]

    source_row = iota((2 * B, CAP), 0)
    low_row[...] = lax.bitwise_and(iota((1152, B), 0), 1023).astype(jnp.int16)

    def one_hots(s, _):
        entry = lists[s]
        row = (entry[1:2, :].astype(I32) - 1) * 256 + entry[2:3, :].astype(I32)
        select[s] = (entry[0:1, :].astype(I32) == source_row).astype(BF16)
        low = jnp.broadcast_to(lax.bitwise_and(row, 1023), (16, CAP)).astype(jnp.int16)
        for side in (0, 1):
            lanes = pl.ds(pl.multiple_of(s * CAP + side * B, B), B)
            same = low_row[...] == jnp.tile(low[:, side * B:(side + 1) * B], (72, 1))
            onehot[:, lanes] = jnp.where(same, jnp.ones((), BF16), jnp.zeros((), BF16))
        block = jnp.broadcast_to(lax.shift_right_arithmetic(row, 10), (16, CAP))
        for j in range(NX):
            factor[s, j] = (block == j).astype(BF16)
        return 0

    own_first, own_last = (0, 5), (10, 13)
    lax.fori_loop(*own_first, one_hots, 0)
    wait_for(item_in, 3, -3)
    lax.fori_loop(5, 7, logits, 0)
    lax.fori_loop(*own_last, one_hots, 0)
    wait_for(item_in, 4, -4)
    lax.fori_loop(7, 8, logits, 0)

    top = jnp.max(tops[...], axis=0, keepdims=True)
    total = jnp.sum(totals[...] * jnp.exp(tops[...] - top), axis=0, keepdims=True)
    weight = pw[...]
    for k in range(NX):
        st_send[k:k + 1, :] = top[:, k * B:(k + 1) * B]
        st_send[NX + k:NX + k + 1, :] = total[:, k * B:(k + 1) * B]
    st_send[8:16, :] = jnp.broadcast_to(weight, (8, B))
    stat_in = {d: send(st_send, st_recv.at[d], at_x(d)) for d in (2, 1, 3)}
    for copy in list_sib:
        copy.wait_recv()
    lax.fori_loop(5, 10, one_hots, 0)
    lax.fori_loop(13, 16, one_hots, 0)
    wait_for(stat_in, 1, 3, 2)
    maxima, factors = [], []
    for k in range(NX):
        part_tops, part_totals = [st_send[k:k + 1, :]], [st_send[NX + k:NX + k + 1, :]]
        for d in range(1, NX):
            j = (k - d) % NX
            part_tops.append(st_recv[d, j:j + 1, :])
            part_totals.append(st_recv[d, NX + j:NX + j + 1, :])
        row_max = part_tops[0]
        for t in part_tops[1:]:
            row_max = jnp.maximum(row_max, t)
        row_total = sum(s * jnp.exp(t - row_max) for t, s in zip(part_tops, part_totals))
        maxima.append(row_max)
        factors.append((weight if k == 0 else st_recv[k, 8:9, :]) / row_total)
    row_max, factors = jnp.concatenate(maxima, axis=1), jnp.concatenate(factors, axis=1)
    totals[...] = factors * jnp.exp(tops[...] - row_max)

    def item_terms(p):
        rows = pl.ds(pl.multiple_of(p * B, B), B)
        block = (ebuf[rows, :] * totals[pl.ds(p, 1), :]).astype(BF16)
        gbuf[rows, :] = block
        return SCALE * dot(block, qbuf[...])

    def far_terms(p, _):
        gi_send[p] = item_terms(p).astype(BF16)
        return 0

    def near_terms(p, _):
        gi_own[p] = item_terms(p)
        return 0

    lax.fori_loop(7, 8, far_terms, 0)
    half_in = [
        send(gi_send.at[7, pl.ds(0, 64), :], gi_half.at[0], at_z(2)),
        send(gi_send.at[7, pl.ds(64, 64), :], gi_half.at[1], at_z(-2)),
    ]
    lax.fori_loop(5, 7, far_terms, 0)
    relay_in = [
        send(gi_send.at[POS[5]], gi_relay.at[0], at_z(1)),
        send(gi_send.at[POS[3]], gi_relay.at[1], at_z(-1)),
    ]
    lax.fori_loop(3, 5, far_terms, 0)
    grad_in = {d: send(gi_send.at[POS[d]], gi_recv.at[POS[d]], at_z(-d)) for d in (7, 1)}
    lax.fori_loop(0, 3, near_terms, 0)
    same = iota((B, B), 0) == iota((B, B), 1)
    diagonal = ebuf[0:B, 0:B] * totals[0:1, 0:B] - jnp.where(same, weight, 0.0)
    gbuf[0:B, 0:B] = diagonal.astype(BF16)
    gi_own[0] = SCALE * dot(gbuf[0:B, :], qbuf[...])

    terms = SCALE * dot(gbuf[...], ibuf[...], TN)
    gq_own[...] = terms[0:B, :]
    for k in range(1, NX):
        gq_send[k] = terms[k * B:(k + 1) * B, :].astype(BF16)
    query_grad_in = {k: send(gq_send.at[k], gq_recv.at[k], at_x(-k)) for k in (2, 1, 3)}
    for side, (d, rows) in enumerate(((6, slice(0, 64)), (2, slice(64, 128)))):
        p = POS[d]
        relay_in[side].wait_recv()
        half_in[side].wait_recv()
        gi_own[p] += gi_relay[side].astype(F32)
        gi_own[p, rows, :] += gi_half[side].astype(F32)
        gi_send[p] = gi_own[p].astype(BF16)
        grad_in[d] = send(gi_send.at[p], gi_recv.at[p], at_z(-d))

    query_grad = gq_own[...]
    for k in (1, 3, 2):
        query_grad_in[k].wait_recv()
        query_grad += gq_recv[k].astype(F32)
    query_grad = query_grad.astype(BF16)

    pooled_in, pooled_sib = {}, {}

    def pooled_slot(half):
        def slot(d, rows):
            rows = pl.ds(0, E) if rows is None else pl.ds(rows * 64, 64)
            return pooled.at[OWN[POS[d]], rows, pl.ds(half * B, B)]

        return slot

    def to_sibling(half, low, high):
        lanes = pl.ds(half * B, B)
        pooled_sib[half, low] = send(
            pooled.at[pl.ds(OWN[low], high - low), :, lanes],
            pooled.at[pl.ds(SIB[low], high - low), :, lanes],
            sibling,
        )

    pooled[0, :, 0:B] = dot(wq[...], query_grad, NT_DIMS).astype(BF16)
    pooled_in[0] = gather_start(pooled_slot(0), at_y)
    to_sibling(0, 0, 1)
    w_part[0:B, :] = dot(pq[...], query_grad, TN)

    gather_pass(pooled_in[0], pooled_slot(0), at_y)
    wait_for(pooled_in[0], 1, -1)
    to_sibling(0, 1, 3)
    to_sibling(0, 3, 5)
    drain()

    item_grad = gi_own[0]
    for d in (1, 7, 2, 6):
        grad_in[d].wait_recv()
        item_grad += gi_recv[POS[d]].astype(F32)
    item_grad = item_grad.astype(BF16)
    pooled[0, :, B:] = dot(wi[...], item_grad, NT_DIMS).astype(BF16)
    pooled_in[1] = gather_start(pooled_slot(1), at_y)
    to_sibling(1, 0, 1)
    w_part[B:, :] = dot(pi[...], item_grad, TN)
    w_in = {}
    for d in (2, 1, 3):
        to_x = lax.rem(x + d, NX)
        w_in[d] = send(w_part.at[pl.ds(pl.multiple_of(to_x * 64, 64), 64), :], wx_recv.at[d], at_x(d))
    wait_for(pooled_in[0], 3, -3, 4, -4)
    to_sibling(0, 5, 8)

    def place_values(s, _):
        got = dot(pooled[s], select[s]).astype(BF16)
        lanes = pl.ds(pl.multiple_of(s * CAP, CAP), CAP)
        for j in range(NX):
            values[j * E:(j + 1) * E, lanes] = got * jnp.tile(factor[s, j], (8, 1))
        return 0

    def quarter_rows(p):
        return pl.ds(pl.multiple_of(lax.rem(z + 4 + p * (p + 1), NZ) * B, B), 256)

    def first_part(p, _):
        t_own[p] = dot(values[:, 0:FIRST], onehot[quarter_rows(p), 0:FIRST], NT_DIMS)
        return 0

    gather_pass(pooled_in[1], pooled_slot(1), at_y)
    wait_for(pooled_in[1], 1, -1)
    to_sibling(1, 1, 3)
    to_sibling(1, 3, 5)
    lax.fori_loop(0, 5, place_values, 0)
    for low in (0, 1, 3):
        pooled_sib[0, low].wait_recv()
        pooled_sib[1, low].wait_recv()
    lax.fori_loop(5, 10, place_values, 0)
    wait_for(pooled_in[1], 3, -3, 4, -4)
    to_sibling(1, 5, 8)
    lax.fori_loop(0, 2, first_part, 0)
    pooled_sib[0, 5].wait_recv()
    pooled_sib[1, 5].wait_recv()
    lax.fori_loop(10, 16, place_values, 0)

    half_base = len(copies)
    copies.extend([None] * 8)

    def half_copy(p, side):
        far = lax.rem(x + 2, NX)
        rows = pl.ds(pl.multiple_of(far * E + side * 64, 64), 64)
        return remote(
            half_base + 2 * p + side, t_send.at[p, rows, :], tx_half.at[p, side], at_x(1 - 2 * side)
        )

    def send_part(p, part):
        t_own[p] = part
        t_send[p] = part.astype(BF16)
        half_copy(p, 0).start()
        half_copy(p, 1).start()

    def last_part(p, _):
        send_part(p, t_own[p] + dot(values[:, FIRST:], onehot[quarter_rows(p), FIRST:], NT_DIMS))
        return 0

    def whole_part(p, _):
        send_part(p, dot(values[...], onehot[quarter_rows(p), :], NT_DIMS))
        return 0

    lax.fori_loop(0, 2, last_part, 0)
    lax.fori_loop(2, 3, whole_part, 0)
    for p in range(4):
        for side in (0, 1):
            copies[half_base + 2 * p + side] = half_copy(p, side)

    relay_in, tz_in = {}, {}

    def table_relay(p):
        for side, step in ((0, 1), (1, -1)):
            copies[half_base + 2 * p + side].wait_recv()
            near = lax.rem(x + step + NX, NX) * E
            for half in (0, 1):
                rows = slice(half * 64, half * 64 + 64)
                part = t_own[p, pl.ds(pl.multiple_of(near + half * 64, 64), 64), :]
                if half == side:
                    part += tx_half[p, side].astype(F32)
                tx_relay[p, side, rows, :] = part.astype(BF16)
            relay_in[p, side] = send(tx_relay.at[p, side], tx_recv.at[p, side], at_x(step))

    def table_sum(p):
        part = t_own[p, pl.ds(pl.multiple_of(x * E, E), E), :]
        for side in (0, 1):
            relay_in[p, side].wait_recv()
            part += tx_recv[p, side].astype(F32)
        for side in (0, 1):
            d = (4 + p * (p + 1)) % NZ + side
            if d == 0:
                tz_own[...] = part[:, 0:B]
            else:
                tz_send[d] = part[:, side * B:(side + 1) * B].astype(BF16)
                tz_in[d] = send(tz_send.at[d], tz_recv.at[d], at_z(d))

    table_relay(0)
    table_relay(1)
    lax.fori_loop(3, 4, whole_part, 0)
    table_sum(0)
    table_relay(2)
    table_sum(1)

    w_sum = w_part[pl.ds(pl.multiple_of(x * 64, 64), 64), :]
    for d in (1, 3, 2):
        w_in[d].wait_recv()
        w_sum += wx_recv[d]
    wz_send[...] = w_sum
    wz_in = {}
    for d in ARRIVE[1:]:
        to_z = lax.rem(z + d, NZ)
        wz_in[d] = send(wz_send.at[pl.ds(pl.multiple_of(to_z * 8, 8), 8), :], wz_recv.at[d], at_z(d))

    table_relay(3)

    w_sum = wz_send[pl.ds(pl.multiple_of(z * 8, 8), 8), :]
    for d in ARRIVE[1:]:
        wz_in[d].wait_recv()
        w_sum += wz_recv[d]
    wy_recv[0, 0] = w_sum
    wy_in = {d: send(wy_recv.at[0, 0], wy_recv.at[0, d], at_y(d)) for d in ARRIVE[1:]}

    table_sum(2)
    drain()
    table_sum(3)

    part = tz_own[...]
    for d in (4, 5, 6, 7, 2, 3, 1):
        tz_in[d].wait_recv()
        part += tz_recv[d].astype(F32)
    t_back[x, 0] = part.T.astype(BF16)

    def back_slot(d, half):
        if half is None:
            return t_back.at[x, POS[d]]
        return t_back.at[x, POS[d], pl.ds(half * 64, 64), :]

    back = gather_start(back_slot, at_z)
    near_in, far_in = {}, []

    def to_near(low, high):
        rows = t_back.at[x, pl.ds(low, high - low)]
        for side, step in ((0, 1), (1, -1)):
            near_in[low, side] = send(rows, rows, at_x(step))

    def to_far(low, high):
        middle = {1: None, 2: low + 1, 3: None}[high - low]
        for side, step in ((0, 1), (1, -1)):
            near_in[low, side].wait_recv()
            held = lax.rem(x - step + NX, NX)
            if middle is None:
                rows = t_back.at[held, pl.ds(low, high - low), pl.ds(side * 64, 64), :]
            else:
                rows = t_back.at[held, low + side]
            far_in.append(send(rows, rows, at_x(step)))

    to_near(0, 1)

    for d in ARRIVE[1:]:
        wy_in[d].wait_recv()
    wy_sib = send(wy_recv.at[0], wy_recv.at[1], sibling)
    gather_pass(back, back_slot, at_z)
    to_near(1, 3)
    to_far(0, 1)
    wait_for(back, 1, -1)
    to_near(3, 5)
    wy_sib.wait_recv()
    w_sum = wy_recv[0, 0]
    for d in range(1, NY):
        w_sum += wy_recv[0, d]
    for d in range(NY):
        w_sum += wy_recv[1, d]

    def w_rows(place):
        return gw_ref.at[pl.ds(pl.multiple_of(place * 8, 8), 8), :]

    gw_ref[pl.ds(pl.multiple_of(dp * 8, 8), 8), :] = w_sum
    w_back = {d: send(w_rows(dp), w_rows(dp), at_z(d)) for d in ARRIVE[1:]}
    to_far(1, 3)
    wait_for(back, 3, -3, 4, -4)
    to_near(5, 8)
    to_far(3, 5)

    def rows_of(far, p, d):
        place = far * NZ + lax.rem(z - d + NZ, NZ)
        table_ref[pl.ds(pl.multiple_of(place * B, B), B), :] = t_back[far, p]

    wait_for(w_back, *ARRIVE[1:])
    w_held = gw_ref.at[pl.ds(pl.multiple_of(x * 64, 64), 64), :]
    for step in (2, 1, 3):
        far_in.append(send(w_held, w_held, at_x(step)))
    to_far(5, 8)
    for p, d in enumerate(ARRIVE):
        rows_of(x, p, d)
        rows_of(lax.rem(x + 1, NX), p, d)
        rows_of(lax.rem(x + 3, NX), p, d)
    for copy in far_in:
        copy.wait_recv()
    for p, d in enumerate(ARRIVE):
        rows_of(lax.rem(x + 2, NX), p, d)
    drain()


def finish(table_ref, gw_ref, out_ref, gwq_ref, gwi_ref):
    out_ref[...] = table_ref[...].astype(F32)

    @pl.when(pl.program_id(0) == 0)
    def _():
        gwq_ref[...] = gw_ref[0:B, :]
        gwi_ref[...] = gw_ref[B:, :]


def on_device(q, it, pq, pi, wq, wi, pw, owner, row):
    def vmem(*shape, dtype=F32):
        return pltpu.VMEM(shape, dtype)

    table, gw = pl.pallas_call(
        kernel,
        out_shape=(
            jax.ShapeDtypeStruct((4096, E), BF16),
            jax.ShapeDtypeStruct((2 * B, W), F32),
        ),
        in_specs=[pl.BlockSpec(memory_space=pltpu.HBM)] * 9,
        out_specs=(pl.BlockSpec(memory_space=pltpu.VMEM),) * 2,
        scratch_shapes=[
            vmem(B, E, dtype=BF16),
            vmem(B, E, dtype=BF16),
            vmem(E, W, dtype=BF16),
            vmem(E, W, dtype=BF16),
            vmem(1, B),
            vmem(16, B, dtype=I32),
            vmem(16, B, dtype=I32),
            vmem(NZ * B, W, dtype=BF16),
            vmem(NX * B, W, dtype=BF16),
            vmem(NZ * B, NX * B),
            vmem(NZ * B, NX * B, dtype=BF16),
            vmem(NZ, NX * B),
            vmem(NZ, NX * B),
            vmem(16, B),
            vmem(NX, 16, B),
            vmem(NZ, B, W, dtype=BF16),
            vmem(2, B, W, dtype=BF16),
            vmem(2, 64, W, dtype=BF16),
            vmem(NZ, B, W, dtype=BF16),
            vmem(3, B, W),
            vmem(NX, B, W, dtype=BF16),
            vmem(NX, B, W, dtype=BF16),
            vmem(B, W),
            vmem(256, B),
            vmem(B, 16 * B, dtype=BF16),
            vmem(CAP, 16 * B, dtype=BF16),
            vmem(B, CAP),
            vmem(NY, 16, CAP),
            vmem(NT, 8, CAP),
            vmem(1152, B, dtype=jnp.int16),
            vmem(1152, NT * CAP, dtype=BF16),
            vmem(NT, 2 * B, CAP, dtype=BF16),
            vmem(NT, NX, 16, CAP, dtype=BF16),
            vmem(NT, E, 2 * B, dtype=BF16),
            vmem(NX * E, NT * CAP, dtype=BF16),
            vmem(2 * B, W),
            vmem(NX, 64, W),
            vmem(64, W),
            vmem(NZ, 8, W),
            vmem(2, NY, 8, W),
            vmem(4, NX * E, 256),
            vmem(4, NX * E, 256, dtype=BF16),
            vmem(4, 2, 64, 256, dtype=BF16),
            vmem(4, 2, E, 256, dtype=BF16),
            vmem(4, 2, E, 256, dtype=BF16),
            vmem(E, B),
            vmem(NZ, E, B, dtype=BF16),
            vmem(NZ, E, B, dtype=BF16),
            vmem(NX, NZ, B, E, dtype=BF16),
            pltpu.SemaphoreType.DMA((9,)),
            pltpu.SemaphoreType.DMA((N_COPIES,)),
            pltpu.SemaphoreType.DMA((N_COPIES,)),
        ],
        compiler_params=pltpu.CompilerParams(
            collective_id=0, has_side_effects=True, vmem_limit_bytes=40 * 1024 * 1024
        ),
    )(*[
        pltpu.with_memory_space_constraint(a, pltpu.HBM)
        for a in (
            q, it, pq, pi, wq, wi, pw.reshape(1, B), owner.reshape(B, 16).T, row.reshape(B, 16).T
        )
    ])
    whole_w = pl.BlockSpec((B, W), lambda i: (0, 0))
    return pl.pallas_call(
        finish,
        grid=(4,),
        out_shape=(
            jax.ShapeDtypeStruct((4096, E), F32),
            jax.ShapeDtypeStruct((B, W), F32),
            jax.ShapeDtypeStruct((B, W), F32),
        ),
        in_specs=[
            pl.BlockSpec((1024, E), lambda i: (i, 0)),
            pl.BlockSpec((2 * B, W), lambda i: (0, 0)),
        ],
        out_specs=(pl.BlockSpec((1024, E), lambda i: (i, 0)), whole_w, whole_w),
        compiler_params=pltpu.CompilerParams(vmem_limit_bytes=8 * 1024 * 1024),
    )(table, gw)


def solution(mesh):
    both = ("dp", "table")
    placed = (
        P(both, None),
        P(both, None),
        P(both, None),
        P(both, None),
        P(),
        P(),
        P(both),
        P(both, None, None),
        P(both, None, None),
    )
    return jax.shard_map(
        on_device,
        mesh=mesh,
        in_specs=placed,
        out_specs=(P("table", None), P(), P()),
        check_vma=False,
    )
```

```python
import math

import jax
import jax.numpy as jnp
from jax import lax
from jax.experimental import pallas as pl
from jax.experimental.pallas import tpu as pltpu
from jax.sharding import PartitionSpec as P

MESH = pl.DeviceIdType.MESH
F32, BF16, I32 = jnp.float32, jnp.bfloat16, jnp.int32
NX, NZ, NY = 4, 8, 8
B, W, E = 128, 256, 128
NT = 2 * NY
CAP = 256
SCALE = 1.0 / math.sqrt(W)
N_COPIES = 176

NN = (((1,), (0,)), ((), ()))
NT_DIMS = (((1,), (1,)), ((), ()))
TN = (((0,), (0,)), ((), ()))


def dot(a, b, dims=NN):
    return lax.dot_general(a, b, dims, preferred_element_type=F32)


def iota(shape, dim):
    return lax.broadcasted_iota(I32, shape, dim)


ARRIVE = (0, 2, 6, 1, 7, 3, 5, 4)
POS = {d: p for p, d in enumerate(ARRIVE)}
OWN = (0, 1, 2, 3, 4, 10, 11, 12)
SIB = (5, 6, 7, 8, 9, 13, 14, 15)
FIRST = 10 * CAP


def kernel(
    q_ref, it_ref, pq_ref, pi_ref, wq_ref, wi_ref, pw_ref, ow_ref, rw_ref,
    table_ref, gw_ref,
    pq, pi, wq, wi, pw, ow, rw,
    ibuf, qbuf, ebuf, gbuf, tops, totals, st_send, st_recv,
    gi_send, gi_relay, gi_half, gi_recv, gi_own, gq_send, gq_recv, gq_own,
    taken, slots_a, slots_b, list_send, list_recv, lists, onehot, select, factor, pooled, values,
    w_part, wx_recv, wz_send, wz_recv, wy_recv,
    t_own, t_send, tx_half, tx_relay, tx_recv, tz_first, tz_own, tz_send, tz_half, tz_relay, tz_back, tz_recv,
    lz_half, lz_relay, lz_own, lz_send, lz_recv, lx_send, lx_recv, t_back, l_back,
    load_sem, send_sem, recv_sem,
):
    dp, tb = lax.axis_index("dp"), lax.axis_index("table")
    x, z = lax.div(dp, NZ), lax.rem(dp, NZ)
    y, core = lax.div(tb, 2), lax.rem(tb, 2)

    def at_x(d):
        return (lax.rem(x + d + NX, NX) * NZ + z, tb)

    def at_z(d):
        return (x * NZ + lax.rem(z + d + NZ, NZ), tb)

    def at_y(d):
        return (dp, lax.rem(y + d + NY, NY) * 2 + core)

    sibling = (dp, tb + 1 - 2 * core)
    partners = (
        [at_x(d) for d in range(1, NX)]
        + [at_z(d) for d in range(1, NZ)]
        + [at_y(d) for d in range(1, NY)]
        + [sibling]
    )
    barrier = pltpu.get_barrier_semaphore()
    for partner in partners:
        pl.semaphore_signal(barrier, inc=1, device_id=partner, device_id_type=MESH)
    loads = [
        pltpu.make_async_copy(src, dst, load_sem.at[i])
        for i, (src, dst) in enumerate((
            (it_ref, ibuf.at[pl.ds(0, B), :]),
            (q_ref, qbuf.at[pl.ds(0, B), :]),
            (ow_ref, ow),
            (rw_ref, rw),
            (pw_ref, pw),
            (pq_ref, pq),
            (pi_ref, pi),
            (wq_ref, wq),
            (wi_ref, wi),
        ))
    ]
    for load in loads:
        load.start()
    pl.semaphore_wait(barrier, len(partners))

    copies, drained = [], [0]

    def remote(index, src, dst, device):
        return pltpu.make_async_remote_copy(
            src_ref=src,
            dst_ref=dst,
            send_sem=send_sem.at[index],
            recv_sem=recv_sem.at[index],
            device_id=device,
            device_id_type=MESH,
        )

    def send(src, dst, device):
        copy = remote(len(copies), src, dst, device)
        copy.start()
        copies.append(copy)
        return copy

    def drain():
        for copy in copies[drained[0]:]:
            copy.wait_send()
        drained[0] = len(copies)

    def gather_start(slot, at, source=None):
        source = slot(0, None) if source is None else source
        return {d: send(source, slot(d % 8, None), at(d)) for d in (2, -2, 1, -1)}

    def gather_pass(got, slot, at):
        got[2].wait_recv()
        got[3] = send(slot(2, None), slot(3, None), at(1))
        got[4] = send(slot(2, 0), slot(4, 0), at(2))
        got[-2].wait_recv()
        got[-3] = send(slot(6, None), slot(5, None), at(-1))
        got[-4] = send(slot(6, 1), slot(4, 1), at(-2))

    def wait_for(got, *names):
        for name in names:
            got[name].wait_recv()

    def item_slot(d, half):
        if half is None:
            return ibuf.at[pl.ds(POS[d] * B, B), :]
        return ibuf.at[pl.ds(POS[d] * B + half * 64, 64), :]

    item_in = gather_start(item_slot, at_z, it_ref)
    query_in = {}
    for d in (1, 3, 2):
        query_in[d] = send(q_ref, qbuf.at[pl.ds(d * B, B), :], at_x(d))

    for load in loads:
        load.wait()
    owner_row = iota((NT, B), 0)
    hits = jnp.concatenate([(ow[k:k + 1, :] == owner_row).astype(F32) for k in range(16)], axis=0)
    before = (iota((B, 2 * B), 0) < iota((B, 2 * B), 1)).astype(BF16)
    counts = dot(hits.astype(BF16), before)
    at_row, at_col = iota((256, 256), 0), iota((256, 256), 1)
    earlier = jnp.logical_and(
        lax.bitwise_and(at_row, 15) == lax.bitwise_and(at_col, 15),
        lax.shift_right_logical(at_col, 4) < lax.shift_right_logical(at_row, 4),
    ).astype(BF16)
    taken[...] = (counts[:, 0:B] + dot(earlier, counts[:, B:].astype(BF16))) * hits
    list_row = iota((B, B), 0)
    list_owner, piece = lax.shift_right_logical(list_row, 3), lax.bitwise_and(list_row, 7)
    pair = iota((1, B), 1)
    place = iota((CAP, B), 0)

    def list_slot(k, _):
        lanes = pl.ds(pl.multiple_of(k * B, B), B)
        ranks = taken[pl.ds(pl.multiple_of(k * NT, NT), NT), :]
        rank = jnp.sum(ranks, axis=0, keepdims=True).astype(I32)
        slots_b[:, lanes] = (place == rank).astype(BF16)
        owner, row = ow[pl.ds(k, 1), :], rw[pl.ds(k, 1), :]
        part = jnp.where(
            piece == 0,
            pair + lax.div(k, 8) * B,
            jnp.where(
                piece == 1,
                lax.shift_right_logical(row, 8) + 1,
                jnp.where(piece == 2, lax.bitwise_and(row, 255), 0),
            ),
        )
        slots_a[:, lanes] = jnp.where(list_owner == owner, part, 0).astype(F32).astype(BF16)
        return 0

    lax.fori_loop(0, 16, list_slot, 0)
    list_send[...] = dot(slots_a[...], slots_b[...], NT_DIMS)
    list_in = {}
    for d in ARRIVE[1:]:
        to_y = lax.rem(y + d, NY)
        list_in[d] = send(
            list_send.at[pl.ds(pl.multiple_of(to_y * 16, 16), 16), :], list_recv.at[POS[d]], at_y(d)
        )
    list_recv[0] = list_send[pl.ds(pl.multiple_of(y * 16, 16), 16), :]

    gather_pass(item_in, item_slot, at_z)

    wait_for(query_in, 1, 3, 2)

    def logits(p, _):
        rows = pl.ds(pl.multiple_of(p * B, B), B)
        block = SCALE * dot(ibuf[rows, :], qbuf[...], NT_DIMS)
        top = jnp.max(block, axis=0, keepdims=True)
        block = jnp.exp(block - top)
        ebuf[rows, :] = block
        tops[pl.ds(p, 1), :] = top
        totals[pl.ds(p, 1), :] = jnp.sum(block, axis=0, keepdims=True)
        return 0

    wait_for(item_in, 1, -1)
    lax.fori_loop(0, 5, logits, 0)

    wait_for(item_in, 3, -3)
    lax.fori_loop(5, 7, logits, 0)
    wait_for(item_in, 4, -4)
    lax.fori_loop(7, 8, logits, 0)

    top = jnp.max(tops[...], axis=0, keepdims=True)
    total = jnp.sum(totals[...] * jnp.exp(tops[...] - top), axis=0, keepdims=True)
    weight = pw[...]
    for k in range(NX):
        st_send[k:k + 1, :] = top[:, k * B:(k + 1) * B]
        st_send[NX + k:NX + k + 1, :] = total[:, k * B:(k + 1) * B]
    st_send[8:16, :] = jnp.broadcast_to(weight, (8, B))
    stat_in = {d: send(st_send, st_recv.at[d], at_x(d)) for d in (2, 1, 3)}
    wait_for(stat_in, 1, 3, 2)
    maxima, factors = [], []
    for k in range(NX):
        part_tops, part_totals = [st_send[k:k + 1, :]], [st_send[NX + k:NX + k + 1, :]]
        for d in range(1, NX):
            j = (k - d) % NX
            part_tops.append(st_recv[d, j:j + 1, :])
            part_totals.append(st_recv[d, NX + j:NX + j + 1, :])
        row_max = part_tops[0]
        for t in part_tops[1:]:
            row_max = jnp.maximum(row_max, t)
        row_total = sum(s * jnp.exp(t - row_max) for t, s in zip(part_tops, part_totals))
        maxima.append(row_max)
        factors.append((weight if k == 0 else st_recv[k, 8:9, :]) / row_total)
    row_max, factors = jnp.concatenate(maxima, axis=1), jnp.concatenate(factors, axis=1)
    totals[...] = factors * jnp.exp(tops[...] - row_max)

    def item_terms(p):
        rows = pl.ds(pl.multiple_of(p * B, B), B)
        block = (ebuf[rows, :] * totals[pl.ds(p, 1), :]).astype(BF16)
        gbuf[rows, :] = block
        return SCALE * dot(block, qbuf[...])

    def far_terms(p, _):
        gi_send[p] = item_terms(p).astype(BF16)
        return 0

    def near_terms(p, _):
        gi_own[p] = item_terms(p)
        return 0

    lax.fori_loop(7, 8, far_terms, 0)
    half_in = [
        send(gi_send.at[7, pl.ds(0, 64), :], gi_half.at[0], at_z(2)),
        send(gi_send.at[7, pl.ds(64, 64), :], gi_half.at[1], at_z(-2)),
    ]
    lax.fori_loop(5, 7, far_terms, 0)
    relay_in = [
        send(gi_send.at[POS[5]], gi_relay.at[0], at_z(1)),
        send(gi_send.at[POS[3]], gi_relay.at[1], at_z(-1)),
    ]
    lax.fori_loop(3, 5, far_terms, 0)
    grad_in = {d: send(gi_send.at[POS[d]], gi_recv.at[POS[d]], at_z(-d)) for d in (7, 1)}
    lax.fori_loop(0, 3, near_terms, 0)
    same = iota((B, B), 0) == iota((B, B), 1)
    diagonal = ebuf[0:B, 0:B] * totals[0:1, 0:B] - jnp.where(same, weight, 0.0)
    gbuf[0:B, 0:B] = diagonal.astype(BF16)
    gi_own[0] = SCALE * dot(gbuf[0:B, :], qbuf[...])

    terms = SCALE * dot(gbuf[...], ibuf[...], TN)
    gq_own[...] = terms[0:B, :]
    for k in range(1, NX):
        gq_send[k] = terms[k * B:(k + 1) * B, :].astype(BF16)
    query_grad_in = {k: send(gq_send.at[k], gq_recv.at[k], at_x(-k)) for k in (2, 1, 3)}
    for side, (d, rows) in enumerate(((6, slice(0, 64)), (2, slice(64, 128)))):
        p = POS[d]
        relay_in[side].wait_recv()
        half_in[side].wait_recv()
        gi_own[p] += gi_relay[side].astype(F32)
        gi_own[p, rows, :] += gi_half[side].astype(F32)
        gi_send[p] = gi_own[p].astype(BF16)
        grad_in[d] = send(gi_send.at[p], gi_recv.at[p], at_z(-d))

    mine = pl.ds(pl.multiple_of(core * 8, 8), 8)
    other = pl.ds(pl.multiple_of((1 - core) * 8, 8), 8)
    for d in ARRIVE[1:]:
        list_in[d].wait_recv()
    list_sib = []
    for low, high in ((0, 5), (5, 8)):
        list_sib.append(send(
            list_recv.at[pl.ds(low, high - low), other, :],
            lists.at[pl.ds(SIB[low], high - low)],
            sibling,
        ))
        for p in range(low, high):
            lists[OWN[p]] = list_recv[p, mine, :]

    query_grad = gq_own[...]
    for k in (1, 3, 2):
        query_grad_in[k].wait_recv()
        query_grad += gq_recv[k].astype(F32)
    query_grad = query_grad.astype(BF16)

    pooled_in, pooled_sib = {}, {}

    def pooled_slot(half):
        def slot(d, rows):
            if rows is None:
                return pooled.at[half, OWN[POS[d]]]
            return pooled.at[half, OWN[POS[d]], pl.ds(rows * 64, 64), :]

        return slot

    def to_sibling(half, low, high):
        pooled_sib[half, low] = send(
            pooled.at[half, pl.ds(OWN[low], high - low)], pooled.at[half, pl.ds(SIB[low], high - low)], sibling
        )

    pooled[0, 0] = dot(wq[...], query_grad, NT_DIMS).astype(BF16)
    pooled_in[0] = gather_start(pooled_slot(0), at_y)
    to_sibling(0, 0, 1)
    w_part[0:B, :] = dot(pq[...], query_grad, TN)

    source_row = iota((2 * B, CAP), 0)
    low_row = lax.bitwise_and(iota((1152, CAP), 0), 1023)

    def one_hots(s, _):
        entry = lists[s]
        row = (entry[1:2, :].astype(I32) - 1) * 256 + entry[2:3, :].astype(I32)
        select[s] = (entry[0:1, :].astype(I32) == source_row).astype(BF16)
        lanes = pl.ds(pl.multiple_of(s * CAP, CAP), CAP)
        onehot[:, lanes] = (lax.bitwise_and(row, 1023) == low_row).astype(BF16)
        block = jnp.broadcast_to(lax.shift_right_arithmetic(row, 10), (16, CAP))
        for j in range(NX):
            factor[s, j] = (block == j).astype(BF16)
        return 0

    lax.fori_loop(0, 5, one_hots, 0)
    gather_pass(pooled_in[0], pooled_slot(0), at_y)
    wait_for(pooled_in[0], 1, -1)
    to_sibling(0, 1, 3)
    to_sibling(0, 3, 5)
    for copy in list_sib:
        copy.wait_recv()
    lax.fori_loop(5, 16, one_hots, 0)
    drain()

    item_grad = gi_own[0]
    for d in (1, 7, 2, 6):
        grad_in[d].wait_recv()
        item_grad += gi_recv[POS[d]].astype(F32)
    item_grad = item_grad.astype(BF16)
    pooled[1, 0] = dot(wi[...], item_grad, NT_DIMS).astype(BF16)
    pooled_in[1] = gather_start(pooled_slot(1), at_y)
    to_sibling(1, 0, 1)
    w_part[B:, :] = dot(pi[...], item_grad, TN)
    w_in = {}
    for d in (2, 1, 3):
        to_x = lax.rem(x + d, NX)
        w_in[d] = send(w_part.at[pl.ds(pl.multiple_of(to_x * 64, 64), 64), :], wx_recv.at[d], at_x(d))
    wait_for(pooled_in[0], 3, -3, 4, -4)
    to_sibling(0, 5, 8)

    def place_values(s, _):
        got = (dot(pooled[0, s], select[s, 0:B, :]) + dot(pooled[1, s], select[s, B:, :])).astype(BF16)
        lanes = pl.ds(pl.multiple_of(s * CAP, CAP), CAP)
        for j in range(NX):
            values[j * E:(j + 1) * E, lanes] = got * jnp.tile(factor[s, j], (8, 1))
        return 0

    def quarter_rows(p):
        return pl.ds(pl.multiple_of(lax.rem(z + 4 + 3 * p * (p + 1), NZ) * B, B), 256)

    def first_part(p, _):
        part = dot(values[:, 0:FIRST], onehot[quarter_rows(p), 0:FIRST], NT_DIMS)
        t_own[p] = part.reshape(NX, E, 256)
        return 0

    gather_pass(pooled_in[1], pooled_slot(1), at_y)
    wait_for(pooled_in[1], 1, -1)
    to_sibling(1, 1, 3)
    to_sibling(1, 3, 5)
    lax.fori_loop(0, 5, place_values, 0)
    for low in (0, 1, 3):
        pooled_sib[0, low].wait_recv()
        pooled_sib[1, low].wait_recv()
    lax.fori_loop(5, 10, place_values, 0)

    w_sum = w_part[pl.ds(pl.multiple_of(x * 64, 64), 64), :]
    for d in (1, 3, 2):
        w_in[d].wait_recv()
        w_sum += wx_recv[d]
    wz_send[...] = w_sum
    wz_in = {}
    for d in ARRIVE[1:]:
        to_z = lax.rem(z + d, NZ)
        wz_in[d] = send(wz_send.at[pl.ds(pl.multiple_of(to_z * 8, 8), 8), :], wz_recv.at[d], at_z(d))

    lax.fori_loop(0, 2, first_part, 0)
    wait_for(pooled_in[1], 3, -3, 4, -4)
    to_sibling(1, 5, 8)
    lax.fori_loop(10, 13, place_values, 0)
    lax.fori_loop(2, 4, first_part, 0)
    pooled_sib[0, 5].wait_recv()
    pooled_sib[1, 5].wait_recv()
    lax.fori_loop(13, 16, place_values, 0)

    half_base = len(copies)
    copies.extend([None] * 8)

    def half_copy(p, side):
        return remote(
            half_base + 2 * p + side,
            t_send.at[p, lax.rem(x + 2, NX), pl.ds(side * 48, 48), :],
            tx_half.at[p, side],
            at_x(1 - 2 * side),
        )

    def send_part(p, part):
        part = t_own[p] + part.reshape(NX, E, 256)
        t_own[p] = part
        t_send[p] = part.astype(BF16)
        half_copy(p, 0).start()
        half_copy(p, 1).start()

    def last_part(p, _):
        send_part(p, dot(values[:, FIRST:], onehot[quarter_rows(p), FIRST:], NT_DIMS))
        return 0

    lax.fori_loop(0, 4, last_part, 0)
    for p in range(4):
        for side in (0, 1):
            copies[half_base + 2 * p + side] = half_copy(p, side)

    def low_columns(p, side):
        return t_send.at[p, :, pl.ds(96, 32), pl.ds(side * B, B)]

    low_half = [
        send(t_send.at[0, pl.ds(2 * side, 2), pl.ds(96, 32), pl.ds(0, B)], lz_half.at[side], at_z(2 - 4 * side))
        for side in (0, 1)
    ]
    low_relay = [
        send(low_columns(1, 1), lz_relay.at[0], at_z(1)),
        send(low_columns(0, 1), lz_relay.at[1], at_z(-1)),
    ]
    low_in = [
        send(low_columns(3, 1), lz_recv.at[0], at_z(1)),
        send(low_columns(2, 1), lz_recv.at[1], at_z(-1)),
    ]

    def low_pass():
        for side in (0, 1):
            low_relay[side].wait_recv()
            low_half[side].wait_recv()
            lz_own[side] = t_own[1 + side, :, 96:, 0:B] + lz_relay[side].astype(F32)
            pair_of = slice(2 * side, 2 * side + 2)
            lz_own[side, pair_of] += lz_half[side].astype(F32)
            lz_send[side] = lz_own[side].astype(BF16)
            low_in.append(send(lz_send.at[side], lz_recv.at[2 + side], at_z(2 - 4 * side)))

    low_x = {}

    def low_sum():
        part = t_own[3, :, 96:, 0:B]
        for k in range(4):
            low_in[k].wait_recv()
            part += lz_recv[k].astype(F32)
        lz_own[2] = part
        lx_send[...] = part.astype(BF16)
        for d in (2, 1, 3):
            low_x[d] = send(lx_send.at[lax.rem(x + d, NX)], lx_recv.at[d], at_x(d))

    relay_in, tz_half_in, tz_relay_in, tz_in = {}, {}, {}, {}

    def table_relay(p):
        for side, step in ((0, 1), (1, -1)):
            copies[half_base + 2 * p + side].wait_recv()
            near = lax.rem(x + step + NX, NX)
            for half in (0, 1):
                rows = slice(half * 48, half * 48 + 48)
                part = t_own[p, near, rows, :]
                if half == side:
                    part += tx_half[p, side].astype(F32)
                tx_relay[p, side, rows, :] = part.astype(BF16)
            relay_in[p, side] = send(tx_relay.at[p, side], tx_recv.at[p, side], at_x(step))

    def table_sum(p):
        part = t_own[p, x, 0:96, :]
        for side in (0, 1):
            relay_in[p, side].wait_recv()
            part += tx_recv[p, side].astype(F32)
        tz_send[p] = part[:, B:].astype(BF16)
        if p == 0:
            tz_first[...] = part[:, 0:B].astype(BF16)
            for side in (0, 1):
                tz_half_in[side] = send(
                    tz_first.at[pl.ds(side * 48, 48), :], tz_half.at[side], at_z(2 - 4 * side)
                )
        else:
            tz_own[p - 1] = part[:, 0:B]
        if p < 2:
            tz_relay_in[1 - p] = send(tz_send.at[p], tz_relay.at[1 - p], at_z(2 * p - 1))
        else:
            tz_in[3 - p] = send(tz_send.at[p], tz_recv.at[3 - p], at_z(2 * p - 5))

    def table_pass():
        for side in (0, 1):
            tz_relay_in[side].wait_recv()
            tz_half_in[side].wait_recv()
            rows = slice(side * 48, side * 48 + 48)
            tz_own[side] += tz_relay[side].astype(F32)
            tz_own[side, rows, :] += tz_half[side].astype(F32)
            tz_back[side] = tz_own[side].astype(BF16)
            tz_in[2 + side] = send(tz_back.at[side], tz_recv.at[2 + side], at_z(2 - 4 * side))

    w_sum = wz_send[pl.ds(pl.multiple_of(z * 8, 8), 8), :]
    for d in ARRIVE[1:]:
        wz_in[d].wait_recv()
        w_sum += wz_recv[d]
    wy_recv[0, 0] = w_sum
    wy_in = {d: send(wy_recv.at[0, 0], wy_recv.at[0, d], at_y(d)) for d in ARRIVE[1:]}

    table_relay(0)
    table_relay(1)
    table_sum(0)
    low_pass()

    for d in ARRIVE[1:]:
        wy_in[d].wait_recv()
    wy_sib = send(wy_recv.at[0], wy_recv.at[1], sibling)
    table_relay(2)
    table_sum(1)

    wy_sib.wait_recv()
    w_sum = wy_recv[0, 0]
    for d in range(1, NY):
        w_sum += wy_recv[0, d]
    for d in range(NY):
        w_sum += wy_recv[1, d]

    def w_rows(place):
        return gw_ref.at[pl.ds(pl.multiple_of(place * 8, 8), 8), :]

    gw_ref[pl.ds(pl.multiple_of(dp * 8, 8), 8), :] = w_sum
    w_back = {d: send(w_rows(dp), w_rows(dp), at_z(d)) for d in ARRIVE[1:]}

    table_relay(3)
    table_sum(2)
    low_sum()
    table_pass()
    table_sum(3)
    drain()

    low = lz_own[2, x]
    for d in (1, 3, 2):
        low_x[d].wait_recv()
        low += lx_recv[d].astype(F32)
    part = tz_own[2]
    for k in (1, 0, 2, 3):
        tz_in[k].wait_recv()
        part += tz_recv[k].astype(F32)
    rows = jnp.concatenate([part, low], axis=0).T.astype(BF16)
    t_back[x, 0] = rows[0:96]
    l_back[0, x] = rows[96:]

    def back_slot(d, half):
        if half is None:
            return t_back.at[x, POS[d]]
        return t_back.at[x, POS[d], pl.ds(half * 48, 48), :]

    def low_slot(d, half):
        if half is None:
            return l_back.at[POS[d]]
        return l_back.at[POS[d], pl.ds(2 * half, 2)]

    back = gather_start(back_slot, at_z)
    low_back = [send(l_back.at[0, x], l_back.at[0, x], at_x(d)) for d in (2, 1, 3)]
    near_in, far_in = {}, []

    def to_near(low, high):
        rows = t_back.at[x, pl.ds(low, high - low)]
        for side, step in ((0, 1), (1, -1)):
            near_in[low, side] = send(rows, rows, at_x(step))

    def to_far(low, high):
        middle = {1: None, 2: low + 1, 3: None}[high - low]
        for side, step in ((0, 1), (1, -1)):
            near_in[low, side].wait_recv()
            held = lax.rem(x - step + NX, NX)
            if middle is None:
                rows = t_back.at[held, pl.ds(low, high - low), pl.ds(side * 48, 48), :]
            else:
                rows = t_back.at[held, low + side]
            far_in.append(send(rows, rows, at_x(step)))

    to_near(0, 1)

    wait_for(w_back, *ARRIVE[1:])
    w_held = gw_ref.at[pl.ds(pl.multiple_of(x * 64, 64), 64), :]
    for step in (2, 1, 3):
        far_in.append(send(w_held, w_held, at_x(step)))


    gather_pass(back, back_slot, at_z)
    to_near(1, 3)
    for copy in low_back:
        copy.wait_recv()
    low_back = gather_start(low_slot, at_z)
    to_far(0, 1)
    wait_for(back, 1, -1)
    to_near(3, 5)
    to_far(1, 3)
    wait_for(back, 3, -3, 4, -4)
    to_near(5, 8)
    gather_pass(low_back, low_slot, at_z)
    to_far(3, 5)

    def rows_of(far, p, d):
        place = (far * NZ + lax.rem(z - d + NZ, NZ)) * B
        table_ref[pl.ds(pl.multiple_of(place, B), 96), :] = t_back[far, p]

    def low_rows_of(p, d):
        for far in range(NX):
            place = (far * NZ + lax.rem(z - d + NZ, NZ)) * B + 96
            table_ref[pl.ds(pl.multiple_of(place, 32), 32), :] = l_back[p, far]

    to_far(5, 8)
    for p, d in enumerate(ARRIVE):
        rows_of(x, p, d)
        rows_of(lax.rem(x + 1, NX), p, d)
        rows_of(lax.rem(x + 3, NX), p, d)
    wait_for(low_back, 1, -1, 3, -3, 4, -4)
    for p, d in enumerate(ARRIVE):
        low_rows_of(p, d)
    drain()
    for copy in far_in:
        copy.wait_recv()
    for p, d in enumerate(ARRIVE):
        rows_of(lax.rem(x + 2, NX), p, d)
    drain()


def finish(table_ref, gw_ref, out_ref, gwq_ref, gwi_ref, wide, sem):
    copies = [
        pltpu.make_async_copy(gw_ref.at[pl.ds(0, B), :], gwq_ref, sem.at[8]),
        pltpu.make_async_copy(gw_ref.at[pl.ds(B, B), :], gwi_ref, sem.at[9]),
    ]
    for copy in copies:
        copy.start()
    for i in range(8):
        wide[i] = table_ref[i * 512:(i + 1) * 512, :].astype(F32)
        copies.append(pltpu.make_async_copy(wide.at[i], out_ref.at[pl.ds(i * 512, 512), :], sem.at[i]))
        copies[-1].start()
    for copy in copies:
        copy.wait()


def on_device(q, it, pq, pi, wq, wi, pw, owner, row):
    def vmem(*shape, dtype=F32):
        return pltpu.VMEM(shape, dtype)

    table, gw = pl.pallas_call(
        kernel,
        out_shape=(
            jax.ShapeDtypeStruct((4096, E), BF16),
            jax.ShapeDtypeStruct((2 * B, W), F32),
        ),
        in_specs=[pl.BlockSpec(memory_space=pltpu.HBM)] * 9,
        out_specs=(pl.BlockSpec(memory_space=pltpu.VMEM),) * 2,
        scratch_shapes=[
            vmem(B, E, dtype=BF16),
            vmem(B, E, dtype=BF16),
            vmem(E, W, dtype=BF16),
            vmem(E, W, dtype=BF16),
            vmem(1, B),
            vmem(16, B, dtype=I32),
            vmem(16, B, dtype=I32),
            vmem(NZ * B, W, dtype=BF16),
            vmem(NX * B, W, dtype=BF16),
            vmem(NZ * B, NX * B),
            vmem(NZ * B, NX * B, dtype=BF16),
            vmem(NZ, NX * B),
            vmem(NZ, NX * B),
            vmem(16, B),
            vmem(NX, 16, B),
            vmem(NZ, B, W, dtype=BF16),
            vmem(2, B, W, dtype=BF16),
            vmem(2, 64, W, dtype=BF16),
            vmem(NZ, B, W, dtype=BF16),
            vmem(3, B, W),
            vmem(NX, B, W, dtype=BF16),
            vmem(NX, B, W, dtype=BF16),
            vmem(B, W),
            vmem(256, B),
            vmem(B, 16 * B, dtype=BF16),
            vmem(CAP, 16 * B, dtype=BF16),
            vmem(B, CAP),
            vmem(NY, 16, CAP),
            vmem(NT, 8, CAP),
            vmem(1152, NT * CAP, dtype=BF16),
            vmem(NT, 2 * B, CAP, dtype=BF16),
            vmem(NT, NX, 16, CAP, dtype=BF16),
            vmem(2, NT, E, B, dtype=BF16),
            vmem(NX * E, NT * CAP, dtype=BF16),
            vmem(2 * B, W),
            vmem(NX, 64, W),
            vmem(64, W),
            vmem(NZ, 8, W),
            vmem(2, NY, 8, W),
            vmem(4, NX, E, 256),
            vmem(4, NX, E, 256, dtype=BF16),
            vmem(4, 2, 48, 256, dtype=BF16),
            vmem(4, 2, 96, 256, dtype=BF16),
            vmem(4, 2, 96, 256, dtype=BF16),
            vmem(96, B, dtype=BF16),
            vmem(3, 96, B),
            vmem(4, 96, B, dtype=BF16),
            vmem(2, 48, B, dtype=BF16),
            vmem(2, 96, B, dtype=BF16),
            vmem(2, 96, B, dtype=BF16),
            vmem(4, 96, B, dtype=BF16),
            vmem(2, 2, 32, B, dtype=BF16),
            vmem(2, NX, 32, B, dtype=BF16),
            vmem(3, NX, 32, B),
            vmem(2, NX, 32, B, dtype=BF16),
            vmem(4, NX, 32, B, dtype=BF16),
            vmem(NX, 32, B, dtype=BF16),
            vmem(NX, 32, B, dtype=BF16),
            vmem(NX, NZ, 96, E, dtype=BF16),
            vmem(NZ, NX, 32, E, dtype=BF16),
            pltpu.SemaphoreType.DMA((9,)),
            pltpu.SemaphoreType.DMA((N_COPIES,)),
            pltpu.SemaphoreType.DMA((N_COPIES,)),
        ],
        compiler_params=pltpu.CompilerParams(
            collective_id=0, has_side_effects=True, vmem_limit_bytes=40 * 1024 * 1024
        ),
    )(*[
        pltpu.with_memory_space_constraint(a, pltpu.HBM)
        for a in (
            q, it, pq, pi, wq, wi, pw.reshape(1, B), owner.reshape(B, 16).T, row.reshape(B, 16).T
        )
    ])
    return pl.pallas_call(
        finish,
        out_shape=(
            jax.ShapeDtypeStruct((4096, E), F32),
            jax.ShapeDtypeStruct((B, W), F32),
            jax.ShapeDtypeStruct((B, W), F32),
        ),
        in_specs=[pl.BlockSpec(memory_space=pltpu.VMEM)] * 2,
        out_specs=(pl.BlockSpec(memory_space=pltpu.HBM),) * 3,
        scratch_shapes=[vmem(8, 512, E), pltpu.SemaphoreType.DMA((10,))],
        compiler_params=pltpu.CompilerParams(vmem_limit_bytes=12 * 1024 * 1024),
    )(table, gw)


def solution(mesh):
    both = ("dp", "table")
    placed = (
        P(both, None),
        P(both, None),
        P(both, None),
        P(both, None),
        P(),
        P(),
        P(both),
        P(both, None, None),
        P(both, None, None),
    )
    return jax.shard_map(
        on_device,
        mesh=mesh,
        in_specs=placed,
        out_specs=(P("table", None), P(), P()),
        check_vma=False,
    )
```

```python
import math

import jax
import jax.numpy as jnp
from jax import lax
from jax.experimental import pallas as pl
from jax.experimental.pallas import tpu as pltpu
from jax.sharding import PartitionSpec as P

MESH = pl.DeviceIdType.MESH
F32, BF16, I32 = jnp.float32, jnp.bfloat16, jnp.int32
NX, NZ, NY = 4, 8, 8
B, W, E = 128, 256, 128
NT = 2 * NY
CAP = 256
SCALE = 1.0 / math.sqrt(W)
N_COPIES = 176

NN = (((1,), (0,)), ((), ()))
NT_DIMS = (((1,), (1,)), ((), ()))
TN = (((0,), (0,)), ((), ()))


def dot(a, b, dims=NN):
    return lax.dot_general(a, b, dims, preferred_element_type=F32)


def iota(shape, dim):
    return lax.broadcasted_iota(I32, shape, dim)


ARRIVE = (0, 2, 6, 1, 7, 3, 5, 4)
POS = {d: p for p, d in enumerate(ARRIVE)}
RING = {d: p for p, d in enumerate((0, 1, 7, 2, 6, 3, 5, 4))}
OWN = (0, 1, 2, 3, 4, 10, 11, 12)
SIB = (5, 6, 7, 8, 9, 13, 14, 15)
FIRST = 10 * CAP


def kernel(
    q_ref, it_ref, pq_ref, pi_ref, wq_ref, wi_ref, pw_ref, ow_ref, rw_ref,
    table_ref, gw_ref,
    pq, pi, wq, wi, pw, ow, rw,
    ibuf, qbuf, ebuf, gbuf, tops, totals, st_send, st_recv,
    gi_send, gi_sum, gi_own, gq_send, gq_recv, gq_own,
    taken, slots_a, slots_b, lists, onehot, select, factor, pooled, values,
    w_part, wx_recv, wz_send, wz_relay, wz_pass, wz_recv, wy_recv, w_own,
    t_own, t_send, tx_half, tx_relay, tx_recv, tz_first, tz_own, tz_send, tz_half, tz_relay, tz_back, tz_recv,
    lz_half, lz_relay, lz_own, lz_send, lz_recv, lx_send, lx_recv, t_back, l_back,
    load_sem, send_sem, recv_sem,
):
    dp, tb = lax.axis_index("dp"), lax.axis_index("table")
    x, z = lax.div(dp, NZ), lax.rem(dp, NZ)
    y, core = lax.div(tb, 2), lax.rem(tb, 2)

    def at_x(d):
        return (lax.rem(x + d + NX, NX) * NZ + z, tb)

    def at_z(d):
        return (x * NZ + lax.rem(z + d + NZ, NZ), tb)

    def at_y(d):
        return (dp, lax.rem(y + d + NY, NY) * 2 + core)

    sibling = (dp, tb + 1 - 2 * core)
    partners = (
        [at_x(d) for d in range(1, NX)]
        + [at_z(d) for d in (1, 2, -1, -2)]
        + [at_y(d) for d in (1, 2, -1, -2)]
        + [sibling]
    )
    barrier = pltpu.get_barrier_semaphore()
    for partner in partners:
        pl.semaphore_signal(barrier, inc=1, device_id=partner, device_id_type=MESH)
    loads = [
        pltpu.make_async_copy(src, dst, load_sem.at[i])
        for i, (src, dst) in enumerate((
            (it_ref, ibuf.at[pl.ds(0, B), :]),
            (q_ref, qbuf.at[pl.ds(0, B), :]),
            (ow_ref, ow),
            (rw_ref, rw),
            (pw_ref, pw),
            (pq_ref, pq),
            (pi_ref, pi),
            (wq_ref, wq),
            (wi_ref, wi),
        ))
    ]
    for load in loads:
        load.start()
    pl.semaphore_wait(barrier, len(partners))

    copies, drained = [], [0]

    def remote(index, src, dst, device):
        return pltpu.make_async_remote_copy(
            src_ref=src,
            dst_ref=dst,
            send_sem=send_sem.at[index],
            recv_sem=recv_sem.at[index],
            device_id=device,
            device_id_type=MESH,
        )

    def send(src, dst, device):
        copy = remote(len(copies), src, dst, device)
        copy.start()
        copies.append(copy)
        return copy

    def drain():
        for copy in copies[drained[0]:]:
            copy.wait_send()
        drained[0] = len(copies)

    def gather_start(slot, at, source=None):
        source = slot(0, None) if source is None else source
        return {d: send(source, slot(d % 8, None), at(d)) for d in (2, -2, 1, -1)}

    def gather_pass(got, slot, at):
        got[2].wait_recv()
        got[3] = send(slot(2, None), slot(3, None), at(1))
        got[4] = send(slot(2, 0), slot(4, 0), at(2))
        got[-2].wait_recv()
        got[-3] = send(slot(6, None), slot(5, None), at(-1))
        got[-4] = send(slot(6, 1), slot(4, 1), at(-2))

    def wait_for(got, *names):
        for name in names:
            got[name].wait_recv()

    def item_half(d, half):
        return ibuf.at[pl.ds(RING[d] * B + half * 64, 64), :]

    item_in = {}
    for up in (0, 1):
        item_in[1, up] = send(it_ref.at[pl.ds(up * 64, 64), :], item_half(1, up), at_z(1))
        item_in[7, 1 - up] = send(it_ref.at[pl.ds(64 - up * 64, 64), :], item_half(7, 1 - up), at_z(-1))

    def item_step(k):
        for up in (0, 1):
            down = 1 - up
            item_in[k, up].wait_recv()
            if k < 3 or up == 0:
                item_in[k + 1, up] = send(item_half(k, up), item_half(k + 1, up), at_z(1))
            item_in[8 - k, down].wait_recv()
            if k < 3 or down == 1:
                item_in[7 - k, down] = send(item_half(8 - k, down), item_half(7 - k, down), at_z(-1))

    query_in = {}
    for d in (1, 3, 2):
        query_in[d] = send(q_ref, qbuf.at[pl.ds(d * B, B), :], at_x(d))

    for load in loads:
        load.wait()
    owner_row = iota((NT, B), 0)
    hits = jnp.concatenate([(ow[k:k + 1, :] == owner_row).astype(F32) for k in range(16)], axis=0)
    before = (iota((B, 2 * B), 0) < iota((B, 2 * B), 1)).astype(BF16)
    counts = dot(hits.astype(BF16), before)
    at_row, at_col = iota((256, 256), 0), iota((256, 256), 1)
    earlier = jnp.logical_and(
        lax.bitwise_and(at_row, 15) == lax.bitwise_and(at_col, 15),
        lax.shift_right_logical(at_col, 4) < lax.shift_right_logical(at_row, 4),
    ).astype(BF16)
    taken[...] = (counts[:, 0:B] + dot(earlier, counts[:, B:].astype(BF16))) * hits
    item_step(1)
    list_row = iota((64, B), 0)
    list_owner, piece = lax.bitwise_and(list_row, 15), lax.shift_right_logical(list_row, 4)
    pair = iota((1, B), 1)
    place = iota((CAP, B), 0)

    def list_slot(k, _):
        lanes = pl.ds(pl.multiple_of(k * B, B), B)
        ranks = taken[pl.ds(pl.multiple_of(k * NT, NT), NT), :]
        rank = jnp.sum(ranks, axis=0, keepdims=True).astype(I32)
        slots_b[:, lanes] = (place == rank).astype(BF16)
        owner, row = ow[pl.ds(k, 1), :], rw[pl.ds(k, 1), :]
        part = jnp.where(
            piece == 0,
            pair + lax.div(k, 8) * B,
            jnp.where(
                piece == 1,
                lax.shift_right_logical(row, 8) + 1,
                jnp.where(piece == 2, lax.bitwise_and(row, 255), 0),
            ),
        )
        slots_a[:, lanes] = jnp.where(list_owner == owner, part, 0).astype(F32).astype(BF16)
        return 0

    lax.fori_loop(0, 16, list_slot, 0)
    lists[0] = dot(slots_a[...], slots_b[...], NT_DIMS).astype(BF16)

    def list_slot_of(d, half):
        if half is None:
            return lists.at[OWN[POS[d]]]
        return lists.at[OWN[POS[d]], pl.ds(half * 32, 32), :]

    list_in = gather_start(list_slot_of, at_y)
    item_step(2)

    wait_for(query_in, 1, 3, 2)

    def logits(p, _):
        rows = pl.ds(pl.multiple_of(p * B, B), B)
        block = SCALE * dot(ibuf[rows, :], qbuf[...], NT_DIMS)
        top = jnp.max(block, axis=0, keepdims=True)
        block = jnp.exp(block - top)
        ebuf[rows, :] = block
        tops[pl.ds(p, 1), :] = top
        totals[pl.ds(p, 1), :] = jnp.sum(block, axis=0, keepdims=True)
        return 0

    lax.fori_loop(0, 3, logits, 0)
    item_step(3)
    lax.fori_loop(3, 7, logits, 0)
    wait_for(item_in, (4, 0), (4, 1))
    lax.fori_loop(7, 8, logits, 0)

    top = jnp.max(tops[...], axis=0, keepdims=True)
    total = jnp.sum(totals[...] * jnp.exp(tops[...] - top), axis=0, keepdims=True)
    weight = pw[...]
    for k in range(NX):
        st_send[k:k + 1, :] = top[:, k * B:(k + 1) * B]
        st_send[NX + k:NX + k + 1, :] = total[:, k * B:(k + 1) * B]
    st_send[8:16, :] = jnp.broadcast_to(weight, (8, B))
    stat_in = {d: send(st_send, st_recv.at[d], at_x(d)) for d in (2, 1, 3)}
    gather_pass(list_in, list_slot_of, at_y)
    wait_for(stat_in, 1, 3, 2)
    maxima, factors = [], []
    for k in range(NX):
        part_tops, part_totals = [st_send[k:k + 1, :]], [st_send[NX + k:NX + k + 1, :]]
        for d in range(1, NX):
            j = (k - d) % NX
            part_tops.append(st_recv[d, j:j + 1, :])
            part_totals.append(st_recv[d, NX + j:NX + j + 1, :])
        row_max = part_tops[0]
        for t in part_tops[1:]:
            row_max = jnp.maximum(row_max, t)
        row_total = sum(s * jnp.exp(t - row_max) for t, s in zip(part_tops, part_totals))
        maxima.append(row_max)
        factors.append((weight if k == 0 else st_recv[k, 8:9, :]) / row_total)
    row_max, factors = jnp.concatenate(maxima, axis=1), jnp.concatenate(factors, axis=1)
    totals[...] = factors * jnp.exp(tops[...] - row_max)

    def item_terms(p):
        rows = pl.ds(pl.multiple_of(p * B, B), B)
        block = (ebuf[rows, :] * totals[pl.ds(p, 1), :]).astype(BF16)
        gbuf[rows, :] = block
        return SCALE * dot(block, qbuf[...])

    def near_terms(p, _):
        gi_own[p] = item_terms(p)
        return 0

    sum_in = {}
    half_of = (slice(0, 64), slice(64, 128))

    def send_sum(way, k, half):
        p = RING[(4, 5, 6, 7)[k] if way == 0 else (4, 3, 2, 1)[k]]
        block = gi_own[p, half_of[half], :]
        if (way, k - 1, half) in sum_in:
            sum_in[way, k - 1, half].wait_recv()
            block += gi_sum[way, k - 1, half].astype(F32)
        gi_send[way, k, half] = block.astype(BF16)
        sum_in[way, k, half] = send(gi_send.at[way, k, half], gi_sum.at[way, k, half], at_z(1 - 2 * way))

    near_terms(7, 0)
    send_sum(0, 0, 0)
    send_sum(1, 0, 1)
    lax.fori_loop(5, 7, near_terms, 0)
    send_sum(0, 1, 1)
    send_sum(1, 1, 0)
    lax.fori_loop(0, 5, near_terms, 0)
    same = iota((B, B), 0) == iota((B, B), 1)
    diagonal = ebuf[0:B, 0:B] * totals[0:1, 0:B] - jnp.where(same, weight, 0.0)
    gbuf[0:B, 0:B] = diagonal.astype(BF16)
    gi_own[0] = SCALE * dot(gbuf[0:B, :], qbuf[...])

    terms = SCALE * dot(gbuf[...], ibuf[...], TN)
    gq_own[...] = terms[0:B, :]
    for k in range(1, NX):
        gq_send[k] = terms[k * B:(k + 1) * B, :].astype(BF16)
    query_grad_in = {k: send(gq_send.at[k], gq_recv.at[k], at_x(-k)) for k in (2, 1, 3)}
    send_sum(0, 1, 0)
    send_sum(1, 1, 1)
    send_sum(0, 2, 1)
    send_sum(1, 2, 0)

    list_sib = []

    def lists_to_sibling(low, high):
        list_sib.append(send(
            lists.at[pl.ds(OWN[low], high - low)], lists.at[pl.ds(SIB[low], high - low)], sibling
        ))

    wait_for(list_in, 1, -1, 3, -3, 4, -4)
    lists_to_sibling(0, 5)
    lists_to_sibling(5, 8)
    send_sum(0, 2, 0)
    send_sum(1, 2, 1)
    send_sum(0, 3, 1)
    send_sum(1, 3, 0)
    source_row = iota((2 * B, CAP), 0)
    owner_row = iota((NT, CAP), 0)
    low_row = lax.bitwise_and(iota((1152, CAP), 0), 1023)

    def one_hots(s, _):
        entry = lists[s].astype(F32)
        source, high, low = [
            jnp.sum(jnp.where(owner_row == tb, entry[16 * k:16 * k + 16, :], 0.0), axis=0, keepdims=True).astype(I32)
            for k in range(3)
        ]
        row = (high - 1) * 256 + low
        select[s] = (source == source_row).astype(BF16)
        lanes = pl.ds(pl.multiple_of(s * CAP, CAP), CAP)
        onehot[:, lanes] = (lax.bitwise_and(row, 1023) == low_row).astype(BF16)
        block = jnp.broadcast_to(lax.shift_right_arithmetic(row, 10), (16, CAP))
        for j in range(NX):
            factor[s, j] = (block == j).astype(BF16)
        return 0

    lax.fori_loop(0, 5, one_hots, 0)
    lax.fori_loop(10, 13, one_hots, 0)
    send_sum(0, 3, 0)
    send_sum(1, 3, 1)

    query_grad = gq_own[...]
    for k in (1, 3, 2):
        query_grad_in[k].wait_recv()
        query_grad += gq_recv[k].astype(F32)
    query_grad = query_grad.astype(BF16)

    pooled_in, pooled_sib = {}, {}

    def pooled_slot(half):
        def slot(d, rows):
            if rows is None:
                return pooled.at[half, OWN[POS[d]]]
            return pooled.at[half, OWN[POS[d]], pl.ds(rows * 64, 64), :]

        return slot

    def to_sibling(half, low, high):
        pooled_sib[half, low] = send(
            pooled.at[half, pl.ds(OWN[low], high - low)], pooled.at[half, pl.ds(SIB[low], high - low)], sibling
        )

    pooled[0, 0] = dot(wq[...], query_grad, NT_DIMS).astype(BF16)
    pooled_in[0] = gather_start(pooled_slot(0), at_y)
    to_sibling(0, 0, 1)
    w_part[0:B, :] = dot(pq[...], query_grad, TN)

    for copy in list_sib:
        copy.wait_recv()
    lax.fori_loop(5, 10, one_hots, 0)
    lax.fori_loop(13, 16, one_hots, 0)
    drain()

    item_grad = gi_own[0]
    for way in (0, 1):
        for half in (0, 1):
            sum_in[way, 3, half].wait_recv()
        item_grad += gi_sum[way, 3].reshape(B, W).astype(F32)
    item_grad = item_grad.astype(BF16)
    pooled[1, 0] = dot(wi[...], item_grad, NT_DIMS).astype(BF16)
    pooled_in[1] = gather_start(pooled_slot(1), at_y)
    to_sibling(1, 0, 1)
    gather_pass(pooled_in[0], pooled_slot(0), at_y)
    wait_for(pooled_in[0], 1, -1)
    to_sibling(0, 1, 3)
    to_sibling(0, 3, 5)
    w_part[B:, :] = dot(pi[...], item_grad, TN)
    w_in = {}
    for d in (2, 1, 3):
        to_x = lax.rem(x + d, NX)
        w_in[d] = send(w_part.at[pl.ds(pl.multiple_of(to_x * 64, 64), 64), :], wx_recv.at[d], at_x(d))

    def place_values(s, _):
        got = (dot(pooled[0, s], select[s, 0:B, :]) + dot(pooled[1, s], select[s, B:, :])).astype(BF16)
        lanes = pl.ds(pl.multiple_of(s * CAP, CAP), CAP)
        for j in range(NX):
            values[j * E:(j + 1) * E, lanes] = got * jnp.tile(factor[s, j], (8, 1))
        return 0

    def quarter_rows(p):
        return pl.ds(pl.multiple_of(lax.rem(z + 4 + 3 * p * (p + 1), NZ) * B, B), 256)

    def first_part(p, _):
        part = dot(values[:, 0:FIRST], onehot[quarter_rows(p), 0:FIRST], NT_DIMS)
        t_own[p] = part.reshape(NX, E, 256)
        return 0

    gather_pass(pooled_in[1], pooled_slot(1), at_y)
    wait_for(pooled_in[1], 1, -1)
    to_sibling(1, 1, 3)
    to_sibling(1, 3, 5)
    lax.fori_loop(0, 5, place_values, 0)
    for low in (0, 1, 3):
        pooled_sib[0, low].wait_recv()
        pooled_sib[1, low].wait_recv()
    lax.fori_loop(5, 10, place_values, 0)

    w_sum = w_part[pl.ds(pl.multiple_of(x * 64, 64), 64), :]
    for d in (1, 3, 2):
        w_in[d].wait_recv()
        w_sum += wx_recv[d]
    wz_send[...] = w_sum

    def w_chunk(d):
        return pl.ds(pl.multiple_of(lax.rem(z + d + NZ, NZ) * 8, 8), 8)

    wz_in = {}
    for d, via, dst in (
        (4, 2, wz_relay.at[0]), (3, 1, wz_relay.at[1]), (-3, -1, wz_relay.at[2]),
        (1, 1, wz_recv.at[0]), (-1, -1, wz_recv.at[1]),
    ):
        wz_in[d] = send(wz_send.at[w_chunk(d), :], dst, at_z(via))

    lax.fori_loop(0, 2, first_part, 0)
    wait_for(pooled_in[0], 3, -3, 4, -4)
    to_sibling(0, 5, 8)
    wait_for(pooled_in[1], 3, -3, 4, -4)
    to_sibling(1, 5, 8)
    lax.fori_loop(10, 13, place_values, 0)
    lax.fori_loop(2, 4, first_part, 0)
    wait_for(wz_in, 4, 3, -3)
    wz_pass[0] = wz_send[w_chunk(2), :] + wz_relay[0] + wz_relay[1]
    wz_pass[1] = wz_send[w_chunk(-2), :] + wz_relay[2]
    for side, d in ((0, 2), (1, -2)):
        wz_in[d] = send(wz_pass.at[side], wz_recv.at[2 + side], at_z(d))
    pooled_sib[0, 5].wait_recv()
    pooled_sib[1, 5].wait_recv()
    lax.fori_loop(13, 16, place_values, 0)

    half_base = len(copies)
    copies.extend([None] * 8)

    def half_copy(p, side):
        return remote(
            half_base + 2 * p + side,
            t_send.at[p, lax.rem(x + 2, NX), pl.ds(side * 48, 48), :],
            tx_half.at[p, side],
            at_x(1 - 2 * side),
        )

    def send_part(p, part):
        part = t_own[p] + part.reshape(NX, E, 256)
        t_own[p] = part
        t_send[p] = part.astype(BF16)
        half_copy(p, 0).start()
        half_copy(p, 1).start()

    def last_part(p, _):
        send_part(p, dot(values[:, FIRST:], onehot[quarter_rows(p), FIRST:], NT_DIMS))
        return 0

    lax.fori_loop(0, 4, last_part, 0)
    for p in range(4):
        for side in (0, 1):
            copies[half_base + 2 * p + side] = half_copy(p, side)

    def low_columns(p, side):
        return t_send.at[p, :, pl.ds(96, 32), pl.ds(side * B, B)]

    low_half = [
        send(t_send.at[0, pl.ds(2 * side, 2), pl.ds(96, 32), pl.ds(0, B)], lz_half.at[side], at_z(2 - 4 * side))
        for side in (0, 1)
    ]
    low_relay = [
        send(low_columns(1, 1), lz_relay.at[0], at_z(1)),
        send(low_columns(0, 1), lz_relay.at[1], at_z(-1)),
    ]
    low_in = [
        send(low_columns(3, 1), lz_recv.at[0], at_z(1)),
        send(low_columns(2, 1), lz_recv.at[1], at_z(-1)),
    ]

    def low_pass():
        for side in (0, 1):
            low_relay[side].wait_recv()
            low_half[side].wait_recv()
            lz_own[side] = t_own[1 + side, :, 96:, 0:B] + lz_relay[side].astype(F32)
            pair_of = slice(2 * side, 2 * side + 2)
            lz_own[side, pair_of] += lz_half[side].astype(F32)
            lz_send[side] = lz_own[side].astype(BF16)
            low_in.append(send(lz_send.at[side], lz_recv.at[2 + side], at_z(2 - 4 * side)))

    low_x = {}

    def low_sum():
        part = t_own[3, :, 96:, 0:B]
        for k in range(4):
            low_in[k].wait_recv()
            part += lz_recv[k].astype(F32)
        lz_own[2] = part
        lx_send[...] = part.astype(BF16)
        for d in (2, 1, 3):
            low_x[d] = send(lx_send.at[lax.rem(x + d, NX)], lx_recv.at[d], at_x(d))

    relay_in, tz_half_in, tz_relay_in, tz_in = {}, {}, {}, {}

    def table_relay(p):
        for side, step in ((0, 1), (1, -1)):
            copies[half_base + 2 * p + side].wait_recv()
            near = lax.rem(x + step + NX, NX)
            for half in (0, 1):
                rows = slice(half * 48, half * 48 + 48)
                part = t_own[p, near, rows, :]
                if half == side:
                    part += tx_half[p, side].astype(F32)
                tx_relay[p, side, rows, :] = part.astype(BF16)
            relay_in[p, side] = send(tx_relay.at[p, side], tx_recv.at[p, side], at_x(step))

    def table_sum(p):
        part = t_own[p, x, 0:96, :]
        for side in (0, 1):
            relay_in[p, side].wait_recv()
            part += tx_recv[p, side].astype(F32)
        tz_send[p] = part[:, B:].astype(BF16)
        if p == 0:
            tz_first[...] = part[:, 0:B].astype(BF16)
            for side in (0, 1):
                tz_half_in[side] = send(
                    tz_first.at[pl.ds(side * 48, 48), :], tz_half.at[side], at_z(2 - 4 * side)
                )
        else:
            tz_own[p - 1] = part[:, 0:B]
        if p < 2:
            tz_relay_in[1 - p] = send(tz_send.at[p], tz_relay.at[1 - p], at_z(2 * p - 1))
        else:
            tz_in[3 - p] = send(tz_send.at[p], tz_recv.at[3 - p], at_z(2 * p - 5))

    def table_pass():
        for side in (0, 1):
            tz_relay_in[side].wait_recv()
            tz_half_in[side].wait_recv()
            rows = slice(side * 48, side * 48 + 48)
            tz_own[side] += tz_relay[side].astype(F32)
            tz_own[side, rows, :] += tz_half[side].astype(F32)
            tz_back[side] = tz_own[side].astype(BF16)
            tz_in[2 + side] = send(tz_back.at[side], tz_recv.at[2 + side], at_z(2 - 4 * side))

    def small_pass(got, slot, at, there):
        got[2].wait_recv()
        got[3] = send(slot(2), there(2, 3), at(1))
        got[4] = send(slot(2), there(2, 4), at(2))
        got[-2].wait_recv()
        got[5] = send(slot(-2), there(-2, 5), at(-1))

    def wy_slot(d):
        return wy_recv.at[0, d % 8]

    def w_rows(d):
        place = x * NZ + lax.rem(z - d + NZ, NZ)
        return gw_ref.at[pl.ds(pl.multiple_of(place * 8, 8), 8), pl.ds(pl.multiple_of(core * B, B), B)]

    table_relay(0)
    table_relay(1)
    w_sum = wz_send[w_chunk(0), :]
    wait_for(wz_in, 1, -1, 2, -2)
    for k in range(4):
        w_sum += wz_recv[k]
    wy_recv[0, 0] = w_sum
    wy_in = {d: send(wy_slot(0), wy_slot(d), at_y(d)) for d in (2, -2, 1, -1)}

    table_sum(0)
    low_pass()
    table_relay(2)
    small_pass(wy_in, wy_slot, at_y, lambda here, d: wy_slot(d))
    table_sum(1)
    table_relay(3)
    wait_for(wy_in, 1, -1, 3, 4, 5)
    wy_sib = send(wy_recv.at[0], wy_recv.at[1], sibling)
    table_sum(2)
    low_sum()
    table_pass()

    wy_sib.wait_recv()
    w_sum = wy_recv[0, 0]
    for d in range(1, NY):
        w_sum += wy_recv[0, d]
    for d in range(NY):
        w_sum += wy_recv[1, d]
    w_own[...] = w_sum
    own_lanes = pl.ds(pl.multiple_of(core * B, B), B)
    gw_ref[pl.ds(pl.multiple_of(dp * 8, 8), 8), own_lanes] = w_own[:, own_lanes]
    w_back = {d: send(w_rows(0), w_rows(0), at_z(d)) for d in (2, -2, 1, -1)}

    table_sum(3)
    drain()

    low = lz_own[2, x]
    for d in (1, 3, 2):
        low_x[d].wait_recv()
        low += lx_recv[d].astype(F32)
    part = tz_own[2]
    for k in (1, 0, 2, 3):
        tz_in[k].wait_recv()
        part += tz_recv[k].astype(F32)
    rows = jnp.concatenate([part, low], axis=0).T.astype(BF16)
    t_back[x, 0] = rows[0:96]
    l_back[0, x] = rows[96:]

    def back_slot(d, half):
        if half is None:
            return t_back.at[x, POS[d]]
        return t_back.at[x, POS[d], pl.ds(half * 48, 48), :]

    def low_slot(d, half):
        if half is None:
            return l_back.at[POS[d]]
        return l_back.at[POS[d], pl.ds(2 * half, 2)]

    back = gather_start(back_slot, at_z)
    low_back = [send(l_back.at[0, x], l_back.at[0, x], at_x(d)) for d in (2, 1, 3)]
    near_in, far_in = {}, []

    def to_near(low, high):
        rows = t_back.at[x, pl.ds(low, high - low)]
        for side, step in ((0, 1), (1, -1)):
            near_in[low, side] = send(rows, rows, at_x(step))

    def to_far(low, high):
        middle = {1: None, 2: low + 1, 3: None}[high - low]
        for side, step in ((0, 1), (1, -1)):
            near_in[low, side].wait_recv()
            held = lax.rem(x - step + NX, NX)
            if middle is None:
                rows = t_back.at[held, pl.ds(low, high - low), pl.ds(side * 48, 48), :]
            else:
                rows = t_back.at[held, low + side]
            far_in.append(send(rows, rows, at_x(step)))

    to_near(0, 1)

    small_pass(w_back, w_rows, at_z, lambda here, d: w_rows(here))
    gather_pass(back, back_slot, at_z)
    to_near(1, 3)
    for copy in low_back:
        copy.wait_recv()
    low_back = gather_start(low_slot, at_z)
    wait_for(w_back, 1, -1, 3, 4, 5)
    w_held = gw_ref.at[pl.ds(pl.multiple_of(x * 64, 64), 64), pl.ds(pl.multiple_of(core * B, B), B)]
    w_x = [send(w_held, w_held, at_x(step)) for step in (2, 1, 3)]
    to_far(0, 1)
    wait_for(back, 1, -1)
    to_near(3, 5)
    to_far(1, 3)
    wait_for(back, 3, -3, 4, -4)
    to_near(5, 8)
    gather_pass(low_back, low_slot, at_z)
    to_far(3, 5)

    def rows_of(far, p, d):
        place = (far * NZ + lax.rem(z - d + NZ, NZ)) * B
        table_ref[pl.ds(pl.multiple_of(place, B), 96), :] = t_back[far, p]

    def low_rows_of(p, d):
        for far in range(NX):
            place = (far * NZ + lax.rem(z - d + NZ, NZ)) * B + 96
            table_ref[pl.ds(pl.multiple_of(place, 32), 32), :] = l_back[p, far]

    to_far(5, 8)
    for copy in w_x:
        copy.wait_recv()
    w_half = gw_ref.at[:, pl.ds(pl.multiple_of(core * B, B), B)]
    far_in.append(send(w_half, w_half, sibling))
    for p, d in enumerate(ARRIVE):
        rows_of(x, p, d)
        rows_of(lax.rem(x + 1, NX), p, d)
        rows_of(lax.rem(x + 3, NX), p, d)
    wait_for(low_back, 1, -1, 3, -3, 4, -4)
    for p, d in enumerate(ARRIVE):
        low_rows_of(p, d)
    drain()
    for copy in far_in:
        copy.wait_recv()
    for p, d in enumerate(ARRIVE):
        rows_of(lax.rem(x + 2, NX), p, d)
    drain()


def finish(table_ref, gw_ref, out_ref, gwq_ref, gwi_ref, wide, sem):
    copies = [
        pltpu.make_async_copy(gw_ref.at[pl.ds(0, B), :], gwq_ref, sem.at[8]),
        pltpu.make_async_copy(gw_ref.at[pl.ds(B, B), :], gwi_ref, sem.at[9]),
    ]
    for copy in copies:
        copy.start()
    for i in range(8):
        wide[i] = table_ref[i * 512:(i + 1) * 512, :].astype(F32)
        copies.append(pltpu.make_async_copy(wide.at[i], out_ref.at[pl.ds(i * 512, 512), :], sem.at[i]))
        copies[-1].start()
    for copy in copies:
        copy.wait()


def on_device(q, it, pq, pi, wq, wi, pw, owner, row):
    def vmem(*shape, dtype=F32):
        return pltpu.VMEM(shape, dtype)

    table, gw = pl.pallas_call(
        kernel,
        out_shape=(
            jax.ShapeDtypeStruct((4096, E), BF16),
            jax.ShapeDtypeStruct((2 * B, W), F32),
        ),
        in_specs=[pl.BlockSpec(memory_space=pltpu.HBM)] * 9,
        out_specs=(pl.BlockSpec(memory_space=pltpu.VMEM),) * 2,
        scratch_shapes=[
            vmem(B, E, dtype=BF16),
            vmem(B, E, dtype=BF16),
            vmem(E, W, dtype=BF16),
            vmem(E, W, dtype=BF16),
            vmem(1, B),
            vmem(16, B, dtype=I32),
            vmem(16, B, dtype=I32),
            vmem(NZ * B, W, dtype=BF16),
            vmem(NX * B, W, dtype=BF16),
            vmem(NZ * B, NX * B),
            vmem(NZ * B, NX * B, dtype=BF16),
            vmem(NZ, NX * B),
            vmem(NZ, NX * B),
            vmem(16, B),
            vmem(NX, 16, B),
            vmem(2, 4, 2, 64, W, dtype=BF16),
            vmem(2, 4, 2, 64, W, dtype=BF16),
            vmem(NZ, B, W),
            vmem(NX, B, W, dtype=BF16),
            vmem(NX, B, W, dtype=BF16),
            vmem(B, W),
            vmem(256, B),
            vmem(64, 16 * B, dtype=BF16),
            vmem(CAP, 16 * B, dtype=BF16),
            vmem(NT, 64, CAP, dtype=BF16),
            vmem(1152, NT * CAP, dtype=BF16),
            vmem(NT, 2 * B, CAP, dtype=BF16),
            vmem(NT, NX, 16, CAP, dtype=BF16),
            vmem(2, NT, E, B, dtype=BF16),
            vmem(NX * E, NT * CAP, dtype=BF16),
            vmem(2 * B, W),
            vmem(NX, 64, W),
            vmem(64, W),
            vmem(3, 8, W),
            vmem(2, 8, W),
            vmem(4, 8, W),
            vmem(2, NY, 8, W),
            vmem(8, W),
            vmem(4, NX, E, 256),
            vmem(4, NX, E, 256, dtype=BF16),
            vmem(4, 2, 48, 256, dtype=BF16),
            vmem(4, 2, 96, 256, dtype=BF16),
            vmem(4, 2, 96, 256, dtype=BF16),
            vmem(96, B, dtype=BF16),
            vmem(3, 96, B),
            vmem(4, 96, B, dtype=BF16),
            vmem(2, 48, B, dtype=BF16),
            vmem(2, 96, B, dtype=BF16),
            vmem(2, 96, B, dtype=BF16),
            vmem(4, 96, B, dtype=BF16),
            vmem(2, 2, 32, B, dtype=BF16),
            vmem(2, NX, 32, B, dtype=BF16),
            vmem(3, NX, 32, B),
            vmem(2, NX, 32, B, dtype=BF16),
            vmem(4, NX, 32, B, dtype=BF16),
            vmem(NX, 32, B, dtype=BF16),
            vmem(NX, 32, B, dtype=BF16),
            vmem(NX, NZ, 96, E, dtype=BF16),
            vmem(NZ, NX, 32, E, dtype=BF16),
            pltpu.SemaphoreType.DMA((9,)),
            pltpu.SemaphoreType.DMA((N_COPIES,)),
            pltpu.SemaphoreType.DMA((N_COPIES,)),
        ],
        compiler_params=pltpu.CompilerParams(
            collective_id=0, has_side_effects=True, vmem_limit_bytes=40 * 1024 * 1024
        ),
    )(*[
        pltpu.with_memory_space_constraint(a, pltpu.HBM)
        for a in (
            q, it, pq, pi, wq, wi, pw.reshape(1, B), owner.reshape(B, 16).T, row.reshape(B, 16).T
        )
    ])
    return pl.pallas_call(
        finish,
        out_shape=(
            jax.ShapeDtypeStruct((4096, E), F32),
            jax.ShapeDtypeStruct((B, W), F32),
            jax.ShapeDtypeStruct((B, W), F32),
        ),
        in_specs=[pl.BlockSpec(memory_space=pltpu.VMEM)] * 2,
        out_specs=(pl.BlockSpec(memory_space=pltpu.HBM),) * 3,
        scratch_shapes=[vmem(8, 512, E), pltpu.SemaphoreType.DMA((10,))],
        compiler_params=pltpu.CompilerParams(vmem_limit_bytes=12 * 1024 * 1024),
    )(table, gw)


def solution(mesh):
    both = ("dp", "table")
    placed = (
        P(both, None),
        P(both, None),
        P(both, None),
        P(both, None),
        P(),
        P(),
        P(both),
        P(both, None, None),
        P(both, None, None),
    )
    return jax.shard_map(
        on_device,
        mesh=mesh,
        in_specs=placed,
        out_specs=(P("table", None), P(), P()),
        check_vma=False,
    )
```

```python
import math

import jax
import jax.numpy as jnp
from jax import lax
from jax.experimental import pallas as pl
from jax.experimental.pallas import tpu as pltpu
from jax.sharding import PartitionSpec as P

MESH = pl.DeviceIdType.MESH
F32, BF16, I32 = jnp.float32, jnp.bfloat16, jnp.int32
NX, NZ, NY = 4, 8, 8
B, W, E = 128, 256, 128
NT = 2 * NY
CAP = 256
SCALE = 1.0 / math.sqrt(W)
N_COPIES = 176

NN = (((1,), (0,)), ((), ()))
NT_DIMS = (((1,), (1,)), ((), ()))
TN = (((0,), (0,)), ((), ()))


def dot(a, b, dims=NN):
    return lax.dot_general(a, b, dims, preferred_element_type=F32)


def iota(shape, dim):
    return lax.broadcasted_iota(I32, shape, dim)


ARRIVE = (0, 2, 6, 1, 7, 3, 5, 4)
POS = {d: p for p, d in enumerate(ARRIVE)}
RING = {d: p for p, d in enumerate((0, 1, 7, 2, 6, 3, 5, 4))}
OWN = (0, 1, 2, 3, 4, 10, 11, 12)
SIB = (5, 6, 7, 8, 9, 13, 14, 15)
FIRST = 10 * CAP


def kernel(
    q_ref, it_ref, pq_ref, pi_ref, wq_ref, wi_ref, pw_ref, ow_ref, rw_ref,
    table_ref, gw_ref,
    pq, pi, wq, wi, pw, ow, rw,
    ibuf, qbuf, ebuf, gbuf, tops, totals, st_send, st_recv,
    gi_send, gi_sum, gi_own, gq_send, gq_recv, gq_own,
    taken, slots_a, slots_b, lists, onehot, select, factor, pooled, values,
    w_part, wx_recv, wz_send, wz_relay, wz_pass, wz_recv, wy_recv, w_own,
    t_own, t_send, tx_half, tx_relay, tx_recv, tz_first, tz_own, tz_send, tz_half, tz_relay, tz_back, tz_recv,
    lz_half, lz_relay, lz_own, lz_send, lz_recv, lx_send, lx_recv, t_back, l_back,
    load_sem, send_sem, recv_sem,
):
    dp, tb = lax.axis_index("dp"), lax.axis_index("table")
    x, z = lax.div(dp, NZ), lax.rem(dp, NZ)
    y, core = lax.div(tb, 2), lax.rem(tb, 2)

    def at_x(d):
        return (lax.rem(x + d + NX, NX) * NZ + z, tb)

    def at_z(d):
        return (x * NZ + lax.rem(z + d + NZ, NZ), tb)

    def at_y(d):
        return (dp, lax.rem(y + d + NY, NY) * 2 + core)

    sibling = (dp, tb + 1 - 2 * core)
    partners = (
        [at_x(d) for d in range(1, NX)]
        + [at_z(d) for d in (1, 2, -1, -2)]
        + [at_y(d) for d in (1, 2, -1, -2)]
        + [sibling]
    )
    barrier = pltpu.get_barrier_semaphore()
    for partner in partners:
        pl.semaphore_signal(barrier, inc=1, device_id=partner, device_id_type=MESH)
    loads = [
        pltpu.make_async_copy(src, dst, load_sem.at[i])
        for i, (src, dst) in enumerate((
            (it_ref, ibuf.at[pl.ds(0, B), :]),
            (q_ref, qbuf.at[pl.ds(0, B), :]),
            (ow_ref, ow),
            (rw_ref, rw),
            (pw_ref, pw),
            (pq_ref, pq),
            (pi_ref, pi),
            (wq_ref, wq),
            (wi_ref, wi),
        ))
    ]
    for load in loads:
        load.start()
    pl.semaphore_wait(barrier, len(partners))

    copies, drained = [], [0]

    def remote(index, src, dst, device):
        return pltpu.make_async_remote_copy(
            src_ref=src,
            dst_ref=dst,
            send_sem=send_sem.at[index],
            recv_sem=recv_sem.at[index],
            device_id=device,
            device_id_type=MESH,
        )

    def send(src, dst, device):
        copy = remote(len(copies), src, dst, device)
        copy.start()
        copies.append(copy)
        return copy

    def drain():
        for copy in copies[drained[0]:]:
            copy.wait_send()
        drained[0] = len(copies)

    def gather_start(slot, at, source=None):
        source = slot(0, None) if source is None else source
        return {d: send(source, slot(d % 8, None), at(d)) for d in (2, -2, 1, -1)}

    def gather_pass(got, slot, at):
        got[2].wait_recv()
        got[3] = send(slot(2, None), slot(3, None), at(1))
        got[4] = send(slot(2, 0), slot(4, 0), at(2))
        got[-2].wait_recv()
        got[-3] = send(slot(6, None), slot(5, None), at(-1))
        got[-4] = send(slot(6, 1), slot(4, 1), at(-2))

    def wait_for(got, *names):
        for name in names:
            got[name].wait_recv()

    def item_half(d, half):
        return ibuf.at[pl.ds(RING[d] * B + half * 64, 64), :]

    item_in = {}
    for up in (0, 1):
        item_in[1, up] = send(it_ref.at[pl.ds(up * 64, 64), :], item_half(1, up), at_z(1))
        item_in[7, 1 - up] = send(it_ref.at[pl.ds(64 - up * 64, 64), :], item_half(7, 1 - up), at_z(-1))

    def item_step(k):
        for up in (0, 1):
            down = 1 - up
            item_in[k, up].wait_recv()
            if k < 3 or up == 0:
                item_in[k + 1, up] = send(item_half(k, up), item_half(k + 1, up), at_z(1))
            item_in[8 - k, down].wait_recv()
            if k < 3 or down == 1:
                item_in[7 - k, down] = send(item_half(8 - k, down), item_half(7 - k, down), at_z(-1))

    query_in = {}
    for d in (1, 3, 2):
        query_in[d] = send(q_ref, qbuf.at[pl.ds(d * B, B), :], at_x(d))

    for load in loads:
        load.wait()
    owner_row = iota((NT, B), 0)
    hits = jnp.concatenate([(ow[k:k + 1, :] == owner_row).astype(F32) for k in range(16)], axis=0)
    before = (iota((B, 2 * B), 0) < iota((B, 2 * B), 1)).astype(BF16)
    counts = dot(hits.astype(BF16), before)
    at_row, at_col = iota((256, 256), 0), iota((256, 256), 1)
    earlier = jnp.logical_and(
        lax.bitwise_and(at_row, 15) == lax.bitwise_and(at_col, 15),
        lax.shift_right_logical(at_col, 4) < lax.shift_right_logical(at_row, 4),
    ).astype(BF16)
    taken[...] = (counts[:, 0:B] + dot(earlier, counts[:, B:].astype(BF16))) * hits
    item_step(1)
    list_row = iota((64, B), 0)
    list_owner, piece = lax.bitwise_and(list_row, 15), lax.shift_right_logical(list_row, 4)
    pair = iota((1, B), 1)
    place = iota((CAP, B), 0)

    def list_slot(k, _):
        lanes = pl.ds(pl.multiple_of(k * B, B), B)
        ranks = taken[pl.ds(pl.multiple_of(k * NT, NT), NT), :]
        rank = jnp.sum(ranks, axis=0, keepdims=True).astype(I32)
        slots_b[:, lanes] = (place == rank).astype(BF16)
        owner, row = ow[pl.ds(k, 1), :], rw[pl.ds(k, 1), :]
        part = jnp.where(
            piece == 0,
            pair + lax.div(k, 8) * B,
            jnp.where(
                piece == 1,
                lax.shift_right_logical(row, 8) + 1,
                jnp.where(piece == 2, lax.bitwise_and(row, 255), 0),
            ),
        )
        slots_a[:, lanes] = jnp.where(list_owner == owner, part, 0).astype(F32).astype(BF16)
        return 0

    lax.fori_loop(0, 16, list_slot, 0)
    lists[0] = dot(slots_a[...], slots_b[...], NT_DIMS).astype(BF16)

    def list_slot_of(d, half):
        if half is None:
            return lists.at[OWN[POS[d]]]
        return lists.at[OWN[POS[d]], pl.ds(half * 32, 32), :]

    list_in = gather_start(list_slot_of, at_y)
    item_step(2)

    wait_for(query_in, 1, 3, 2)

    def logits(p, _):
        rows = pl.ds(pl.multiple_of(p * B, B), B)
        block = SCALE * dot(ibuf[rows, :], qbuf[...], NT_DIMS)
        top = jnp.max(block, axis=0, keepdims=True)
        block = jnp.exp(block - top)
        ebuf[rows, :] = block
        tops[pl.ds(p, 1), :] = top
        totals[pl.ds(p, 1), :] = jnp.sum(block, axis=0, keepdims=True)
        return 0

    lax.fori_loop(0, 3, logits, 0)
    item_step(3)
    lax.fori_loop(3, 7, logits, 0)
    wait_for(item_in, (4, 0), (4, 1))
    lax.fori_loop(7, 8, logits, 0)

    top = jnp.max(tops[...], axis=0, keepdims=True)
    total = jnp.sum(totals[...] * jnp.exp(tops[...] - top), axis=0, keepdims=True)
    weight = pw[...]
    for k in range(NX):
        st_send[k:k + 1, :] = top[:, k * B:(k + 1) * B]
        st_send[NX + k:NX + k + 1, :] = total[:, k * B:(k + 1) * B]
    st_send[8:16, :] = jnp.broadcast_to(weight, (8, B))
    stat_in = {d: send(st_send, st_recv.at[d], at_x(d)) for d in (2, 1, 3)}
    gather_pass(list_in, list_slot_of, at_y)
    wait_for(stat_in, 1, 3, 2)
    maxima, factors = [], []
    for k in range(NX):
        part_tops, part_totals = [st_send[k:k + 1, :]], [st_send[NX + k:NX + k + 1, :]]
        for d in range(1, NX):
            j = (k - d) % NX
            part_tops.append(st_recv[d, j:j + 1, :])
            part_totals.append(st_recv[d, NX + j:NX + j + 1, :])
        row_max = part_tops[0]
        for t in part_tops[1:]:
            row_max = jnp.maximum(row_max, t)
        row_total = sum(s * jnp.exp(t - row_max) for t, s in zip(part_tops, part_totals))
        maxima.append(row_max)
        factors.append((weight if k == 0 else st_recv[k, 8:9, :]) / row_total)
    row_max, factors = jnp.concatenate(maxima, axis=1), jnp.concatenate(factors, axis=1)
    totals[...] = factors * jnp.exp(tops[...] - row_max)

    def item_terms(p):
        rows = pl.ds(pl.multiple_of(p * B, B), B)
        block = (ebuf[rows, :] * totals[pl.ds(p, 1), :]).astype(BF16)
        gbuf[rows, :] = block
        return SCALE * dot(block, qbuf[...])

    def near_terms(p, _):
        gi_own[p] = item_terms(p)
        return 0

    sum_in = {}
    half_of = (slice(0, 64), slice(64, 128))

    def send_sum(way, k, half):
        p = RING[(4, 5, 6, 7)[k] if way == 0 else (4, 3, 2, 1)[k]]
        block = gi_own[p, half_of[half], :]
        if (way, k - 1, half) in sum_in:
            sum_in[way, k - 1, half].wait_recv()
            block += gi_sum[way, k - 1, half].astype(F32)
        gi_send[way, k, half] = block.astype(BF16)
        sum_in[way, k, half] = send(gi_send.at[way, k, half], gi_sum.at[way, k, half], at_z(1 - 2 * way))

    near_terms(7, 0)
    send_sum(0, 0, 0)
    send_sum(1, 0, 1)
    lax.fori_loop(5, 7, near_terms, 0)
    send_sum(0, 1, 1)
    send_sum(1, 1, 0)
    lax.fori_loop(0, 5, near_terms, 0)
    same = iota((B, B), 0) == iota((B, B), 1)
    diagonal = ebuf[0:B, 0:B] * totals[0:1, 0:B] - jnp.where(same, weight, 0.0)
    gbuf[0:B, 0:B] = diagonal.astype(BF16)
    gi_own[0] = SCALE * dot(gbuf[0:B, :], qbuf[...])

    terms = SCALE * dot(gbuf[...], ibuf[...], TN)
    gq_own[...] = terms[0:B, :]
    for k in range(1, NX):
        gq_send[k] = terms[k * B:(k + 1) * B, :].astype(BF16)
    query_grad_in = {k: send(gq_send.at[k], gq_recv.at[k], at_x(-k)) for k in (2, 1, 3)}
    send_sum(0, 1, 0)
    send_sum(1, 1, 1)
    send_sum(0, 2, 1)
    send_sum(1, 2, 0)

    list_sib = []

    def lists_to_sibling(low, high):
        list_sib.append(send(
            lists.at[pl.ds(OWN[low], high - low)], lists.at[pl.ds(SIB[low], high - low)], sibling
        ))

    wait_for(list_in, 1, -1, 3, -3, 4, -4)
    lists_to_sibling(0, 5)
    lists_to_sibling(5, 8)
    send_sum(0, 2, 0)
    send_sum(1, 2, 1)
    send_sum(0, 3, 1)
    send_sum(1, 3, 0)
    source_row = iota((2 * B, CAP), 0)
    owner_row = iota((NT, CAP), 0)
    low_row = iota((1024, CAP), 0)

    def one_hots(s, _):
        entry = lists[s].astype(F32)
        source, high, low = [
            jnp.sum(jnp.where(owner_row == tb, entry[16 * k:16 * k + 16, :], 0.0), axis=0, keepdims=True).astype(I32)
            for k in range(3)
        ]
        row = (high - 1) * 256 + low
        select[s] = (source == source_row).astype(BF16)
        lanes = pl.ds(pl.multiple_of(s * CAP, CAP), CAP)
        onehot[:, lanes] = (lax.bitwise_and(row - z * B, 1023) == low_row).astype(BF16)
        block = jnp.broadcast_to(lax.shift_right_arithmetic(row, 10), (16, CAP))
        for j in range(NX):
            factor[s, j] = (block == j).astype(BF16)
        return 0

    lax.fori_loop(0, 5, one_hots, 0)
    send_sum(0, 3, 0)
    send_sum(1, 3, 1)

    query_grad = gq_own[...]
    for k in (1, 3, 2):
        query_grad_in[k].wait_recv()
        query_grad += gq_recv[k].astype(F32)
    query_grad = query_grad.astype(BF16)

    pooled_in, pooled_sib = {}, {}

    def pooled_slot(half):
        def slot(d, rows):
            if rows is None:
                return pooled.at[half, OWN[POS[d]]]
            return pooled.at[half, OWN[POS[d]], pl.ds(rows * 64, 64), :]

        return slot

    def to_sibling(half, low, high):
        pooled_sib[half, low] = send(
            pooled.at[half, pl.ds(OWN[low], high - low)], pooled.at[half, pl.ds(SIB[low], high - low)], sibling
        )

    pooled[0, 0] = dot(wq[...], query_grad, NT_DIMS).astype(BF16)
    pooled_in[0] = gather_start(pooled_slot(0), at_y)
    to_sibling(0, 0, 1)
    w_part[0:B, :] = dot(pq[...], query_grad, TN)

    for copy in list_sib:
        copy.wait_recv()
    lax.fori_loop(5, 16, one_hots, 0)
    drain()

    item_grad = gi_own[0]
    for way in (0, 1):
        for half in (0, 1):
            sum_in[way, 3, half].wait_recv()
        item_grad += gi_sum[way, 3].reshape(B, W).astype(F32)
    item_grad = item_grad.astype(BF16)
    pooled[1, 0] = dot(wi[...], item_grad, NT_DIMS).astype(BF16)
    pooled_in[1] = gather_start(pooled_slot(1), at_y)
    to_sibling(1, 0, 1)
    gather_pass(pooled_in[0], pooled_slot(0), at_y)
    wait_for(pooled_in[0], 1, -1)
    to_sibling(0, 1, 3)
    to_sibling(0, 3, 5)
    w_part[B:, :] = dot(pi[...], item_grad, TN)
    w_in = {}
    for d in (2, 1, 3):
        to_x = lax.rem(x + d, NX)
        w_in[d] = send(w_part.at[pl.ds(pl.multiple_of(to_x * 64, 64), 64), :], wx_recv.at[d], at_x(d))

    def place_values(s, _):
        got = (dot(pooled[0, s], select[s, 0:B, :]) + dot(pooled[1, s], select[s, B:, :])).astype(BF16)
        lanes = pl.ds(pl.multiple_of(s * CAP, CAP), CAP)
        for j in range(NX):
            values[j * E:(j + 1) * E, lanes] = got * jnp.tile(factor[s, j], (8, 1))
        return 0

    def two_blocks(b, columns):
        rows = pl.ds(pl.multiple_of(b * 2 * E, 2 * E), 2 * E)
        return dot(onehot[:, columns], values[rows, columns], NT_DIMS)

    def first_part(b, _):
        part = two_blocks(b, slice(0, FIRST))
        for j in (0, 1):
            t_own[2 * b + j] = part[:, j * E:(j + 1) * E].reshape(NZ, B, E)
        return 0

    gather_pass(pooled_in[1], pooled_slot(1), at_y)
    wait_for(pooled_in[1], 1, -1)
    to_sibling(1, 1, 3)
    to_sibling(1, 3, 5)
    lax.fori_loop(0, 5, place_values, 0)
    for low in (0, 1, 3):
        pooled_sib[0, low].wait_recv()
        pooled_sib[1, low].wait_recv()
    lax.fori_loop(5, 10, place_values, 0)

    lax.fori_loop(0, 1, first_part, 0)
    wait_for(pooled_in[0], 3, -3, 4, -4)
    to_sibling(0, 5, 8)
    wait_for(pooled_in[1], 3, -3, 4, -4)
    to_sibling(1, 5, 8)
    lax.fori_loop(10, 13, place_values, 0)
    lax.fori_loop(1, 2, first_part, 0)

    w_sum = w_part[pl.ds(pl.multiple_of(x * 64, 64), 64), :]
    for d in (1, 3, 2):
        w_in[d].wait_recv()
        w_sum += wx_recv[d]
    wz_send[...] = w_sum

    def w_chunk(d):
        return pl.ds(pl.multiple_of(lax.rem(z + d + NZ, NZ) * 8, 8), 8)

    wz_in = {}
    for d, via, dst in (
        (4, 2, wz_relay.at[0]), (3, 1, wz_relay.at[1]), (-3, -1, wz_relay.at[2]),
        (1, 1, wz_recv.at[0]), (-1, -1, wz_recv.at[1]),
    ):
        wz_in[d] = send(wz_send.at[w_chunk(d), :], dst, at_z(via))

    pooled_sib[0, 5].wait_recv()
    pooled_sib[1, 5].wait_recv()
    lax.fori_loop(13, 16, place_values, 0)

    bases = (4, 2, 6, 0)
    half_base = len(copies)
    copies.extend([None] * 8)

    def half_copy(p, side):
        return remote(
            half_base + 2 * p + side,
            t_send.at[lax.rem(x + 2, NX), pl.ds(bases[p], 2), pl.ds(side * 48, 48), :],
            tx_half.at[p, side],
            at_x(1 - 2 * side),
        )

    def last_part(i, _):
        b = lax.rem(lax.div(x, 2) + 1 + i, 2)
        part = two_blocks(b, slice(FIRST, NT * CAP))
        for j in (0, 1):
            block = t_own[2 * b + j] + part[:, j * E:(j + 1) * E].reshape(NZ, B, E)
            t_own[2 * b + j] = block
            t_send[2 * b + j] = block.astype(BF16)

        @pl.when(i == 0)
        def _():
            for p in range(4):
                for side in (0, 1):
                    half_copy(p, side).start()

        return 0

    lax.fori_loop(0, 2, last_part, 0)
    for p in range(4):
        for side in (0, 1):
            copies[half_base + 2 * p + side] = half_copy(p, side)

    def low_columns(d):
        return t_send.at[:, d, pl.ds(96, 32), :]

    low_half = [
        send(t_send.at[pl.ds(2 * side, 2), 4, pl.ds(96, 32), :], lz_half.at[side], at_z(2 - 4 * side))
        for side in (0, 1)
    ]
    low_relay = [
        send(low_columns(3), lz_relay.at[0], at_z(1)),
        send(low_columns(5), lz_relay.at[1], at_z(-1)),
    ]
    low_in = [
        send(low_columns(1), lz_recv.at[0], at_z(1)),
        send(low_columns(7), lz_recv.at[1], at_z(-1)),
    ]

    def low_pass():
        for side in (0, 1):
            low_relay[side].wait_recv()
            low_half[side].wait_recv()
            d = (2, 6)[side]
            lz_own[side] = t_own[:, d, 96:, :] + lz_relay[side].astype(F32)
            pair_of = slice(2 * side, 2 * side + 2)
            lz_own[side, pair_of] += lz_half[side].astype(F32)
            lz_send[side] = lz_own[side].astype(BF16)
            low_in.append(send(lz_send.at[side], lz_recv.at[2 + side], at_z(2 - 4 * side)))

    low_x = {}

    def low_sum():
        part = t_own[:, 0, 96:, :]
        for k in range(4):
            low_in[k].wait_recv()
            part += lz_recv[k].astype(F32)
        lz_own[2] = part
        lx_send[...] = part.astype(BF16)
        for d in (2, 1, 3):
            low_x[d] = send(lx_send.at[lax.rem(x + d, NX)], lx_recv.at[d], at_x(d))

    relay_in, tz_half_in, tz_relay_in, tz_in = {}, {}, {}, {}

    def table_relay(p):
        for side, step in ((0, 1), (1, -1)):
            copies[half_base + 2 * p + side].wait_recv()
            near = lax.rem(x + step + NX, NX)
            for half in (0, 1):
                rows = slice(half * 48, half * 48 + 48)
                part = t_own[near, bases[p]:bases[p] + 2, rows, :]
                if half == side:
                    part += tx_half[p, side].astype(F32)
                tx_relay[p, side, :, rows, :] = part.astype(BF16)
            relay_in[p, side] = send(tx_relay.at[p, side], tx_recv.at[p, side], at_x(step))

    def table_sum(p):
        part = t_own[x, bases[p]:bases[p] + 2, 0:96, :]
        for side in (0, 1):
            relay_in[p, side].wait_recv()
            part += tx_recv[p, side].astype(F32)
        tz_send[p] = part[1].astype(BF16)
        if p == 0:
            tz_first[...] = part[0].astype(BF16)
            for side in (0, 1):
                tz_half_in[side] = send(
                    tz_first.at[pl.ds(side * 48, 48), :], tz_half.at[side], at_z(2 - 4 * side)
                )
        else:
            tz_own[p - 1] = part[0]
        if p < 2:
            tz_relay_in[1 - p] = send(tz_send.at[p], tz_relay.at[1 - p], at_z(2 * p - 1))
        else:
            tz_in[3 - p] = send(tz_send.at[p], tz_recv.at[3 - p], at_z(2 * p - 5))

    def table_pass():
        for side in (0, 1):
            tz_relay_in[side].wait_recv()
            tz_half_in[side].wait_recv()
            rows = slice(side * 48, side * 48 + 48)
            tz_own[side] += tz_relay[side].astype(F32)
            tz_own[side, rows, :] += tz_half[side].astype(F32)
            tz_back[side] = tz_own[side].astype(BF16)
            tz_in[2 + side] = send(tz_back.at[side], tz_recv.at[2 + side], at_z(2 - 4 * side))

    def small_pass(got, slot, at, there):
        got[2].wait_recv()
        got[3] = send(slot(2), there(2, 3), at(1))
        got[4] = send(slot(2), there(2, 4), at(2))
        got[-2].wait_recv()
        got[5] = send(slot(-2), there(-2, 5), at(-1))

    def wy_slot(d):
        return wy_recv.at[0, d % 8]

    def w_rows(d):
        place = x * NZ + lax.rem(z - d + NZ, NZ)
        return gw_ref.at[pl.ds(pl.multiple_of(place * 8, 8), 8), pl.ds(pl.multiple_of(core * B, B), B)]

    table_relay(0)
    wait_for(wz_in, 4, 3, -3)
    wz_pass[0] = wz_send[w_chunk(2), :] + wz_relay[0] + wz_relay[1]
    wz_pass[1] = wz_send[w_chunk(-2), :] + wz_relay[2]
    for side, d in ((0, 2), (1, -2)):
        wz_in[d] = send(wz_pass.at[side], wz_recv.at[2 + side], at_z(d))
    table_relay(1)
    table_sum(0)
    low_pass()
    w_sum = wz_send[w_chunk(0), :]
    wait_for(wz_in, 1, -1, 2, -2)
    for k in range(4):
        w_sum += wz_recv[k]
    wy_recv[0, 0] = w_sum
    wy_in = {d: send(wy_slot(0), wy_slot(d), at_y(d)) for d in (2, -2, 1, -1)}

    table_relay(2)
    table_sum(1)
    table_relay(3)
    small_pass(wy_in, wy_slot, at_y, lambda here, d: wy_slot(d))
    table_sum(2)
    low_sum()
    table_pass()
    wait_for(wy_in, 1, -1, 3, 4, 5)
    wy_sib = send(wy_recv.at[0], wy_recv.at[1], sibling)
    table_sum(3)
    drain()
    wy_sib.wait_recv()
    w_sum = wy_recv[0, 0]
    for d in range(1, NY):
        w_sum += wy_recv[0, d]
    for d in range(NY):
        w_sum += wy_recv[1, d]
    w_own[...] = w_sum
    own_lanes = pl.ds(pl.multiple_of(core * B, B), B)
    gw_ref[pl.ds(pl.multiple_of(dp * 8, 8), 8), own_lanes] = w_own[:, own_lanes]
    w_back = {d: send(w_rows(0), w_rows(0), at_z(d)) for d in (2, -2, 1, -1)}


    low = lz_own[2, x]
    for d in (1, 3, 2):
        low_x[d].wait_recv()
        low += lx_recv[d].astype(F32)
    part = tz_own[2]
    for k in (1, 0, 2, 3):
        tz_in[k].wait_recv()
        part += tz_recv[k].astype(F32)
    t_back[x, 0] = part.astype(BF16)
    l_back[0, x] = low.astype(BF16)

    def back_slot(d, half):
        if half is None:
            return t_back.at[x, POS[d]]
        return t_back.at[x, POS[d], pl.ds(half * 48, 48), :]

    def low_slot(d, half):
        if half is None:
            return l_back.at[POS[d]]
        return l_back.at[POS[d], pl.ds(2 * half, 2)]

    back = gather_start(back_slot, at_z)
    low_back = [send(l_back.at[0, x], l_back.at[0, x], at_x(d)) for d in (2, 1, 3)]
    near_in, far_in = {}, []

    def to_near(low, high):
        rows = t_back.at[x, pl.ds(low, high - low)]
        for side, step in ((0, 1), (1, -1)):
            near_in[low, side] = send(rows, rows, at_x(step))

    def to_far(low, high):
        middle = {1: None, 2: low + 1, 3: None}[high - low]
        for side, step in ((0, 1), (1, -1)):
            near_in[low, side].wait_recv()
            held = lax.rem(x - step + NX, NX)
            if middle is None:
                rows = t_back.at[held, pl.ds(low, high - low), pl.ds(side * 48, 48), :]
            else:
                rows = t_back.at[held, low + side]
            far_in.append(send(rows, rows, at_x(step)))

    to_near(0, 1)

    gather_pass(back, back_slot, at_z)
    to_near(1, 3)
    for copy in low_back:
        copy.wait_recv()
    low_back = gather_start(low_slot, at_z)
    small_pass(w_back, w_rows, at_z, lambda here, d: w_rows(here))
    to_far(0, 1)
    wait_for(back, 1, -1)
    to_near(3, 5)
    wait_for(w_back, 1, -1, 3, 4, 5)
    w_held = gw_ref.at[pl.ds(pl.multiple_of(x * 64, 64), 64), pl.ds(pl.multiple_of(core * B, B), B)]
    w_x = [send(w_held, w_held, at_x(step)) for step in (2, 1, 3)]
    to_far(1, 3)
    wait_for(back, 3, -3, 4, -4)
    to_near(5, 8)
    gather_pass(low_back, low_slot, at_z)
    to_far(3, 5)

    def rows_of(far, p, d):
        place = (far * NZ + lax.rem(z - d + NZ, NZ)) * B
        table_ref[pl.ds(pl.multiple_of(place, B), 96), :] = t_back[far, p]

    def low_rows_of(p, d):
        for far in range(NX):
            place = (far * NZ + lax.rem(z - d + NZ, NZ)) * B + 96
            table_ref[pl.ds(pl.multiple_of(place, 32), 32), :] = l_back[p, far]

    to_far(5, 8)
    for copy in w_x:
        copy.wait_recv()
    w_half = gw_ref.at[:, pl.ds(pl.multiple_of(core * B, B), B)]
    far_in.append(send(w_half, w_half, sibling))
    for p, d in enumerate(ARRIVE):
        rows_of(x, p, d)
        rows_of(lax.rem(x + 1, NX), p, d)
        rows_of(lax.rem(x + 3, NX), p, d)
    wait_for(low_back, 1, -1, 3, -3, 4, -4)
    for p, d in enumerate(ARRIVE):
        low_rows_of(p, d)
    drain()
    for copy in far_in:
        copy.wait_recv()
    for p, d in enumerate(ARRIVE):
        rows_of(lax.rem(x + 2, NX), p, d)
    drain()


def finish(table_ref, gw_ref, out_ref, gwq_ref, gwi_ref, wide, sem):
    copies = [
        pltpu.make_async_copy(gw_ref.at[pl.ds(0, B), :], gwq_ref, sem.at[8]),
        pltpu.make_async_copy(gw_ref.at[pl.ds(B, B), :], gwi_ref, sem.at[9]),
    ]
    for copy in copies:
        copy.start()
    for i in range(8):
        wide[i] = table_ref[i * 512:(i + 1) * 512, :].astype(F32)
        copies.append(pltpu.make_async_copy(wide.at[i], out_ref.at[pl.ds(i * 512, 512), :], sem.at[i]))
        copies[-1].start()
    for copy in copies:
        copy.wait()


def on_device(q, it, pq, pi, wq, wi, pw, owner, row):
    def vmem(*shape, dtype=F32):
        return pltpu.VMEM(shape, dtype)

    table, gw = pl.pallas_call(
        kernel,
        out_shape=(
            jax.ShapeDtypeStruct((4096, E), BF16),
            jax.ShapeDtypeStruct((2 * B, W), F32),
        ),
        in_specs=[pl.BlockSpec(memory_space=pltpu.HBM)] * 9,
        out_specs=(pl.BlockSpec(memory_space=pltpu.VMEM),) * 2,
        scratch_shapes=[
            vmem(B, E, dtype=BF16),
            vmem(B, E, dtype=BF16),
            vmem(E, W, dtype=BF16),
            vmem(E, W, dtype=BF16),
            vmem(1, B),
            vmem(16, B, dtype=I32),
            vmem(16, B, dtype=I32),
            vmem(NZ * B, W, dtype=BF16),
            vmem(NX * B, W, dtype=BF16),
            vmem(NZ * B, NX * B),
            vmem(NZ * B, NX * B, dtype=BF16),
            vmem(NZ, NX * B),
            vmem(NZ, NX * B),
            vmem(16, B),
            vmem(NX, 16, B),
            vmem(2, 4, 2, 64, W, dtype=BF16),
            vmem(2, 4, 2, 64, W, dtype=BF16),
            vmem(NZ, B, W),
            vmem(NX, B, W, dtype=BF16),
            vmem(NX, B, W, dtype=BF16),
            vmem(B, W),
            vmem(256, B),
            vmem(64, 16 * B, dtype=BF16),
            vmem(CAP, 16 * B, dtype=BF16),
            vmem(NT, 64, CAP, dtype=BF16),
            vmem(1024, NT * CAP, dtype=BF16),
            vmem(NT, 2 * B, CAP, dtype=BF16),
            vmem(NT, NX, 16, CAP, dtype=BF16),
            vmem(2, NT, E, B, dtype=BF16),
            vmem(NX * E, NT * CAP, dtype=BF16),
            vmem(2 * B, W),
            vmem(NX, 64, W),
            vmem(64, W),
            vmem(3, 8, W),
            vmem(2, 8, W),
            vmem(4, 8, W),
            vmem(2, NY, 8, W),
            vmem(8, W),
            vmem(NX, NZ, B, E),
            vmem(NX, NZ, B, E, dtype=BF16),
            vmem(4, 2, 2, 48, E, dtype=BF16),
            vmem(4, 2, 2, 96, E, dtype=BF16),
            vmem(4, 2, 2, 96, E, dtype=BF16),
            vmem(96, B, dtype=BF16),
            vmem(3, 96, B),
            vmem(4, 96, B, dtype=BF16),
            vmem(2, 48, B, dtype=BF16),
            vmem(2, 96, B, dtype=BF16),
            vmem(2, 96, B, dtype=BF16),
            vmem(4, 96, B, dtype=BF16),
            vmem(2, 2, 32, B, dtype=BF16),
            vmem(2, NX, 32, B, dtype=BF16),
            vmem(3, NX, 32, B),
            vmem(2, NX, 32, B, dtype=BF16),
            vmem(4, NX, 32, B, dtype=BF16),
            vmem(NX, 32, B, dtype=BF16),
            vmem(NX, 32, B, dtype=BF16),
            vmem(NX, NZ, 96, E, dtype=BF16),
            vmem(NZ, NX, 32, E, dtype=BF16),
            pltpu.SemaphoreType.DMA((9,)),
            pltpu.SemaphoreType.DMA((N_COPIES,)),
            pltpu.SemaphoreType.DMA((N_COPIES,)),
        ],
        compiler_params=pltpu.CompilerParams(
            collective_id=0, has_side_effects=True, vmem_limit_bytes=40 * 1024 * 1024
        ),
    )(*[
        pltpu.with_memory_space_constraint(a, pltpu.HBM)
        for a in (
            q, it, pq, pi, wq, wi, pw.reshape(1, B), owner.reshape(B, 16).T, row.reshape(B, 16).T
        )
    ])
    return pl.pallas_call(
        finish,
        out_shape=(
            jax.ShapeDtypeStruct((4096, E), F32),
            jax.ShapeDtypeStruct((B, W), F32),
            jax.ShapeDtypeStruct((B, W), F32),
        ),
        in_specs=[pl.BlockSpec(memory_space=pltpu.VMEM)] * 2,
        out_specs=(pl.BlockSpec(memory_space=pltpu.HBM),) * 3,
        scratch_shapes=[vmem(8, 512, E), pltpu.SemaphoreType.DMA((10,))],
        compiler_params=pltpu.CompilerParams(vmem_limit_bytes=12 * 1024 * 1024),
    )(table, gw)


def solution(mesh):
    both = ("dp", "table")
    placed = (
        P(both, None),
        P(both, None),
        P(both, None),
        P(both, None),
        P(),
        P(),
        P(both),
        P(both, None, None),
        P(both, None, None),
    )
    return jax.shard_map(
        on_device,
        mesh=mesh,
        in_specs=placed,
        out_specs=(P("table", None), P(), P()),
        check_vma=False,
    )
```

```python
import math

import jax
import jax.numpy as jnp
from jax import lax
from jax.experimental import pallas as pl
from jax.experimental.pallas import tpu as pltpu
from jax.sharding import PartitionSpec as P

MESH = pl.DeviceIdType.MESH
F32, BF16, I32 = jnp.float32, jnp.bfloat16, jnp.int32
NX, NZ, NY = 4, 8, 8
B, W, E = 128, 256, 128
NT = 2 * NY
CAP = 256
SCALE = 1.0 / math.sqrt(W)
N_COPIES = 176

NN = (((1,), (0,)), ((), ()))
NT_DIMS = (((1,), (1,)), ((), ()))
TN = (((0,), (0,)), ((), ()))


def dot(a, b, dims=NN):
    return lax.dot_general(a, b, dims, preferred_element_type=F32)


def iota(shape, dim):
    return lax.broadcasted_iota(I32, shape, dim)


ARRIVE = (0, 2, 6, 1, 7, 3, 5, 4)
POS = {d: p for p, d in enumerate(ARRIVE)}
RING = {d: p for p, d in enumerate((0, 1, 7, 2, 6, 3, 5, 4))}
OWN = (0, 1, 2, 3, 4, 10, 11, 12)
SIB = (5, 6, 7, 8, 9, 13, 14, 15)
FIRST = 10 * CAP


def kernel(
    q_ref, it_ref, pq_ref, pi_ref, wq_ref, wi_ref, pw_ref, ow_ref, rw_ref,
    table_ref, gw_ref,
    pq, pi, wq, wi, pw, ow, rw,
    ibuf, qbuf, ebuf, gbuf, tops, totals, st_send, st_recv,
    gi_send, gi_sum, gi_own, gq_send, gq_recv, gq_own,
    taken, slots_a, slots_b, lists, onehot, select, factor, pooled, values,
    w_part, wx_recv, wz_send, wz_recv, wy_recv,
    t_own, t_send, tx_half, tx_relay, tx_recv, tz_first, tz_own, tz_send, tz_half, tz_relay, tz_back, tz_recv,
    lz_half, lz_relay, lz_own, lz_send, lz_recv, lx_send, lx_recv, t_back, l_back,
    load_sem, send_sem, recv_sem,
):
    dp, tb = lax.axis_index("dp"), lax.axis_index("table")
    x, z = lax.div(dp, NZ), lax.rem(dp, NZ)
    y, core = lax.div(tb, 2), lax.rem(tb, 2)

    def at_x(d):
        return (lax.rem(x + d + NX, NX) * NZ + z, tb)

    def at_z(d):
        return (x * NZ + lax.rem(z + d + NZ, NZ), tb)

    def at_y(d):
        return (dp, lax.rem(y + d + NY, NY) * 2 + core)

    sibling = (dp, tb + 1 - 2 * core)
    partners = (
        [at_x(d) for d in range(1, NX)]
        + [at_z(d) for d in range(1, NZ)]
        + [at_y(d) for d in range(1, NY)]
        + [sibling]
    )
    barrier = pltpu.get_barrier_semaphore()
    for partner in partners:
        pl.semaphore_signal(barrier, inc=1, device_id=partner, device_id_type=MESH)
    loads = [
        pltpu.make_async_copy(src, dst, load_sem.at[i])
        for i, (src, dst) in enumerate((
            (it_ref, ibuf.at[pl.ds(0, B), :]),
            (q_ref, qbuf.at[pl.ds(0, B), :]),
            (ow_ref, ow),
            (rw_ref, rw),
            (pw_ref, pw),
            (pq_ref, pq),
            (pi_ref, pi),
            (wq_ref, wq),
            (wi_ref, wi),
        ))
    ]
    for load in loads:
        load.start()
    pl.semaphore_wait(barrier, len(partners))

    copies, drained = [], [0]

    def remote(index, src, dst, device):
        return pltpu.make_async_remote_copy(
            src_ref=src,
            dst_ref=dst,
            send_sem=send_sem.at[index],
            recv_sem=recv_sem.at[index],
            device_id=device,
            device_id_type=MESH,
        )

    def send(src, dst, device):
        copy = remote(len(copies), src, dst, device)
        copy.start()
        copies.append(copy)
        return copy

    def drain():
        for copy in copies[drained[0]:]:
            copy.wait_send()
        drained[0] = len(copies)

    def gather_start(slot, at, source=None):
        source = slot(0, None) if source is None else source
        return {d: send(source, slot(d % 8, None), at(d)) for d in (2, -2, 1, -1)}

    def gather_pass(got, slot, at):
        got[2].wait_recv()
        got[3] = send(slot(2, None), slot(3, None), at(1))
        got[4] = send(slot(2, 0), slot(4, 0), at(2))
        got[-2].wait_recv()
        got[-3] = send(slot(6, None), slot(5, None), at(-1))
        got[-4] = send(slot(6, 1), slot(4, 1), at(-2))

    def wait_for(got, *names):
        for name in names:
            got[name].wait_recv()

    def item_half(d, half):
        return ibuf.at[pl.ds(RING[d] * B + half * 64, 64), :]

    item_in = {}
    for up in (0, 1):
        item_in[1, up] = send(it_ref.at[pl.ds(up * 64, 64), :], item_half(1, up), at_z(1))
        item_in[7, 1 - up] = send(it_ref.at[pl.ds(64 - up * 64, 64), :], item_half(7, 1 - up), at_z(-1))

    def item_step(k):
        for up in (0, 1):
            down = 1 - up
            item_in[k, up].wait_recv()
            if k < 3 or up == 0:
                item_in[k + 1, up] = send(item_half(k, up), item_half(k + 1, up), at_z(1))
            item_in[8 - k, down].wait_recv()
            if k < 3 or down == 1:
                item_in[7 - k, down] = send(item_half(8 - k, down), item_half(7 - k, down), at_z(-1))

    query_in = {}
    for d in (1, 3, 2):
        query_in[d] = send(q_ref, qbuf.at[pl.ds(d * B, B), :], at_x(d))

    for load in loads:
        load.wait()
    owner_row = iota((NT, B), 0)
    hits = jnp.concatenate([(ow[k:k + 1, :] == owner_row).astype(F32) for k in range(16)], axis=0)
    before = (iota((B, 2 * B), 0) < iota((B, 2 * B), 1)).astype(BF16)
    counts = dot(hits.astype(BF16), before)
    at_row, at_col = iota((256, 256), 0), iota((256, 256), 1)
    earlier = jnp.logical_and(
        lax.bitwise_and(at_row, 15) == lax.bitwise_and(at_col, 15),
        lax.shift_right_logical(at_col, 4) < lax.shift_right_logical(at_row, 4),
    ).astype(BF16)
    taken[...] = (counts[:, 0:B] + dot(earlier, counts[:, B:].astype(BF16))) * hits
    item_step(1)
    list_row = iota((64, B), 0)
    list_owner, piece = lax.bitwise_and(list_row, 15), lax.shift_right_logical(list_row, 4)
    pair = iota((1, B), 1)
    place = iota((CAP, B), 0)

    def list_slot(k, _):
        lanes = pl.ds(pl.multiple_of(k * B, B), B)
        ranks = taken[pl.ds(pl.multiple_of(k * NT, NT), NT), :]
        rank = jnp.sum(ranks, axis=0, keepdims=True).astype(I32)
        slots_b[:, lanes] = (place == rank).astype(BF16)
        owner, row = ow[pl.ds(k, 1), :], rw[pl.ds(k, 1), :]
        part = jnp.where(
            piece == 0,
            pair + lax.div(k, 8) * B,
            jnp.where(
                piece == 1,
                lax.shift_right_logical(row, 8) + 1,
                jnp.where(piece == 2, lax.bitwise_and(row, 255), 0),
            ),
        )
        slots_a[:, lanes] = jnp.where(list_owner == owner, part, 0).astype(F32).astype(BF16)
        return 0

    lax.fori_loop(0, 16, list_slot, 0)
    lists[0] = dot(slots_a[...], slots_b[...], NT_DIMS).astype(BF16)

    def list_slot_of(d, half):
        if half is None:
            return lists.at[OWN[POS[d]]]
        return lists.at[OWN[POS[d]], pl.ds(half * 32, 32), :]

    list_in = gather_start(list_slot_of, at_y)
    item_step(2)

    wait_for(query_in, 1, 3, 2)

    def logits(p, _):
        rows = pl.ds(pl.multiple_of(p * B, B), B)
        block = SCALE * dot(ibuf[rows, :], qbuf[...], NT_DIMS)
        top = jnp.max(block, axis=0, keepdims=True)
        block = jnp.exp(block - top)
        ebuf[rows, :] = block
        tops[pl.ds(p, 1), :] = top
        totals[pl.ds(p, 1), :] = jnp.sum(block, axis=0, keepdims=True)
        return 0

    lax.fori_loop(0, 3, logits, 0)
    item_step(3)
    lax.fori_loop(3, 7, logits, 0)
    wait_for(item_in, (4, 0), (4, 1))
    lax.fori_loop(7, 8, logits, 0)

    top = jnp.max(tops[...], axis=0, keepdims=True)
    total = jnp.sum(totals[...] * jnp.exp(tops[...] - top), axis=0, keepdims=True)
    weight = pw[...]
    for k in range(NX):
        st_send[k:k + 1, :] = top[:, k * B:(k + 1) * B]
        st_send[NX + k:NX + k + 1, :] = total[:, k * B:(k + 1) * B]
    st_send[8:16, :] = jnp.broadcast_to(weight, (8, B))
    stat_in = {d: send(st_send, st_recv.at[d], at_x(d)) for d in (2, 1, 3)}
    gather_pass(list_in, list_slot_of, at_y)
    wait_for(stat_in, 1, 3, 2)
    maxima, factors = [], []
    for k in range(NX):
        part_tops, part_totals = [st_send[k:k + 1, :]], [st_send[NX + k:NX + k + 1, :]]
        for d in range(1, NX):
            j = (k - d) % NX
            part_tops.append(st_recv[d, j:j + 1, :])
            part_totals.append(st_recv[d, NX + j:NX + j + 1, :])
        row_max = part_tops[0]
        for t in part_tops[1:]:
            row_max = jnp.maximum(row_max, t)
        row_total = sum(s * jnp.exp(t - row_max) for t, s in zip(part_tops, part_totals))
        maxima.append(row_max)
        factors.append((weight if k == 0 else st_recv[k, 8:9, :]) / row_total)
    row_max, factors = jnp.concatenate(maxima, axis=1), jnp.concatenate(factors, axis=1)
    totals[...] = factors * jnp.exp(tops[...] - row_max)

    def item_terms(p):
        rows = pl.ds(pl.multiple_of(p * B, B), B)
        block = (ebuf[rows, :] * totals[pl.ds(p, 1), :]).astype(BF16)
        gbuf[rows, :] = block
        return SCALE * dot(block, qbuf[...])

    def near_terms(p, _):
        gi_own[p] = item_terms(p)
        return 0

    sum_in = {}
    half_of = (slice(0, 64), slice(64, 128))

    def send_sum(way, k, half):
        p = RING[(4, 5, 6, 7)[k] if way == 0 else (4, 3, 2, 1)[k]]
        block = gi_own[p, half_of[half], :]
        if (way, k - 1, half) in sum_in:
            sum_in[way, k - 1, half].wait_recv()
            block += gi_sum[way, k - 1, half].astype(F32)
        gi_send[way, k, half] = block.astype(BF16)
        sum_in[way, k, half] = send(gi_send.at[way, k, half], gi_sum.at[way, k, half], at_z(1 - 2 * way))

    near_terms(7, 0)
    send_sum(0, 0, 0)
    send_sum(1, 0, 1)
    lax.fori_loop(5, 7, near_terms, 0)
    send_sum(0, 1, 1)
    send_sum(1, 1, 0)
    lax.fori_loop(0, 5, near_terms, 0)
    same = iota((B, B), 0) == iota((B, B), 1)
    diagonal = ebuf[0:B, 0:B] * totals[0:1, 0:B] - jnp.where(same, weight, 0.0)
    gbuf[0:B, 0:B] = diagonal.astype(BF16)
    gi_own[0] = SCALE * dot(gbuf[0:B, :], qbuf[...])

    terms = SCALE * dot(gbuf[...], ibuf[...], TN)
    gq_own[...] = terms[0:B, :]
    for k in range(1, NX):
        gq_send[k] = terms[k * B:(k + 1) * B, :].astype(BF16)
    query_grad_in = {k: send(gq_send.at[k], gq_recv.at[k], at_x(-k)) for k in (2, 1, 3)}
    send_sum(0, 1, 0)
    send_sum(1, 1, 1)
    send_sum(0, 2, 1)
    send_sum(1, 2, 0)

    list_sib = []

    def lists_to_sibling(low, high):
        list_sib.append(send(
            lists.at[pl.ds(OWN[low], high - low)], lists.at[pl.ds(SIB[low], high - low)], sibling
        ))

    wait_for(list_in, 1, -1, 3, -3, 4, -4)
    lists_to_sibling(0, 5)
    lists_to_sibling(5, 8)
    send_sum(0, 2, 0)
    send_sum(1, 2, 1)
    send_sum(0, 3, 1)
    send_sum(1, 3, 0)
    source_row = iota((2 * B, CAP), 0)
    owner_row = iota((NT, CAP), 0)
    low_row = lax.bitwise_and(iota((1152, CAP), 0), 1023)

    def one_hots(s, _):
        entry = lists[s].astype(F32)
        source, high, low = [
            jnp.sum(jnp.where(owner_row == tb, entry[16 * k:16 * k + 16, :], 0.0), axis=0, keepdims=True).astype(I32)
            for k in range(3)
        ]
        row = (high - 1) * 256 + low
        select[s] = (source == source_row).astype(BF16)
        lanes = pl.ds(pl.multiple_of(s * CAP, CAP), CAP)
        onehot[:, lanes] = (lax.bitwise_and(row, 1023) == low_row).astype(BF16)
        block = jnp.broadcast_to(lax.shift_right_arithmetic(row, 10), (16, CAP))
        for j in range(NX):
            factor[s, j] = (block == j).astype(BF16)
        return 0

    lax.fori_loop(0, 5, one_hots, 0)
    send_sum(0, 3, 0)
    send_sum(1, 3, 1)

    query_grad = gq_own[...]
    for k in (1, 3, 2):
        query_grad_in[k].wait_recv()
        query_grad += gq_recv[k].astype(F32)
    query_grad = query_grad.astype(BF16)

    pooled_in, pooled_sib = {}, {}

    def pooled_slot(half):
        def slot(d, rows):
            if rows is None:
                return pooled.at[half, OWN[POS[d]]]
            return pooled.at[half, OWN[POS[d]], pl.ds(rows * 64, 64), :]

        return slot

    def to_sibling(half, low, high):
        pooled_sib[half, low] = send(
            pooled.at[half, pl.ds(OWN[low], high - low)], pooled.at[half, pl.ds(SIB[low], high - low)], sibling
        )

    pooled[0, 0] = dot(wq[...], query_grad, NT_DIMS).astype(BF16)
    pooled_in[0] = gather_start(pooled_slot(0), at_y)
    to_sibling(0, 0, 1)
    w_part[0:B, :] = dot(pq[...], query_grad, TN)

    for copy in list_sib:
        copy.wait_recv()
    lax.fori_loop(5, 16, one_hots, 0)
    drain()

    item_grad = gi_own[0]
    for way in (0, 1):
        for half in (0, 1):
            sum_in[way, 3, half].wait_recv()
        item_grad += gi_sum[way, 3].reshape(B, W).astype(F32)
    item_grad = item_grad.astype(BF16)
    pooled[1, 0] = dot(wi[...], item_grad, NT_DIMS).astype(BF16)
    pooled_in[1] = gather_start(pooled_slot(1), at_y)
    to_sibling(1, 0, 1)
    gather_pass(pooled_in[0], pooled_slot(0), at_y)
    wait_for(pooled_in[0], 1, -1)
    to_sibling(0, 1, 3)
    to_sibling(0, 3, 5)
    w_part[B:, :] = dot(pi[...], item_grad, TN)
    w_in = {}
    for d in (2, 1, 3):
        to_x = lax.rem(x + d, NX)
        w_in[d] = send(w_part.at[pl.ds(pl.multiple_of(to_x * 64, 64), 64), :], wx_recv.at[d], at_x(d))

    def place_values(s, _):
        got = (dot(pooled[0, s], select[s, 0:B, :]) + dot(pooled[1, s], select[s, B:, :])).astype(BF16)
        lanes = pl.ds(pl.multiple_of(s * CAP, CAP), CAP)
        for j in range(NX):
            values[j * E:(j + 1) * E, lanes] = got * jnp.tile(factor[s, j], (8, 1))
        return 0

    def quarter_rows(p):
        return pl.ds(pl.multiple_of(lax.rem(z + 4 + 3 * p * (p + 1), NZ) * B, B), 256)

    def first_part(p, _):
        part = dot(values[:, 0:FIRST], onehot[quarter_rows(p), 0:FIRST], NT_DIMS)
        t_own[p] = part.reshape(NX, E, 256)
        return 0

    gather_pass(pooled_in[1], pooled_slot(1), at_y)
    wait_for(pooled_in[1], 1, -1)
    to_sibling(1, 1, 3)
    to_sibling(1, 3, 5)
    lax.fori_loop(0, 5, place_values, 0)
    for low in (0, 1, 3):
        pooled_sib[0, low].wait_recv()
        pooled_sib[1, low].wait_recv()
    lax.fori_loop(5, 10, place_values, 0)

    lax.fori_loop(0, 2, first_part, 0)
    wait_for(pooled_in[0], 3, -3, 4, -4)
    to_sibling(0, 5, 8)
    wait_for(pooled_in[1], 3, -3, 4, -4)
    to_sibling(1, 5, 8)
    lax.fori_loop(10, 13, place_values, 0)

    w_sum = w_part[pl.ds(pl.multiple_of(x * 64, 64), 64), :]
    for d in (1, 3, 2):
        w_in[d].wait_recv()
        w_sum += wx_recv[d]
    wz_send[...] = w_sum
    wz_in = {}
    for d in ARRIVE[1:]:
        to_z = lax.rem(z + d, NZ)
        wz_in[d] = send(wz_send.at[pl.ds(pl.multiple_of(to_z * 8, 8), 8), :], wz_recv.at[d], at_z(d))

    lax.fori_loop(2, 4, first_part, 0)
    pooled_sib[0, 5].wait_recv()
    pooled_sib[1, 5].wait_recv()
    lax.fori_loop(13, 16, place_values, 0)

    half_base = len(copies)
    copies.extend([None] * 8)

    def half_copy(p, side):
        return remote(
            half_base + 2 * p + side,
            t_send.at[p, lax.rem(x + 2, NX), pl.ds(side * 48, 48), :],
            tx_half.at[p, side],
            at_x(1 - 2 * side),
        )

    def send_part(p, part):
        part = t_own[p] + part.reshape(NX, E, 256)
        t_own[p] = part
        t_send[p] = part.astype(BF16)
        half_copy(p, 0).start()
        half_copy(p, 1).start()

    def last_part(p, _):
        send_part(p, dot(values[:, FIRST:], onehot[quarter_rows(p), FIRST:], NT_DIMS))
        return 0

    lax.fori_loop(0, 4, last_part, 0)
    for p in range(4):
        for side in (0, 1):
            copies[half_base + 2 * p + side] = half_copy(p, side)

    def low_columns(p, side):
        return t_send.at[p, :, pl.ds(96, 32), pl.ds(side * B, B)]

    low_half = [
        send(t_send.at[0, pl.ds(2 * side, 2), pl.ds(96, 32), pl.ds(0, B)], lz_half.at[side], at_z(2 - 4 * side))
        for side in (0, 1)
    ]
    low_relay = [
        send(low_columns(1, 1), lz_relay.at[0], at_z(1)),
        send(low_columns(0, 1), lz_relay.at[1], at_z(-1)),
    ]
    low_in = [
        send(low_columns(3, 1), lz_recv.at[0], at_z(1)),
        send(low_columns(2, 1), lz_recv.at[1], at_z(-1)),
    ]

    def low_pass():
        for side in (0, 1):
            low_relay[side].wait_recv()
            low_half[side].wait_recv()
            lz_own[side] = t_own[1 + side, :, 96:, 0:B] + lz_relay[side].astype(F32)
            pair_of = slice(2 * side, 2 * side + 2)
            lz_own[side, pair_of] += lz_half[side].astype(F32)
            lz_send[side] = lz_own[side].astype(BF16)
            low_in.append(send(lz_send.at[side], lz_recv.at[2 + side], at_z(2 - 4 * side)))

    low_x = {}

    def low_sum():
        part = t_own[3, :, 96:, 0:B]
        for k in range(4):
            low_in[k].wait_recv()
            part += lz_recv[k].astype(F32)
        lz_own[2] = part
        lx_send[...] = part.astype(BF16)
        for d in (2, 1, 3):
            low_x[d] = send(lx_send.at[lax.rem(x + d, NX)], lx_recv.at[d], at_x(d))

    relay_in, tz_half_in, tz_relay_in, tz_in = {}, {}, {}, {}

    def table_relay(p):
        for side, step in ((0, 1), (1, -1)):
            copies[half_base + 2 * p + side].wait_recv()
            near = lax.rem(x + step + NX, NX)
            for half in (0, 1):
                rows = slice(half * 48, half * 48 + 48)
                part = t_own[p, near, rows, :]
                if half == side:
                    part += tx_half[p, side].astype(F32)
                tx_relay[p, side, rows, :] = part.astype(BF16)
            relay_in[p, side] = send(tx_relay.at[p, side], tx_recv.at[p, side], at_x(step))

    def table_sum(p):
        part = t_own[p, x, 0:96, :]
        for side in (0, 1):
            relay_in[p, side].wait_recv()
            part += tx_recv[p, side].astype(F32)
        tz_send[p] = part[:, B:].astype(BF16)
        if p == 0:
            tz_first[...] = part[:, 0:B].astype(BF16)
            for side in (0, 1):
                tz_half_in[side] = send(
                    tz_first.at[pl.ds(side * 48, 48), :], tz_half.at[side], at_z(2 - 4 * side)
                )
        else:
            tz_own[p - 1] = part[:, 0:B]
        if p < 2:
            tz_relay_in[1 - p] = send(tz_send.at[p], tz_relay.at[1 - p], at_z(2 * p - 1))
        else:
            tz_in[3 - p] = send(tz_send.at[p], tz_recv.at[3 - p], at_z(2 * p - 5))

    def table_pass():
        for side in (0, 1):
            tz_relay_in[side].wait_recv()
            tz_half_in[side].wait_recv()
            rows = slice(side * 48, side * 48 + 48)
            tz_own[side] += tz_relay[side].astype(F32)
            tz_own[side, rows, :] += tz_half[side].astype(F32)
            tz_back[side] = tz_own[side].astype(BF16)
            tz_in[2 + side] = send(tz_back.at[side], tz_recv.at[2 + side], at_z(2 - 4 * side))

    w_sum = wz_send[pl.ds(pl.multiple_of(z * 8, 8), 8), :]
    for d in ARRIVE[1:]:
        wz_in[d].wait_recv()
        w_sum += wz_recv[d]
    wy_recv[0, 0] = w_sum
    wy_in = {d: send(wy_recv.at[0, 0], wy_recv.at[0, d], at_y(d)) for d in ARRIVE[1:]}

    table_relay(0)
    table_relay(1)
    table_sum(0)
    low_pass()

    for d in ARRIVE[1:]:
        wy_in[d].wait_recv()
    wy_sib = send(wy_recv.at[0], wy_recv.at[1], sibling)
    table_relay(2)
    table_sum(1)

    wy_sib.wait_recv()
    w_sum = wy_recv[0, 0]
    for d in range(1, NY):
        w_sum += wy_recv[0, d]
    for d in range(NY):
        w_sum += wy_recv[1, d]
    w_rows = gw_ref.at[pl.ds(pl.multiple_of(dp * 8, 8), 8), :]
    gw_ref[pl.ds(pl.multiple_of(dp * 8, 8), 8), :] = w_sum
    w_back = {d: send(w_rows, w_rows, at_z(d)) for d in ARRIVE[1:]}

    table_relay(3)
    table_sum(2)
    low_sum()
    table_pass()
    table_sum(3)
    drain()

    low = lz_own[2, x]
    for d in (1, 3, 2):
        low_x[d].wait_recv()
        low += lx_recv[d].astype(F32)
    part = tz_own[2]
    for k in (1, 0, 2, 3):
        tz_in[k].wait_recv()
        part += tz_recv[k].astype(F32)
    rows = jnp.concatenate([part, low], axis=0).T.astype(BF16)
    t_back[x, 0] = rows[0:96]
    l_back[0, x] = rows[96:]

    def back_slot(d, half):
        if half is None:
            return t_back.at[x, POS[d]]
        return t_back.at[x, POS[d], pl.ds(half * 48, 48), :]

    def low_slot(d, half):
        if half is None:
            return l_back.at[POS[d]]
        return l_back.at[POS[d], pl.ds(2 * half, 2)]

    back = gather_start(back_slot, at_z)
    low_back = [send(l_back.at[0, x], l_back.at[0, x], at_x(d)) for d in (2, 1, 3)]
    near_in, far_in = {}, []

    def to_near(low, high):
        rows = t_back.at[x, pl.ds(low, high - low)]
        for side, step in ((0, 1), (1, -1)):
            near_in[low, side] = send(rows, rows, at_x(step))

    def to_far(low, high):
        middle = {1: None, 2: low + 1, 3: None}[high - low]
        for side, step in ((0, 1), (1, -1)):
            near_in[low, side].wait_recv()
            held = lax.rem(x - step + NX, NX)
            if middle is None:
                rows = t_back.at[held, pl.ds(low, high - low), pl.ds(side * 48, 48), :]
            else:
                rows = t_back.at[held, low + side]
            far_in.append(send(rows, rows, at_x(step)))

    to_near(0, 1)

    wait_for(w_back, *ARRIVE[1:])
    w_held = gw_ref.at[pl.ds(pl.multiple_of(x * 64, 64), 64), :]
    for step in (2, 1, 3):
        far_in.append(send(w_held, w_held, at_x(step)))

    gather_pass(back, back_slot, at_z)
    to_near(1, 3)
    for copy in low_back:
        copy.wait_recv()
    low_back = gather_start(low_slot, at_z)
    to_far(0, 1)
    wait_for(back, 1, -1)
    to_near(3, 5)
    to_far(1, 3)
    wait_for(back, 3, -3, 4, -4)
    to_near(5, 8)
    gather_pass(low_back, low_slot, at_z)
    to_far(3, 5)

    def rows_of(far, p, d):
        place = (far * NZ + lax.rem(z - d + NZ, NZ)) * B
        table_ref[pl.ds(pl.multiple_of(place, B), 96), :] = t_back[far, p]

    def low_rows_of(p, d):
        for far in range(NX):
            place = (far * NZ + lax.rem(z - d + NZ, NZ)) * B + 96
            table_ref[pl.ds(pl.multiple_of(place, 32), 32), :] = l_back[p, far]

    to_far(5, 8)
    for p, d in enumerate(ARRIVE):
        rows_of(x, p, d)
        rows_of(lax.rem(x + 1, NX), p, d)
        rows_of(lax.rem(x + 3, NX), p, d)
    wait_for(low_back, 1, -1, 3, -3, 4, -4)
    for p, d in enumerate(ARRIVE):
        low_rows_of(p, d)
    drain()
    for copy in far_in:
        copy.wait_recv()
    for p, d in enumerate(ARRIVE):
        rows_of(lax.rem(x + 2, NX), p, d)
    drain()


def finish(table_ref, gw_ref, out_ref, gwq_ref, gwi_ref, wide, sem):
    copies = [
        pltpu.make_async_copy(gw_ref.at[pl.ds(0, B), :], gwq_ref, sem.at[8]),
        pltpu.make_async_copy(gw_ref.at[pl.ds(B, B), :], gwi_ref, sem.at[9]),
    ]
    for copy in copies:
        copy.start()
    for i in range(8):
        wide[i] = table_ref[i * 512:(i + 1) * 512, :].astype(F32)
        copies.append(pltpu.make_async_copy(wide.at[i], out_ref.at[pl.ds(i * 512, 512), :], sem.at[i]))
        copies[-1].start()
    for copy in copies:
        copy.wait()


def on_device(q, it, pq, pi, wq, wi, pw, owner, row):
    def vmem(*shape, dtype=F32):
        return pltpu.VMEM(shape, dtype)

    table, gw = pl.pallas_call(
        kernel,
        out_shape=(
            jax.ShapeDtypeStruct((4096, E), BF16),
            jax.ShapeDtypeStruct((2 * B, W), F32),
        ),
        in_specs=[pl.BlockSpec(memory_space=pltpu.HBM)] * 9,
        out_specs=(pl.BlockSpec(memory_space=pltpu.VMEM),) * 2,
        scratch_shapes=[
            vmem(B, E, dtype=BF16),
            vmem(B, E, dtype=BF16),
            vmem(E, W, dtype=BF16),
            vmem(E, W, dtype=BF16),
            vmem(1, B),
            vmem(16, B, dtype=I32),
            vmem(16, B, dtype=I32),
            vmem(NZ * B, W, dtype=BF16),
            vmem(NX * B, W, dtype=BF16),
            vmem(NZ * B, NX * B),
            vmem(NZ * B, NX * B, dtype=BF16),
            vmem(NZ, NX * B),
            vmem(NZ, NX * B),
            vmem(16, B),
            vmem(NX, 16, B),
            vmem(2, 4, 2, 64, W, dtype=BF16),
            vmem(2, 4, 2, 64, W, dtype=BF16),
            vmem(NZ, B, W),
            vmem(NX, B, W, dtype=BF16),
            vmem(NX, B, W, dtype=BF16),
            vmem(B, W),
            vmem(256, B),
            vmem(64, 16 * B, dtype=BF16),
            vmem(CAP, 16 * B, dtype=BF16),
            vmem(NT, 64, CAP, dtype=BF16),
            vmem(1152, NT * CAP, dtype=BF16),
            vmem(NT, 2 * B, CAP, dtype=BF16),
            vmem(NT, NX, 16, CAP, dtype=BF16),
            vmem(2, NT, E, B, dtype=BF16),
            vmem(NX * E, NT * CAP, dtype=BF16),
            vmem(2 * B, W),
            vmem(NX, 64, W),
            vmem(64, W),
            vmem(NZ, 8, W),
            vmem(2, NY, 8, W),
            vmem(4, NX, E, 256),
            vmem(4, NX, E, 256, dtype=BF16),
            vmem(4, 2, 48, 256, dtype=BF16),
            vmem(4, 2, 96, 256, dtype=BF16),
            vmem(4, 2, 96, 256, dtype=BF16),
            vmem(96, B, dtype=BF16),
            vmem(3, 96, B),
            vmem(4, 96, B, dtype=BF16),
            vmem(2, 48, B, dtype=BF16),
            vmem(2, 96, B, dtype=BF16),
            vmem(2, 96, B, dtype=BF16),
            vmem(4, 96, B, dtype=BF16),
            vmem(2, 2, 32, B, dtype=BF16),
            vmem(2, NX, 32, B, dtype=BF16),
            vmem(3, NX, 32, B),
            vmem(2, NX, 32, B, dtype=BF16),
            vmem(4, NX, 32, B, dtype=BF16),
            vmem(NX, 32, B, dtype=BF16),
            vmem(NX, 32, B, dtype=BF16),
            vmem(NX, NZ, 96, E, dtype=BF16),
            vmem(NZ, NX, 32, E, dtype=BF16),
            pltpu.SemaphoreType.DMA((9,)),
            pltpu.SemaphoreType.DMA((N_COPIES,)),
            pltpu.SemaphoreType.DMA((N_COPIES,)),
        ],
        compiler_params=pltpu.CompilerParams(
            collective_id=0, has_side_effects=True, vmem_limit_bytes=40 * 1024 * 1024
        ),
    )(*[
        pltpu.with_memory_space_constraint(a, pltpu.HBM)
        for a in (
            q, it, pq, pi, wq, wi, pw.reshape(1, B), owner.reshape(B, 16).T, row.reshape(B, 16).T
        )
    ])
    return pl.pallas_call(
        finish,
        out_shape=(
            jax.ShapeDtypeStruct((4096, E), F32),
            jax.ShapeDtypeStruct((B, W), F32),
            jax.ShapeDtypeStruct((B, W), F32),
        ),
        in_specs=[pl.BlockSpec(memory_space=pltpu.VMEM)] * 2,
        out_specs=(pl.BlockSpec(memory_space=pltpu.HBM),) * 3,
        scratch_shapes=[vmem(8, 512, E), pltpu.SemaphoreType.DMA((10,))],
        compiler_params=pltpu.CompilerParams(vmem_limit_bytes=12 * 1024 * 1024),
    )(table, gw)


def solution(mesh):
    both = ("dp", "table")
    placed = (
        P(both, None),
        P(both, None),
        P(both, None),
        P(both, None),
        P(),
        P(),
        P(both),
        P(both, None, None),
        P(both, None, None),
    )
    return jax.shard_map(
        on_device,
        mesh=mesh,
        in_specs=placed,
        out_specs=(P("table", None), P(), P()),
        check_vma=False,
    )
```

```python
import math

import jax
import jax.numpy as jnp
from jax import lax
from jax.experimental import pallas as pl
from jax.experimental.pallas import tpu as pltpu
from jax.sharding import PartitionSpec as P

MESH = pl.DeviceIdType.MESH
F32, BF16, I32 = jnp.float32, jnp.bfloat16, jnp.int32
NX, NZ, NY = 4, 8, 8
B, W, E = 128, 256, 128
NT = 2 * NY
CAP = 256
SCALE = 1.0 / math.sqrt(W)
N_COPIES = 176

NN = (((1,), (0,)), ((), ()))
NT_DIMS = (((1,), (1,)), ((), ()))
TN = (((0,), (0,)), ((), ()))


def dot(a, b, dims=NN):
    return lax.dot_general(a, b, dims, preferred_element_type=F32)


def iota(shape, dim):
    return lax.broadcasted_iota(I32, shape, dim)


ARRIVE = (0, 2, 6, 1, 7, 3, 5, 4)
POS = {d: p for p, d in enumerate(ARRIVE)}
OWN = (0, 1, 2, 3, 4, 10, 11, 12)
SIB = (5, 6, 7, 8, 9, 13, 14, 15)
FIRST = 10 * CAP


def kernel(
    q_ref, it_ref, pq_ref, pi_ref, wq_ref, wi_ref, pw_ref, ow_ref, rw_ref,
    table_ref, gw_ref,
    pq, pi, wq, wi, pw, ow, rw,
    ibuf, qbuf, ebuf, gbuf, tops, totals, st_send, st_recv,
    gi_send, gi_relay, gi_half, gi_recv, gi_own, gq_send, gq_recv, gq_own,
    taken, slots_a, slots_b, lists, onehot, select, factor, pooled, values,
    w_part, wx_recv, wz_send, wz_relay, wz_pass, wz_recv, wy_recv, w_own,
    t_own, t_send, tx_half, tx_relay, tx_recv, tz_first, tz_own, tz_send, tz_half, tz_relay, tz_back, tz_recv,
    lz_half, lz_relay, lz_own, lz_send, lz_recv, lx_send, lx_recv, t_back, l_back,
    load_sem, send_sem, recv_sem,
):
    dp, tb = lax.axis_index("dp"), lax.axis_index("table")
    x, z = lax.div(dp, NZ), lax.rem(dp, NZ)
    y, core = lax.div(tb, 2), lax.rem(tb, 2)

    def at_x(d):
        return (lax.rem(x + d + NX, NX) * NZ + z, tb)

    def at_z(d):
        return (x * NZ + lax.rem(z + d + NZ, NZ), tb)

    def at_y(d):
        return (dp, lax.rem(y + d + NY, NY) * 2 + core)

    sibling = (dp, tb + 1 - 2 * core)
    partners = (
        [at_x(d) for d in range(1, NX)]
        + [at_z(d) for d in (1, 2, -1, -2)]
        + [at_y(d) for d in (1, 2, -1, -2)]
        + [sibling]
    )
    barrier = pltpu.get_barrier_semaphore()
    for partner in partners:
        pl.semaphore_signal(barrier, inc=1, device_id=partner, device_id_type=MESH)
    loads = [
        pltpu.make_async_copy(src, dst, load_sem.at[i])
        for i, (src, dst) in enumerate((
            (it_ref, ibuf.at[pl.ds(0, B), :]),
            (q_ref, qbuf.at[pl.ds(0, B), :]),
            (ow_ref, ow),
            (rw_ref, rw),
            (pw_ref, pw),
            (pq_ref, pq),
            (pi_ref, pi),
            (wq_ref, wq),
            (wi_ref, wi),
        ))
    ]
    for load in loads:
        load.start()
    pl.semaphore_wait(barrier, len(partners))

    copies, drained = [], [0]

    def remote(index, src, dst, device):
        return pltpu.make_async_remote_copy(
            src_ref=src,
            dst_ref=dst,
            send_sem=send_sem.at[index],
            recv_sem=recv_sem.at[index],
            device_id=device,
            device_id_type=MESH,
        )

    def send(src, dst, device):
        copy = remote(len(copies), src, dst, device)
        copy.start()
        copies.append(copy)
        return copy

    def drain():
        for copy in copies[drained[0]:]:
            copy.wait_send()
        drained[0] = len(copies)

    def gather_start(slot, at, source=None):
        source = slot(0, None) if source is None else source
        return {d: send(source, slot(d % 8, None), at(d)) for d in (2, -2, 1, -1)}

    def gather_pass(got, slot, at):
        got[2].wait_recv()
        got[3] = send(slot(2, None), slot(3, None), at(1))
        got[4] = send(slot(2, 0), slot(4, 0), at(2))
        got[-2].wait_recv()
        got[-3] = send(slot(6, None), slot(5, None), at(-1))
        got[-4] = send(slot(6, 1), slot(4, 1), at(-2))

    def wait_for(got, *names):
        for name in names:
            got[name].wait_recv()

    def item_slot(d, half):
        if half is None:
            return ibuf.at[pl.ds(POS[d] * B, B), :]
        return ibuf.at[pl.ds(POS[d] * B + half * 64, 64), :]

    item_in = gather_start(item_slot, at_z, it_ref)
    query_in = {}
    for d in (1, 3, 2):
        query_in[d] = send(q_ref, qbuf.at[pl.ds(d * B, B), :], at_x(d))

    for load in loads:
        load.wait()
    owner_row = iota((NT, B), 0)
    hits = jnp.concatenate([(ow[k:k + 1, :] == owner_row).astype(F32) for k in range(16)], axis=0)
    before = (iota((B, 2 * B), 0) < iota((B, 2 * B), 1)).astype(BF16)
    counts = dot(hits.astype(BF16), before)
    at_row, at_col = iota((256, 256), 0), iota((256, 256), 1)
    earlier = jnp.logical_and(
        lax.bitwise_and(at_row, 15) == lax.bitwise_and(at_col, 15),
        lax.shift_right_logical(at_col, 4) < lax.shift_right_logical(at_row, 4),
    ).astype(BF16)
    taken[...] = (counts[:, 0:B] + dot(earlier, counts[:, B:].astype(BF16))) * hits
    list_row = iota((64, B), 0)
    list_owner, piece = lax.bitwise_and(list_row, 15), lax.shift_right_logical(list_row, 4)
    pair = iota((1, B), 1)
    place = iota((CAP, B), 0)

    def list_slot(k, _):
        lanes = pl.ds(pl.multiple_of(k * B, B), B)
        ranks = taken[pl.ds(pl.multiple_of(k * NT, NT), NT), :]
        rank = jnp.sum(ranks, axis=0, keepdims=True).astype(I32)
        slots_b[:, lanes] = (place == rank).astype(BF16)
        owner, row = ow[pl.ds(k, 1), :], rw[pl.ds(k, 1), :]
        part = jnp.where(
            piece == 0,
            pair + lax.div(k, 8) * B,
            jnp.where(
                piece == 1,
                lax.shift_right_logical(row, 8) + 1,
                jnp.where(piece == 2, lax.bitwise_and(row, 255), 0),
            ),
        )
        slots_a[:, lanes] = jnp.where(list_owner == owner, part, 0).astype(F32).astype(BF16)
        return 0

    lax.fori_loop(0, 16, list_slot, 0)
    lists[0] = dot(slots_a[...], slots_b[...], NT_DIMS).astype(BF16)

    def list_slot_of(d, half):
        if half is None:
            return lists.at[OWN[POS[d]]]
        return lists.at[OWN[POS[d]], pl.ds(half * 32, 32), :]

    list_in = gather_start(list_slot_of, at_y)
    gather_pass(item_in, item_slot, at_z)

    wait_for(query_in, 1, 3, 2)

    def logits(p, _):
        rows = pl.ds(pl.multiple_of(p * B, B), B)
        block = SCALE * dot(ibuf[rows, :], qbuf[...], NT_DIMS)
        top = jnp.max(block, axis=0, keepdims=True)
        block = jnp.exp(block - top)
        ebuf[rows, :] = block
        tops[pl.ds(p, 1), :] = top
        totals[pl.ds(p, 1), :] = jnp.sum(block, axis=0, keepdims=True)
        return 0

    wait_for(item_in, 1, -1)
    lax.fori_loop(0, 5, logits, 0, unroll=True)
    wait_for(item_in, 3, -3)
    lax.fori_loop(5, 7, logits, 0, unroll=True)
    wait_for(item_in, 4, -4)
    logits(7, 0)

    top = jnp.max(tops[...], axis=0, keepdims=True)
    total = jnp.sum(totals[...] * jnp.exp(tops[...] - top), axis=0, keepdims=True)
    weight = pw[...]
    for k in range(NX):
        st_send[k:k + 1, :] = top[:, k * B:(k + 1) * B]
        st_send[NX + k:NX + k + 1, :] = total[:, k * B:(k + 1) * B]
    st_send[8:16, :] = jnp.broadcast_to(weight, (8, B))
    stat_in = {d: send(st_send, st_recv.at[d], at_x(d)) for d in (2, 1, 3)}
    gather_pass(list_in, list_slot_of, at_y)
    wait_for(stat_in, 1, 3, 2)
    maxima, factors = [], []
    for k in range(NX):
        part_tops, part_totals = [st_send[k:k + 1, :]], [st_send[NX + k:NX + k + 1, :]]
        for d in range(1, NX):
            j = (k - d) % NX
            part_tops.append(st_recv[d, j:j + 1, :])
            part_totals.append(st_recv[d, NX + j:NX + j + 1, :])
        row_max = part_tops[0]
        for t in part_tops[1:]:
            row_max = jnp.maximum(row_max, t)
        row_total = sum(s * jnp.exp(t - row_max) for t, s in zip(part_tops, part_totals))
        maxima.append(row_max)
        factors.append((weight if k == 0 else st_recv[k, 8:9, :]) / row_total)
    row_max, factors = jnp.concatenate(maxima, axis=1), jnp.concatenate(factors, axis=1)
    totals[...] = factors * jnp.exp(tops[...] - row_max)

    def item_terms(p):
        rows = pl.ds(pl.multiple_of(p * B, B), B)
        block = (ebuf[rows, :] * totals[pl.ds(p, 1), :]).astype(BF16)
        gbuf[rows, :] = block
        return SCALE * dot(block, qbuf[...])

    def far_terms(p, _):
        gi_send[p] = item_terms(p).astype(BF16)
        return 0

    def near_terms(p, _):
        gi_own[p] = item_terms(p)
        return 0

    far_terms(7, 0)
    half_in = [
        send(gi_send.at[7, pl.ds(0, 64), :], gi_half.at[0], at_z(2)),
        send(gi_send.at[7, pl.ds(64, 64), :], gi_half.at[1], at_z(-2)),
    ]
    lax.fori_loop(5, 7, far_terms, 0, unroll=True)
    relay_in = [
        send(gi_send.at[POS[5]], gi_relay.at[0], at_z(1)),
        send(gi_send.at[POS[3]], gi_relay.at[1], at_z(-1)),
    ]
    lax.fori_loop(3, 5, far_terms, 0, unroll=True)
    grad_in = {d: send(gi_send.at[POS[d]], gi_recv.at[POS[d]], at_z(-d)) for d in (7, 1)}
    lax.fori_loop(0, 3, near_terms, 0, unroll=True)
    same = iota((B, B), 0) == iota((B, B), 1)
    diagonal = ebuf[0:B, 0:B] * totals[0:1, 0:B] - jnp.where(same, weight, 0.0)
    gbuf[0:B, 0:B] = diagonal.astype(BF16)
    gi_own[0] = SCALE * dot(gbuf[0:B, :], qbuf[...])

    terms = SCALE * dot(gbuf[...], ibuf[...], TN)
    gq_own[...] = terms[0:B, :]
    for k in range(1, NX):
        gq_send[k] = terms[k * B:(k + 1) * B, :].astype(BF16)
    query_grad_in = {k: send(gq_send.at[k], gq_recv.at[k], at_x(-k)) for k in (2, 1, 3)}
    for side, (d, rows) in enumerate(((6, slice(0, 64)), (2, slice(64, 128)))):
        p = POS[d]
        relay_in[side].wait_recv()
        half_in[side].wait_recv()
        gi_own[p] += gi_relay[side].astype(F32)
        gi_own[p, rows, :] += gi_half[side].astype(F32)
        gi_send[p] = gi_own[p].astype(BF16)
        grad_in[d] = send(gi_send.at[p], gi_recv.at[p], at_z(-d))

    list_sib = []

    def lists_to_sibling(low, high):
        list_sib.append(send(
            lists.at[pl.ds(OWN[low], high - low)], lists.at[pl.ds(SIB[low], high - low)], sibling
        ))

    wait_for(list_in, 1, -1, 3, -3, 4, -4)
    lists_to_sibling(0, 5)
    lists_to_sibling(5, 8)
    source_row = iota((2 * B, CAP), 0)
    owner_row = iota((NT, CAP), 0)
    low_row = lax.bitwise_and(iota((1152, CAP), 0), 1023)

    def one_hots(s, _):
        entry = lists[s].astype(F32)
        source, high, low = [
            jnp.sum(jnp.where(owner_row == tb, entry[16 * k:16 * k + 16, :], 0.0), axis=0, keepdims=True).astype(I32)
            for k in range(3)
        ]
        row = (high - 1) * 256 + low
        select[s] = (source == source_row).astype(BF16)
        lanes = pl.ds(pl.multiple_of(s * CAP, CAP), CAP)
        onehot[:, lanes] = (lax.bitwise_and(row, 1023) == low_row).astype(BF16)
        block = jnp.broadcast_to(lax.shift_right_arithmetic(row, 10), (16, CAP))
        for j in range(NX):
            factor[s, j] = (block == j).astype(BF16)
        return 0

    lax.fori_loop(0, 5, one_hots, 0)
    lax.fori_loop(10, 13, one_hots, 0)

    query_grad = gq_own[...]
    for k in (1, 3, 2):
        query_grad_in[k].wait_recv()
        query_grad += gq_recv[k].astype(F32)
    query_grad = query_grad.astype(BF16)

    pooled_in, pooled_sib = {}, {}

    def pooled_slot(half):
        def slot(d, rows):
            if rows is None:
                return pooled.at[half, OWN[POS[d]]]
            return pooled.at[half, OWN[POS[d]], pl.ds(rows * 64, 64), :]

        return slot

    def to_sibling(half, low, high):
        pooled_sib[half, low] = send(
            pooled.at[half, pl.ds(OWN[low], high - low)], pooled.at[half, pl.ds(SIB[low], high - low)], sibling
        )

    pooled[0, 0] = dot(wq[...], query_grad, NT_DIMS).astype(BF16)
    pooled_in[0] = gather_start(pooled_slot(0), at_y)
    to_sibling(0, 0, 1)
    w_part[0:B, :] = dot(pq[...], query_grad, TN)

    for copy in list_sib:
        copy.wait_recv()
    lax.fori_loop(5, 10, one_hots, 0)
    lax.fori_loop(13, 16, one_hots, 0)
    drain()

    item_grad = gi_own[0]
    for d in (1, 7, 2, 6):
        grad_in[d].wait_recv()
        item_grad += gi_recv[POS[d]].astype(F32)
    item_grad = item_grad.astype(BF16)
    pooled[1, 0] = dot(wi[...], item_grad, NT_DIMS).astype(BF16)
    pooled_in[1] = gather_start(pooled_slot(1), at_y)
    to_sibling(1, 0, 1)
    gather_pass(pooled_in[0], pooled_slot(0), at_y)
    wait_for(pooled_in[0], 1, -1)
    to_sibling(0, 1, 3)
    to_sibling(0, 3, 5)
    w_part[B:, :] = dot(pi[...], item_grad, TN)
    w_in = {}
    for d in (2, 1, 3):
        to_x = lax.rem(x + d, NX)
        w_in[d] = send(w_part.at[pl.ds(pl.multiple_of(to_x * 64, 64), 64), :], wx_recv.at[d], at_x(d))

    def place_values(s, _):
        got = (dot(pooled[0, s], select[s, 0:B, :]) + dot(pooled[1, s], select[s, B:, :])).astype(BF16)
        lanes = pl.ds(pl.multiple_of(s * CAP, CAP), CAP)
        for j in range(NX):
            values[j * E:(j + 1) * E, lanes] = got * jnp.tile(factor[s, j], (8, 1))
        return 0

    def quarter_rows(p):
        return pl.ds(pl.multiple_of(lax.rem(z + 4 + 3 * p * (p + 1), NZ) * B, B), 256)

    def first_part(p, _):
        part = dot(values[:, 0:FIRST], onehot[quarter_rows(p), 0:FIRST], NT_DIMS)
        t_own[p] = part.reshape(NX, E, 256)
        return 0

    gather_pass(pooled_in[1], pooled_slot(1), at_y)
    wait_for(pooled_in[1], 1, -1)
    to_sibling(1, 1, 3)
    to_sibling(1, 3, 5)
    lax.fori_loop(0, 5, place_values, 0, unroll=True)
    for low in (0, 1, 3):
        pooled_sib[0, low].wait_recv()
        pooled_sib[1, low].wait_recv()
    lax.fori_loop(5, 10, place_values, 0, unroll=True)

    w_sum = w_part[pl.ds(pl.multiple_of(x * 64, 64), 64), :]
    for d in (1, 3, 2):
        w_in[d].wait_recv()
        w_sum += wx_recv[d]
    wz_send[...] = w_sum

    def w_chunk(d):
        return pl.ds(pl.multiple_of(lax.rem(z + d + NZ, NZ) * 8, 8), 8)

    wz_in = {}
    for d, via, dst in (
        (4, 2, wz_relay.at[0]), (3, 1, wz_relay.at[1]), (-3, -1, wz_relay.at[2]),
        (1, 1, wz_recv.at[0]), (-1, -1, wz_recv.at[1]),
    ):
        wz_in[d] = send(wz_send.at[w_chunk(d), :], dst, at_z(via))

    lax.fori_loop(0, 2, first_part, 0)
    wait_for(pooled_in[0], 3, -3, 4, -4)
    to_sibling(0, 5, 8)
    wait_for(pooled_in[1], 3, -3, 4, -4)
    to_sibling(1, 5, 8)
    lax.fori_loop(10, 13, place_values, 0, unroll=True)
    lax.fori_loop(2, 4, first_part, 0)
    wait_for(wz_in, 4, 3, -3)
    wz_pass[0] = wz_send[w_chunk(2), :] + wz_relay[0] + wz_relay[1]
    wz_pass[1] = wz_send[w_chunk(-2), :] + wz_relay[2]
    for side, d in ((0, 2), (1, -2)):
        wz_in[d] = send(wz_pass.at[side], wz_recv.at[2 + side], at_z(d))
    pooled_sib[0, 5].wait_recv()
    pooled_sib[1, 5].wait_recv()
    lax.fori_loop(13, 16, place_values, 0, unroll=True)

    half_base = len(copies)
    copies.extend([None] * 8)

    def half_copy(p, side):
        return remote(
            half_base + 2 * p + side,
            t_send.at[p, lax.rem(x + 2, NX), pl.ds(side * 48, 48), :],
            tx_half.at[p, side],
            at_x(1 - 2 * side),
        )

    def send_part(p, part):
        part = t_own[p] + part.reshape(NX, E, 256)
        t_own[p] = part
        t_send[p] = part.astype(BF16)
        half_copy(p, 0).start()
        half_copy(p, 1).start()

    def last_part(p, _):
        send_part(p, dot(values[:, FIRST:], onehot[quarter_rows(p), FIRST:], NT_DIMS))
        return 0

    lax.fori_loop(0, 4, last_part, 0)
    for p in range(4):
        for side in (0, 1):
            copies[half_base + 2 * p + side] = half_copy(p, side)

    def low_columns(p, side):
        return t_send.at[p, :, pl.ds(96, 32), pl.ds(side * B, B)]

    low_half = [
        send(t_send.at[0, pl.ds(2 * side, 2), pl.ds(96, 32), pl.ds(0, B)], lz_half.at[side], at_z(2 - 4 * side))
        for side in (0, 1)
    ]
    low_relay = [
        send(low_columns(1, 1), lz_relay.at[0], at_z(1)),
        send(low_columns(0, 1), lz_relay.at[1], at_z(-1)),
    ]
    low_in = [
        send(low_columns(3, 1), lz_recv.at[0], at_z(1)),
        send(low_columns(2, 1), lz_recv.at[1], at_z(-1)),
    ]

    def low_pass():
        for side in (0, 1):
            low_relay[side].wait_recv()
            low_half[side].wait_recv()
            lz_own[side] = t_own[1 + side, :, 96:, 0:B] + lz_relay[side].astype(F32)
            pair_of = slice(2 * side, 2 * side + 2)
            lz_own[side, pair_of] += lz_half[side].astype(F32)
            lz_send[side] = lz_own[side].astype(BF16)
            low_in.append(send(lz_send.at[side], lz_recv.at[2 + side], at_z(2 - 4 * side)))

    low_x = {}

    def low_sum():
        part = t_own[3, :, 96:, 0:B]
        for k in range(4):
            low_in[k].wait_recv()
            part += lz_recv[k].astype(F32)
        lz_own[2] = part
        lx_send[...] = part.astype(BF16)
        for d in (2, 1, 3):
            low_x[d] = send(lx_send.at[lax.rem(x + d, NX)], lx_recv.at[d], at_x(d))

    relay_in, tz_half_in, tz_relay_in, tz_in = {}, {}, {}, {}

    def table_relay(p):
        for side, step in ((0, 1), (1, -1)):
            copies[half_base + 2 * p + side].wait_recv()
            near = lax.rem(x + step + NX, NX)
            for half in (0, 1):
                rows = slice(half * 48, half * 48 + 48)
                part = t_own[p, near, rows, :]
                if half == side:
                    part += tx_half[p, side].astype(F32)
                tx_relay[p, side, rows, :] = part.astype(BF16)
            relay_in[p, side] = send(tx_relay.at[p, side], tx_recv.at[p, side], at_x(step))

    def table_sum(p):
        part = t_own[p, x, 0:96, :]
        for side in (0, 1):
            relay_in[p, side].wait_recv()
            part += tx_recv[p, side].astype(F32)
        tz_send[p] = part[:, B:].astype(BF16)
        if p == 0:
            tz_first[...] = part[:, 0:B].astype(BF16)
            for side in (0, 1):
                tz_half_in[side] = send(
                    tz_first.at[pl.ds(side * 48, 48), :], tz_half.at[side], at_z(2 - 4 * side)
                )
        else:
            tz_own[p - 1] = part[:, 0:B]
        if p < 2:
            tz_relay_in[1 - p] = send(tz_send.at[p], tz_relay.at[1 - p], at_z(2 * p - 1))
        else:
            tz_in[3 - p] = send(tz_send.at[p], tz_recv.at[3 - p], at_z(2 * p - 5))

    def table_pass():
        for side in (0, 1):
            tz_relay_in[side].wait_recv()
            tz_half_in[side].wait_recv()
            rows = slice(side * 48, side * 48 + 48)
            tz_own[side] += tz_relay[side].astype(F32)
            tz_own[side, rows, :] += tz_half[side].astype(F32)
            tz_back[side] = tz_own[side].astype(BF16)
            tz_in[2 + side] = send(tz_back.at[side], tz_recv.at[2 + side], at_z(2 - 4 * side))

    def small_pass(got, slot, at, there):
        got[2].wait_recv()
        got[3] = send(slot(2), there(2, 3), at(1))
        got[4] = send(slot(2), there(2, 4), at(2))
        got[-2].wait_recv()
        got[5] = send(slot(-2), there(-2, 5), at(-1))

    def wy_slot(d):
        return wy_recv.at[0, d % 8]

    def w_rows(d):
        place = x * NZ + lax.rem(z - d + NZ, NZ)
        return gw_ref.at[pl.ds(pl.multiple_of(place * 8, 8), 8), pl.ds(pl.multiple_of(core * B, B), B)]

    table_relay(0)
    table_relay(1)
    w_sum = wz_send[w_chunk(0), :]
    wait_for(wz_in, 1, -1, 2, -2)
    for k in range(4):
        w_sum += wz_recv[k]
    wy_recv[0, 0] = w_sum
    wy_in = {d: send(wy_slot(0), wy_slot(d), at_y(d)) for d in (2, -2, 1, -1)}

    table_sum(0)
    low_pass()
    table_relay(2)
    small_pass(wy_in, wy_slot, at_y, lambda here, d: wy_slot(d))
    table_sum(1)
    table_relay(3)
    wait_for(wy_in, 1, -1, 3, 4, 5)
    wy_sib = send(wy_recv.at[0], wy_recv.at[1], sibling)
    table_sum(2)
    low_sum()
    table_pass()

    wy_sib.wait_recv()
    w_sum = wy_recv[0, 0]
    for d in range(1, NY):
        w_sum += wy_recv[0, d]
    for d in range(NY):
        w_sum += wy_recv[1, d]
    w_own[...] = w_sum
    own_lanes = pl.ds(pl.multiple_of(core * B, B), B)
    gw_ref[pl.ds(pl.multiple_of(dp * 8, 8), 8), own_lanes] = w_own[:, own_lanes]
    w_back = {d: send(w_rows(0), w_rows(0), at_z(d)) for d in (2, -2, 1, -1)}

    table_sum(3)
    drain()

    low = lz_own[2, x]
    for d in (1, 3, 2):
        low_x[d].wait_recv()
        low += lx_recv[d].astype(F32)
    part = tz_own[2]
    for k in (1, 0, 2, 3):
        tz_in[k].wait_recv()
        part += tz_recv[k].astype(F32)
    rows = jnp.concatenate([part, low], axis=0).T.astype(BF16)
    t_back[x, 0] = rows[0:96]
    l_back[0, x] = rows[96:]

    def back_slot(d, half):
        if half is None:
            return t_back.at[x, POS[d]]
        return t_back.at[x, POS[d], pl.ds(half * 48, 48), :]

    def low_slot(d, half):
        if half is None:
            return l_back.at[POS[d]]
        return l_back.at[POS[d], pl.ds(2 * half, 2)]

    back = gather_start(back_slot, at_z)
    low_back = [send(l_back.at[0, x], l_back.at[0, x], at_x(d)) for d in (2, 1, 3)]
    near_in, far_in = {}, []

    def to_near(low, high):
        rows = t_back.at[x, pl.ds(low, high - low)]
        for side, step in ((0, 1), (1, -1)):
            near_in[low, side] = send(rows, rows, at_x(step))

    def to_far(low, high):
        middle = {1: None, 2: low + 1, 3: None}[high - low]
        for side, step in ((0, 1), (1, -1)):
            near_in[low, side].wait_recv()
            held = lax.rem(x - step + NX, NX)
            if middle is None:
                rows = t_back.at[held, pl.ds(low, high - low), pl.ds(side * 48, 48), :]
            else:
                rows = t_back.at[held, low + side]
            far_in.append(send(rows, rows, at_x(step)))

    to_near(0, 1)

    small_pass(w_back, w_rows, at_z, lambda here, d: w_rows(here))
    gather_pass(back, back_slot, at_z)
    to_near(1, 3)
    for copy in low_back:
        copy.wait_recv()
    low_back = gather_start(low_slot, at_z)
    wait_for(w_back, 1, -1, 3, 4, 5)
    w_held = gw_ref.at[pl.ds(pl.multiple_of(x * 64, 64), 64), pl.ds(pl.multiple_of(core * B, B), B)]
    w_x = [send(w_held, w_held, at_x(step)) for step in (2, 1, 3)]
    to_far(0, 1)
    wait_for(back, 1, -1)
    to_near(3, 5)
    to_far(1, 3)
    wait_for(back, 3, -3, 4, -4)
    to_near(5, 8)
    gather_pass(low_back, low_slot, at_z)
    to_far(3, 5)

    def rows_of(far, p, d):
        place = (far * NZ + lax.rem(z - d + NZ, NZ)) * B
        table_ref[pl.ds(pl.multiple_of(place, B), 96), :] = t_back[far, p]

    def low_rows_of(p, d):
        for far in range(NX):
            place = (far * NZ + lax.rem(z - d + NZ, NZ)) * B + 96
            table_ref[pl.ds(pl.multiple_of(place, 32), 32), :] = l_back[p, far]

    to_far(5, 8)
    for copy in w_x:
        copy.wait_recv()
    w_half = gw_ref.at[:, pl.ds(pl.multiple_of(core * B, B), B)]
    far_in.append(send(w_half, w_half, sibling))
    for p, d in enumerate(ARRIVE):
        rows_of(x, p, d)
        rows_of(lax.rem(x + 1, NX), p, d)
        rows_of(lax.rem(x + 3, NX), p, d)
    wait_for(low_back, 1, -1, 3, -3, 4, -4)
    for p, d in enumerate(ARRIVE):
        low_rows_of(p, d)
    drain()
    for copy in far_in:
        copy.wait_recv()
    for p, d in enumerate(ARRIVE):
        rows_of(lax.rem(x + 2, NX), p, d)
    drain()


def finish(table_ref, gw_ref, out_ref, gwq_ref, gwi_ref, wide, sem):
    copies = [
        pltpu.make_async_copy(gw_ref.at[pl.ds(0, B), :], gwq_ref, sem.at[8]),
        pltpu.make_async_copy(gw_ref.at[pl.ds(B, B), :], gwi_ref, sem.at[9]),
    ]
    for copy in copies:
        copy.start()
    for i in range(8):
        wide[i] = table_ref[i * 512:(i + 1) * 512, :].astype(F32)
        copies.append(pltpu.make_async_copy(wide.at[i], out_ref.at[pl.ds(i * 512, 512), :], sem.at[i]))
        copies[-1].start()
    for copy in copies:
        copy.wait()


def on_device(q, it, pq, pi, wq, wi, pw, owner, row):
    def vmem(*shape, dtype=F32):
        return pltpu.VMEM(shape, dtype)

    table, gw = pl.pallas_call(
        kernel,
        out_shape=(
            jax.ShapeDtypeStruct((4096, E), BF16),
            jax.ShapeDtypeStruct((2 * B, W), F32),
        ),
        in_specs=[pl.BlockSpec(memory_space=pltpu.HBM)] * 9,
        out_specs=(pl.BlockSpec(memory_space=pltpu.VMEM),) * 2,
        scratch_shapes=[
            vmem(B, E, dtype=BF16),
            vmem(B, E, dtype=BF16),
            vmem(E, W, dtype=BF16),
            vmem(E, W, dtype=BF16),
            vmem(1, B),
            vmem(16, B, dtype=I32),
            vmem(16, B, dtype=I32),
            vmem(NZ * B, W, dtype=BF16),
            vmem(NX * B, W, dtype=BF16),
            vmem(NZ * B, NX * B),
            vmem(NZ * B, NX * B, dtype=BF16),
            vmem(NZ, NX * B),
            vmem(NZ, NX * B),
            vmem(16, B),
            vmem(NX, 16, B),
            vmem(NZ, B, W, dtype=BF16),
            vmem(2, B, W, dtype=BF16),
            vmem(2, 64, W, dtype=BF16),
            vmem(NZ, B, W, dtype=BF16),
            vmem(3, B, W),
            vmem(NX, B, W, dtype=BF16),
            vmem(NX, B, W, dtype=BF16),
            vmem(B, W),
            vmem(256, B),
            vmem(64, 16 * B, dtype=BF16),
            vmem(CAP, 16 * B, dtype=BF16),
            vmem(NT, 64, CAP, dtype=BF16),
            vmem(1152, NT * CAP, dtype=BF16),
            vmem(NT, 2 * B, CAP, dtype=BF16),
            vmem(NT, NX, 16, CAP, dtype=BF16),
            vmem(2, NT, E, B, dtype=BF16),
            vmem(NX * E, NT * CAP, dtype=BF16),
            vmem(2 * B, W),
            vmem(NX, 64, W),
            vmem(64, W),
            vmem(3, 8, W),
            vmem(2, 8, W),
            vmem(4, 8, W),
            vmem(2, NY, 8, W),
            vmem(8, W),
            vmem(4, NX, E, 256),
            vmem(4, NX, E, 256, dtype=BF16),
            vmem(4, 2, 48, 256, dtype=BF16),
            vmem(4, 2, 96, 256, dtype=BF16),
            vmem(4, 2, 96, 256, dtype=BF16),
            vmem(96, B, dtype=BF16),
            vmem(3, 96, B),
            vmem(4, 96, B, dtype=BF16),
            vmem(2, 48, B, dtype=BF16),
            vmem(2, 96, B, dtype=BF16),
            vmem(2, 96, B, dtype=BF16),
            vmem(4, 96, B, dtype=BF16),
            vmem(2, 2, 32, B, dtype=BF16),
            vmem(2, NX, 32, B, dtype=BF16),
            vmem(3, NX, 32, B),
            vmem(2, NX, 32, B, dtype=BF16),
            vmem(4, NX, 32, B, dtype=BF16),
            vmem(NX, 32, B, dtype=BF16),
            vmem(NX, 32, B, dtype=BF16),
            vmem(NX, NZ, 96, E, dtype=BF16),
            vmem(NZ, NX, 32, E, dtype=BF16),
            pltpu.SemaphoreType.DMA((9,)),
            pltpu.SemaphoreType.DMA((N_COPIES,)),
            pltpu.SemaphoreType.DMA((N_COPIES,)),
        ],
        compiler_params=pltpu.CompilerParams(
            collective_id=0, has_side_effects=True, vmem_limit_bytes=40 * 1024 * 1024
        ),
    )(*[
        pltpu.with_memory_space_constraint(a, pltpu.HBM)
        for a in (
            q, it, pq, pi, wq, wi, pw.reshape(1, B), owner.reshape(B, 16).T, row.reshape(B, 16).T
        )
    ])
    return pl.pallas_call(
        finish,
        out_shape=(
            jax.ShapeDtypeStruct((4096, E), F32),
            jax.ShapeDtypeStruct((B, W), F32),
            jax.ShapeDtypeStruct((B, W), F32),
        ),
        in_specs=[pl.BlockSpec(memory_space=pltpu.VMEM)] * 2,
        out_specs=(pl.BlockSpec(memory_space=pltpu.HBM),) * 3,
        scratch_shapes=[vmem(8, 512, E), pltpu.SemaphoreType.DMA((10,))],
        compiler_params=pltpu.CompilerParams(vmem_limit_bytes=12 * 1024 * 1024),
    )(table, gw)


def solution(mesh):
    both = ("dp", "table")
    placed = (
        P(both, None),
        P(both, None),
        P(both, None),
        P(both, None),
        P(),
        P(),
        P(both),
        P(both, None, None),
        P(both, None, None),
    )
    return jax.shard_map(
        on_device,
        mesh=mesh,
        in_specs=placed,
        out_specs=(P("table", None), P(), P()),
        check_vma=False,
    )
```

```python
import math

import jax
import jax.numpy as jnp
from jax import lax
from jax.experimental import pallas as pl
from jax.experimental.pallas import tpu as pltpu
from jax.sharding import PartitionSpec as P

MESH = pl.DeviceIdType.MESH
F32, BF16, I32 = jnp.float32, jnp.bfloat16, jnp.int32
NX, NZ, NY = 4, 8, 8
B, W, E = 128, 256, 128
NT = 2 * NY
CAP = 256
SCALE = 1.0 / math.sqrt(W)
N_COPIES = 176

NN = (((1,), (0,)), ((), ()))
NT_DIMS = (((1,), (1,)), ((), ()))
TN = (((0,), (0,)), ((), ()))


def dot(a, b, dims=NN):
    return lax.dot_general(a, b, dims, preferred_element_type=F32)


def iota(shape, dim):
    return lax.broadcasted_iota(I32, shape, dim)


ARRIVE = (0, 2, 6, 1, 7, 3, 5, 4)
POS = {d: p for p, d in enumerate(ARRIVE)}
OWN = (0, 1, 2, 3, 4, 10, 11, 12)
SIB = (5, 6, 7, 8, 9, 13, 14, 15)
FIRST = 10 * CAP


def kernel(
    q_ref, it_ref, pq_ref, pi_ref, wq_ref, wi_ref, pw_ref, ow_ref, rw_ref,
    table_ref, gw_ref,
    pq, pi, wq, wi, pw, ow, rw,
    ibuf, qbuf, ebuf, gbuf, tops, totals, st_send, st_recv,
    gi_send, gi_relay, gi_half, gi_recv, gi_own, gq_send, gq_recv, gq_own,
    taken, slots_a, slots_b, lists, onehot, select, factor, pooled, values,
    w_part, wx_recv, wz_send, wz_relay, wz_pass, wz_recv, wy_recv, w_own,
    t_own, t_send, tx_half, tx_relay, tx_recv, tz_first, tz_own, tz_send, tz_half, tz_relay, tz_back, tz_recv,
    lz_half, lz_relay, lz_own, lz_send, lz_recv, lx_send, lx_recv, t_back, l_back,
    load_sem, send_sem, recv_sem,
):
    dp, tb = lax.axis_index("dp"), lax.axis_index("table")
    x, z = lax.div(dp, NZ), lax.rem(dp, NZ)
    y, core = lax.div(tb, 2), lax.rem(tb, 2)

    def at_x(d):
        return (lax.rem(x + d + NX, NX) * NZ + z, tb)

    def at_z(d):
        return (x * NZ + lax.rem(z + d + NZ, NZ), tb)

    def at_y(d):
        return (dp, lax.rem(y + d + NY, NY) * 2 + core)

    sibling = (dp, tb + 1 - 2 * core)
    partners = (
        [at_x(d) for d in range(1, NX)]
        + [at_z(d) for d in (1, 2, -1, -2)]
        + [at_y(d) for d in (1, 2, -1, -2)]
        + [sibling]
    )
    barrier = pltpu.get_barrier_semaphore()
    for partner in partners:
        pl.semaphore_signal(barrier, inc=1, device_id=partner, device_id_type=MESH)
    loads = [
        pltpu.make_async_copy(src, dst, load_sem.at[i])
        for i, (src, dst) in enumerate((
            (it_ref, ibuf.at[pl.ds(0, B), :]),
            (q_ref, qbuf.at[pl.ds(0, B), :]),
            (ow_ref, ow),
            (rw_ref, rw),
            (pw_ref, pw),
            (pq_ref, pq),
            (pi_ref, pi),
            (wq_ref, wq),
            (wi_ref, wi),
        ))
    ]
    for load in loads:
        load.start()
    pl.semaphore_wait(barrier, len(partners))

    copies, drained = [], [0]

    def remote(index, src, dst, device):
        return pltpu.make_async_remote_copy(
            src_ref=src,
            dst_ref=dst,
            send_sem=send_sem.at[index],
            recv_sem=recv_sem.at[index],
            device_id=device,
            device_id_type=MESH,
        )

    def send(src, dst, device):
        copy = remote(len(copies), src, dst, device)
        copy.start()
        copies.append(copy)
        return copy

    def drain():
        for copy in copies[drained[0]:]:
            copy.wait_send()
        drained[0] = len(copies)

    def gather_start(slot, at, source=None):
        source = slot(0, None) if source is None else source
        return {d: send(source, slot(d % 8, None), at(d)) for d in (2, -2, 1, -1)}

    def gather_pass(got, slot, at):
        got[2].wait_recv()
        got[3] = send(slot(2, None), slot(3, None), at(1))
        got[4] = send(slot(2, 0), slot(4, 0), at(2))
        got[-2].wait_recv()
        got[-3] = send(slot(6, None), slot(5, None), at(-1))
        got[-4] = send(slot(6, 1), slot(4, 1), at(-2))

    def wait_for(got, *names):
        for name in names:
            got[name].wait_recv()

    def item_slot(d, half):
        if half is None:
            return ibuf.at[pl.ds(POS[d] * B, B), :]
        return ibuf.at[pl.ds(POS[d] * B + half * 64, 64), :]

    item_in = gather_start(item_slot, at_z, it_ref)
    query_in = {}
    for d in (1, 3, 2):
        query_in[d] = send(q_ref, qbuf.at[pl.ds(d * B, B), :], at_x(d))

    for load in loads:
        load.wait()
    owner_row = iota((NT, B), 0)
    hits = jnp.concatenate([(ow[k:k + 1, :] == owner_row).astype(F32) for k in range(16)], axis=0)
    before = (iota((B, 2 * B), 0) < iota((B, 2 * B), 1)).astype(BF16)
    counts = dot(hits.astype(BF16), before)
    at_row, at_col = iota((256, 256), 0), iota((256, 256), 1)
    earlier = jnp.logical_and(
        lax.bitwise_and(at_row, 15) == lax.bitwise_and(at_col, 15),
        lax.shift_right_logical(at_col, 4) < lax.shift_right_logical(at_row, 4),
    ).astype(BF16)
    taken[...] = (counts[:, 0:B] + dot(earlier, counts[:, B:].astype(BF16))) * hits
    list_row = iota((64, B), 0)
    list_owner, piece = lax.bitwise_and(list_row, 15), lax.shift_right_logical(list_row, 4)
    pair = iota((1, B), 1)
    place = iota((CAP, B), 0)

    def list_slot(k, _):
        lanes = pl.ds(pl.multiple_of(k * B, B), B)
        ranks = taken[pl.ds(pl.multiple_of(k * NT, NT), NT), :]
        rank = jnp.sum(ranks, axis=0, keepdims=True).astype(I32)
        slots_b[:, lanes] = (place == rank).astype(BF16)
        owner, row = ow[pl.ds(k, 1), :], rw[pl.ds(k, 1), :]
        part = jnp.where(
            piece == 0,
            pair + lax.div(k, 8) * B,
            jnp.where(
                piece == 1,
                lax.shift_right_logical(row, 8) + 1,
                jnp.where(piece == 2, lax.bitwise_and(row, 255), 0),
            ),
        )
        slots_a[:, lanes] = jnp.where(list_owner == owner, part, 0).astype(F32).astype(BF16)
        return 0

    lax.fori_loop(0, 16, list_slot, 0, unroll=True)
    lists[0] = dot(slots_a[...], slots_b[...], NT_DIMS).astype(BF16)

    def list_slot_of(d, half):
        if half is None:
            return lists.at[OWN[POS[d]]]
        return lists.at[OWN[POS[d]], pl.ds(half * 32, 32), :]

    list_in = gather_start(list_slot_of, at_y)
    gather_pass(item_in, item_slot, at_z)

    wait_for(query_in, 1, 3, 2)

    def logits(p, _):
        rows = pl.ds(pl.multiple_of(p * B, B), B)
        block = SCALE * dot(ibuf[rows, :], qbuf[...], NT_DIMS)
        top = jnp.max(block, axis=0, keepdims=True)
        block = jnp.exp(block - top)
        ebuf[rows, :] = block
        tops[pl.ds(p, 1), :] = top
        totals[pl.ds(p, 1), :] = jnp.sum(block, axis=0, keepdims=True)
        return 0

    wait_for(item_in, 1, -1)
    lax.fori_loop(0, 5, logits, 0, unroll=True)
    wait_for(item_in, 3, -3)
    lax.fori_loop(5, 7, logits, 0, unroll=True)
    wait_for(item_in, 4, -4)
    logits(7, 0)

    top = jnp.max(tops[...], axis=0, keepdims=True)
    total = jnp.sum(totals[...] * jnp.exp(tops[...] - top), axis=0, keepdims=True)
    weight = pw[...]
    for k in range(NX):
        st_send[k:k + 1, :] = top[:, k * B:(k + 1) * B]
        st_send[NX + k:NX + k + 1, :] = total[:, k * B:(k + 1) * B]
    st_send[8:16, :] = jnp.broadcast_to(weight, (8, B))
    stat_in = {d: send(st_send, st_recv.at[d], at_x(d)) for d in (2, 1, 3)}
    gather_pass(list_in, list_slot_of, at_y)
    wait_for(stat_in, 1, 3, 2)
    maxima, factors = [], []
    for k in range(NX):
        part_tops, part_totals = [st_send[k:k + 1, :]], [st_send[NX + k:NX + k + 1, :]]
        for d in range(1, NX):
            j = (k - d) % NX
            part_tops.append(st_recv[d, j:j + 1, :])
            part_totals.append(st_recv[d, NX + j:NX + j + 1, :])
        row_max = part_tops[0]
        for t in part_tops[1:]:
            row_max = jnp.maximum(row_max, t)
        row_total = sum(s * jnp.exp(t - row_max) for t, s in zip(part_tops, part_totals))
        maxima.append(row_max)
        factors.append((weight if k == 0 else st_recv[k, 8:9, :]) / row_total)
    row_max, factors = jnp.concatenate(maxima, axis=1), jnp.concatenate(factors, axis=1)
    totals[...] = factors * jnp.exp(tops[...] - row_max)

    def item_terms(p):
        rows = pl.ds(pl.multiple_of(p * B, B), B)
        block = (ebuf[rows, :] * totals[pl.ds(p, 1), :]).astype(BF16)
        gbuf[rows, :] = block
        return SCALE * dot(block, qbuf[...])

    def far_terms(p, _):
        gi_send[p] = item_terms(p).astype(BF16)
        return 0

    def near_terms(p, _):
        gi_own[p] = item_terms(p)
        return 0

    far_terms(7, 0)
    half_in = [
        send(gi_send.at[7, pl.ds(0, 64), :], gi_half.at[0], at_z(2)),
        send(gi_send.at[7, pl.ds(64, 64), :], gi_half.at[1], at_z(-2)),
    ]
    lax.fori_loop(5, 7, far_terms, 0, unroll=True)
    relay_in = [
        send(gi_send.at[POS[5]], gi_relay.at[0], at_z(1)),
        send(gi_send.at[POS[3]], gi_relay.at[1], at_z(-1)),
    ]
    lax.fori_loop(3, 5, far_terms, 0, unroll=True)
    grad_in = {d: send(gi_send.at[POS[d]], gi_recv.at[POS[d]], at_z(-d)) for d in (7, 1)}
    lax.fori_loop(0, 3, near_terms, 0, unroll=True)
    same = iota((B, B), 0) == iota((B, B), 1)
    diagonal = ebuf[0:B, 0:B] * totals[0:1, 0:B] - jnp.where(same, weight, 0.0)
    gbuf[0:B, 0:B] = diagonal.astype(BF16)
    gi_own[0] = SCALE * dot(gbuf[0:B, :], qbuf[...])

    terms = SCALE * dot(gbuf[...], ibuf[...], TN)
    gq_own[...] = terms[0:B, :]
    for k in range(1, NX):
        gq_send[k] = terms[k * B:(k + 1) * B, :].astype(BF16)
    query_grad_in = {k: send(gq_send.at[k], gq_recv.at[k], at_x(-k)) for k in (2, 1, 3)}
    for side, (d, rows) in enumerate(((6, slice(0, 64)), (2, slice(64, 128)))):
        p = POS[d]
        relay_in[side].wait_recv()
        half_in[side].wait_recv()
        gi_own[p] += gi_relay[side].astype(F32)
        gi_own[p, rows, :] += gi_half[side].astype(F32)
        gi_send[p] = gi_own[p].astype(BF16)
        grad_in[d] = send(gi_send.at[p], gi_recv.at[p], at_z(-d))

    list_sib = []

    def lists_to_sibling(low, high):
        list_sib.append(send(
            lists.at[pl.ds(OWN[low], high - low)], lists.at[pl.ds(SIB[low], high - low)], sibling
        ))

    wait_for(list_in, 1, -1, 3, -3, 4, -4)
    lists_to_sibling(0, 5)
    lists_to_sibling(5, 8)
    source_row = iota((2 * B, CAP), 0)
    owner_row = iota((NT, CAP), 0)
    low_row = iota((1024, CAP), 0)

    def one_hots(s, _):
        entry = lists[s].astype(F32)
        source, high, low = [
            jnp.sum(jnp.where(owner_row == tb, entry[16 * k:16 * k + 16, :], 0.0), axis=0, keepdims=True).astype(I32)
            for k in range(3)
        ]
        row = (high - 1) * 256 + low
        select[s] = (source == source_row).astype(BF16)
        lanes = pl.ds(pl.multiple_of(s * CAP, CAP), CAP)
        onehot[:, lanes] = (lax.bitwise_and(row - z * B, 1023) == low_row).astype(BF16)
        block = jnp.broadcast_to(lax.shift_right_arithmetic(row, 10), (16, CAP))
        for j in range(NX):
            factor[s, j] = (block == j).astype(BF16)
        return 0

    lax.fori_loop(0, 5, one_hots, 0, unroll=True)
    lax.fori_loop(10, 13, one_hots, 0, unroll=True)

    query_grad = gq_own[...]
    for k in (1, 3, 2):
        query_grad_in[k].wait_recv()
        query_grad += gq_recv[k].astype(F32)
    query_grad = query_grad.astype(BF16)

    pooled_in, pooled_sib = {}, {}

    def pooled_slot(half):
        def slot(d, rows):
            if rows is None:
                return pooled.at[half, OWN[POS[d]]]
            return pooled.at[half, OWN[POS[d]], pl.ds(rows * 64, 64), :]

        return slot

    def to_sibling(half, low, high):
        pooled_sib[half, low] = send(
            pooled.at[half, pl.ds(OWN[low], high - low)], pooled.at[half, pl.ds(SIB[low], high - low)], sibling
        )

    pooled[0, 0] = dot(wq[...], query_grad, NT_DIMS).astype(BF16)
    pooled_in[0] = gather_start(pooled_slot(0), at_y)
    to_sibling(0, 0, 1)
    w_part[0:B, :] = dot(pq[...], query_grad, TN)

    for copy in list_sib:
        copy.wait_recv()
    lax.fori_loop(5, 10, one_hots, 0, unroll=True)
    lax.fori_loop(13, 16, one_hots, 0, unroll=True)
    drain()

    item_grad = gi_own[0]
    for d in (1, 7, 2, 6):
        grad_in[d].wait_recv()
        item_grad += gi_recv[POS[d]].astype(F32)
    item_grad = item_grad.astype(BF16)
    pooled[1, 0] = dot(wi[...], item_grad, NT_DIMS).astype(BF16)
    pooled_in[1] = gather_start(pooled_slot(1), at_y)
    to_sibling(1, 0, 1)
    gather_pass(pooled_in[0], pooled_slot(0), at_y)
    wait_for(pooled_in[0], 1, -1)
    to_sibling(0, 1, 3)
    to_sibling(0, 3, 5)
    w_part[B:, :] = dot(pi[...], item_grad, TN)
    w_in = {}
    for d in (2, 1, 3):
        to_x = lax.rem(x + d, NX)
        w_in[d] = send(w_part.at[pl.ds(pl.multiple_of(to_x * 64, 64), 64), :], wx_recv.at[d], at_x(d))

    def place_values(s, _):
        got = (dot(pooled[0, s], select[s, 0:B, :]) + dot(pooled[1, s], select[s, B:, :])).astype(BF16)
        lanes = pl.ds(pl.multiple_of(s * CAP, CAP), CAP)
        for j in range(NX):
            values[j * E:(j + 1) * E, lanes] = got * jnp.tile(factor[s, j], (8, 1))
        return 0

    def quarter_rows(p):
        return pl.ds(pl.multiple_of(lax.rem(4 + 3 * p * (p + 1), NZ) * B, B), 256)

    def first_part(p, _):
        part = dot(values[:, 0:FIRST], onehot[quarter_rows(p), 0:FIRST], NT_DIMS)
        t_own[p] = part.reshape(NX, E, 256)
        return 0

    gather_pass(pooled_in[1], pooled_slot(1), at_y)
    wait_for(pooled_in[1], 1, -1)
    to_sibling(1, 1, 3)
    to_sibling(1, 3, 5)
    lax.fori_loop(0, 5, place_values, 0, unroll=True)
    for low in (0, 1, 3):
        pooled_sib[0, low].wait_recv()
        pooled_sib[1, low].wait_recv()
    lax.fori_loop(5, 10, place_values, 0, unroll=True)

    w_sum = w_part[pl.ds(pl.multiple_of(x * 64, 64), 64), :]
    for d in (1, 3, 2):
        w_in[d].wait_recv()
        w_sum += wx_recv[d]
    wz_send[...] = w_sum

    def w_chunk(d):
        return pl.ds(pl.multiple_of(lax.rem(z + d + NZ, NZ) * 8, 8), 8)

    wz_in = {}
    for d, via, dst in (
        (4, 2, wz_relay.at[0]), (3, 1, wz_relay.at[1]), (-3, -1, wz_relay.at[2]),
        (1, 1, wz_recv.at[0]), (-1, -1, wz_recv.at[1]),
    ):
        wz_in[d] = send(wz_send.at[w_chunk(d), :], dst, at_z(via))

    lax.fori_loop(0, 2, first_part, 0)
    wait_for(pooled_in[0], 3, -3, 4, -4)
    to_sibling(0, 5, 8)
    wait_for(pooled_in[1], 3, -3, 4, -4)
    to_sibling(1, 5, 8)
    lax.fori_loop(10, 13, place_values, 0, unroll=True)
    lax.fori_loop(2, 4, first_part, 0)
    wait_for(wz_in, 4, 3, -3)
    wz_pass[0] = wz_send[w_chunk(2), :] + wz_relay[0] + wz_relay[1]
    wz_pass[1] = wz_send[w_chunk(-2), :] + wz_relay[2]
    for side, d in ((0, 2), (1, -2)):
        wz_in[d] = send(wz_pass.at[side], wz_recv.at[2 + side], at_z(d))
    pooled_sib[0, 5].wait_recv()
    pooled_sib[1, 5].wait_recv()
    lax.fori_loop(13, 16, place_values, 0, unroll=True)

    half_base = len(copies)
    copies.extend([None] * 8)

    def half_copy(p, side):
        return remote(
            half_base + 2 * p + side,
            t_send.at[p, lax.rem(x + 2, NX), pl.ds(side * 48, 48), :],
            tx_half.at[p, side],
            at_x(1 - 2 * side),
        )

    def send_part(p, part):
        part = t_own[p] + part.reshape(NX, E, 256)
        t_own[p] = part
        t_send[p] = part.astype(BF16)
        half_copy(p, 0).start()
        half_copy(p, 1).start()

    def last_part(p, _):
        send_part(p, dot(values[:, FIRST:], onehot[quarter_rows(p), FIRST:], NT_DIMS))
        return 0

    lax.fori_loop(0, 4, last_part, 0)
    for p in range(4):
        for side in (0, 1):
            copies[half_base + 2 * p + side] = half_copy(p, side)

    def low_columns(p, side):
        return t_send.at[p, :, pl.ds(96, 32), pl.ds(side * B, B)]

    low_half = [
        send(t_send.at[0, pl.ds(2 * side, 2), pl.ds(96, 32), pl.ds(0, B)], lz_half.at[side], at_z(2 - 4 * side))
        for side in (0, 1)
    ]
    low_relay = [
        send(low_columns(1, 1), lz_relay.at[0], at_z(1)),
        send(low_columns(0, 1), lz_relay.at[1], at_z(-1)),
    ]
    low_in = [
        send(low_columns(3, 1), lz_recv.at[0], at_z(1)),
        send(low_columns(2, 1), lz_recv.at[1], at_z(-1)),
    ]

    def low_pass():
        for side in (0, 1):
            low_relay[side].wait_recv()
            low_half[side].wait_recv()
            lz_own[side] = t_own[1 + side, :, 96:, 0:B] + lz_relay[side].astype(F32)
            pair_of = slice(2 * side, 2 * side + 2)
            lz_own[side, pair_of] += lz_half[side].astype(F32)
            lz_send[side] = lz_own[side].astype(BF16)
            low_in.append(send(lz_send.at[side], lz_recv.at[2 + side], at_z(2 - 4 * side)))

    low_x = {}

    def low_sum():
        part = t_own[3, :, 96:, 0:B]
        for k in range(4):
            low_in[k].wait_recv()
            part += lz_recv[k].astype(F32)
        lz_own[2] = part
        lx_send[...] = part.astype(BF16)
        for d in (2, 1, 3):
            low_x[d] = send(lx_send.at[lax.rem(x + d, NX)], lx_recv.at[d], at_x(d))

    relay_in, tz_half_in, tz_relay_in, tz_in = {}, {}, {}, {}

    def table_relay(p):
        for side, step in ((0, 1), (1, -1)):
            copies[half_base + 2 * p + side].wait_recv()
            near = lax.rem(x + step + NX, NX)
            for half in (0, 1):
                rows = slice(half * 48, half * 48 + 48)
                part = t_own[p, near, rows, :]
                if half == side:
                    part += tx_half[p, side].astype(F32)
                tx_relay[p, side, rows, :] = part.astype(BF16)
            relay_in[p, side] = send(tx_relay.at[p, side], tx_recv.at[p, side], at_x(step))

    def table_sum(p):
        part = t_own[p, x, 0:96, :]
        for side in (0, 1):
            relay_in[p, side].wait_recv()
            part += tx_recv[p, side].astype(F32)
        tz_send[p] = part[:, B:].astype(BF16)
        if p == 0:
            tz_first[...] = part[:, 0:B].astype(BF16)
            for side in (0, 1):
                tz_half_in[side] = send(
                    tz_first.at[pl.ds(side * 48, 48), :], tz_half.at[side], at_z(2 - 4 * side)
                )
        else:
            tz_own[p - 1] = part[:, 0:B]
        if p < 2:
            tz_relay_in[1 - p] = send(tz_send.at[p], tz_relay.at[1 - p], at_z(2 * p - 1))
        else:
            tz_in[3 - p] = send(tz_send.at[p], tz_recv.at[3 - p], at_z(2 * p - 5))

    def table_pass():
        for side in (0, 1):
            tz_relay_in[side].wait_recv()
            tz_half_in[side].wait_recv()
            rows = slice(side * 48, side * 48 + 48)
            tz_own[side] += tz_relay[side].astype(F32)
            tz_own[side, rows, :] += tz_half[side].astype(F32)
            tz_back[side] = tz_own[side].astype(BF16)
            tz_in[2 + side] = send(tz_back.at[side], tz_recv.at[2 + side], at_z(2 - 4 * side))

    def small_pass(got, slot, at, there):
        got[2].wait_recv()
        got[3] = send(slot(2), there(2, 3), at(1))
        got[4] = send(slot(2), there(2, 4), at(2))
        got[-2].wait_recv()
        got[5] = send(slot(-2), there(-2, 5), at(-1))

    def wy_slot(d):
        return wy_recv.at[0, d % 8]

    def w_rows(d):
        place = x * NZ + lax.rem(z - d + NZ, NZ)
        return gw_ref.at[pl.ds(pl.multiple_of(place * 8, 8), 8), pl.ds(pl.multiple_of(core * B, B), B)]

    table_relay(0)
    table_relay(1)
    w_sum = wz_send[w_chunk(0), :]
    wait_for(wz_in, 1, -1, 2, -2)
    for k in range(4):
        w_sum += wz_recv[k]
    wy_recv[0, 0] = w_sum
    wy_in = {d: send(wy_slot(0), wy_slot(d), at_y(d)) for d in (2, -2, 1, -1)}

    table_sum(0)
    low_pass()
    table_relay(2)
    small_pass(wy_in, wy_slot, at_y, lambda here, d: wy_slot(d))
    table_sum(1)
    table_relay(3)
    wait_for(wy_in, 1, -1, 3, 4, 5)
    wy_sib = send(wy_recv.at[0], wy_recv.at[1], sibling)
    table_sum(2)
    low_sum()
    table_pass()

    wy_sib.wait_recv()
    w_sum = wy_recv[0, 0]
    for d in range(1, NY):
        w_sum += wy_recv[0, d]
    for d in range(NY):
        w_sum += wy_recv[1, d]
    w_own[...] = w_sum
    own_lanes = pl.ds(pl.multiple_of(core * B, B), B)
    gw_ref[pl.ds(pl.multiple_of(dp * 8, 8), 8), own_lanes] = w_own[:, own_lanes]
    w_back = {d: send(w_rows(0), w_rows(0), at_z(d)) for d in (2, -2, 1, -1)}

    table_sum(3)
    drain()

    low = lz_own[2, x]
    for d in (1, 3, 2):
        low_x[d].wait_recv()
        low += lx_recv[d].astype(F32)
    part = tz_own[2]
    for k in (1, 0, 2, 3):
        tz_in[k].wait_recv()
        part += tz_recv[k].astype(F32)
    rows = jnp.concatenate([part, low], axis=0).T.astype(BF16)
    t_back[x, 0] = rows[0:96]
    l_back[0, x] = rows[96:]

    def back_slot(d, half):
        if half is None:
            return t_back.at[x, POS[d]]
        return t_back.at[x, POS[d], pl.ds(half * 48, 48), :]

    def low_slot(d, half):
        if half is None:
            return l_back.at[POS[d]]
        return l_back.at[POS[d], pl.ds(2 * half, 2)]

    back = gather_start(back_slot, at_z)
    low_back = [send(l_back.at[0, x], l_back.at[0, x], at_x(d)) for d in (2, 1, 3)]
    near_in, far_in = {}, []

    def to_near(low, high):
        rows = t_back.at[x, pl.ds(low, high - low)]
        for side, step in ((0, 1), (1, -1)):
            near_in[low, side] = send(rows, rows, at_x(step))

    def to_far(low, high):
        middle = {1: None, 2: low + 1, 3: None}[high - low]
        for side, step in ((0, 1), (1, -1)):
            near_in[low, side].wait_recv()
            held = lax.rem(x - step + NX, NX)
            if middle is None:
                rows = t_back.at[held, pl.ds(low, high - low), pl.ds(side * 48, 48), :]
            else:
                rows = t_back.at[held, low + side]
            far_in.append(send(rows, rows, at_x(step)))

    to_near(0, 1)

    small_pass(w_back, w_rows, at_z, lambda here, d: w_rows(here))
    gather_pass(back, back_slot, at_z)
    to_near(1, 3)
    for copy in low_back:
        copy.wait_recv()
    low_back = gather_start(low_slot, at_z)
    wait_for(w_back, 1, -1, 3, 4, 5)
    w_held = gw_ref.at[pl.ds(pl.multiple_of(x * 64, 64), 64), pl.ds(pl.multiple_of(core * B, B), B)]
    w_x = [send(w_held, w_held, at_x(step)) for step in (2, 1, 3)]
    to_far(0, 1)
    wait_for(back, 1, -1)
    to_near(3, 5)
    to_far(1, 3)
    wait_for(back, 3, -3, 4, -4)
    to_near(5, 8)
    gather_pass(low_back, low_slot, at_z)
    to_far(3, 5)

    def rows_of(far, p, d):
        place = (far * NZ + lax.rem(z - d + NZ, NZ)) * B
        table_ref[pl.ds(pl.multiple_of(place, B), 96), :] = t_back[far, p]

    def low_rows_of(p, d):
        for far in range(NX):
            place = (far * NZ + lax.rem(z - d + NZ, NZ)) * B + 96
            table_ref[pl.ds(pl.multiple_of(place, 32), 32), :] = l_back[p, far]

    to_far(5, 8)
    for copy in w_x:
        copy.wait_recv()
    w_half = gw_ref.at[:, pl.ds(pl.multiple_of(core * B, B), B)]
    far_in.append(send(w_half, w_half, sibling))
    for p, d in enumerate(ARRIVE):
        rows_of(x, p, d)
        rows_of(lax.rem(x + 1, NX), p, d)
        rows_of(lax.rem(x + 3, NX), p, d)
    wait_for(low_back, 1, -1, 3, -3, 4, -4)
    for p, d in enumerate(ARRIVE):
        low_rows_of(p, d)
    drain()
    for copy in far_in:
        copy.wait_recv()
    for p, d in enumerate(ARRIVE):
        rows_of(lax.rem(x + 2, NX), p, d)
    drain()


def finish(table_ref, gw_ref, out_ref, gwq_ref, gwi_ref, wide, sem):
    copies = [
        pltpu.make_async_copy(gw_ref.at[pl.ds(0, B), :], gwq_ref, sem.at[8]),
        pltpu.make_async_copy(gw_ref.at[pl.ds(B, B), :], gwi_ref, sem.at[9]),
    ]
    for copy in copies:
        copy.start()
    for i in range(8):
        wide[i] = table_ref[i * 512:(i + 1) * 512, :].astype(F32)
        copies.append(pltpu.make_async_copy(wide.at[i], out_ref.at[pl.ds(i * 512, 512), :], sem.at[i]))
        copies[-1].start()
    for copy in copies:
        copy.wait()


def on_device(q, it, pq, pi, wq, wi, pw, owner, row):
    def vmem(*shape, dtype=F32):
        return pltpu.VMEM(shape, dtype)

    table, gw = pl.pallas_call(
        kernel,
        out_shape=(
            jax.ShapeDtypeStruct((4096, E), BF16),
            jax.ShapeDtypeStruct((2 * B, W), F32),
        ),
        in_specs=[pl.BlockSpec(memory_space=pltpu.HBM)] * 9,
        out_specs=(pl.BlockSpec(memory_space=pltpu.VMEM),) * 2,
        scratch_shapes=[
            vmem(B, E, dtype=BF16),
            vmem(B, E, dtype=BF16),
            vmem(E, W, dtype=BF16),
            vmem(E, W, dtype=BF16),
            vmem(1, B),
            vmem(16, B, dtype=I32),
            vmem(16, B, dtype=I32),
            vmem(NZ * B, W, dtype=BF16),
            vmem(NX * B, W, dtype=BF16),
            vmem(NZ * B, NX * B),
            vmem(NZ * B, NX * B, dtype=BF16),
            vmem(NZ, NX * B),
            vmem(NZ, NX * B),
            vmem(16, B),
            vmem(NX, 16, B),
            vmem(NZ, B, W, dtype=BF16),
            vmem(2, B, W, dtype=BF16),
            vmem(2, 64, W, dtype=BF16),
            vmem(NZ, B, W, dtype=BF16),
            vmem(3, B, W),
            vmem(NX, B, W, dtype=BF16),
            vmem(NX, B, W, dtype=BF16),
            vmem(B, W),
            vmem(256, B),
            vmem(64, 16 * B, dtype=BF16),
            vmem(CAP, 16 * B, dtype=BF16),
            vmem(NT, 64, CAP, dtype=BF16),
            vmem(1024, NT * CAP, dtype=BF16),
            vmem(NT, 2 * B, CAP, dtype=BF16),
            vmem(NT, NX, 16, CAP, dtype=BF16),
            vmem(2, NT, E, B, dtype=BF16),
            vmem(NX * E, NT * CAP, dtype=BF16),
            vmem(2 * B, W),
            vmem(NX, 64, W),
            vmem(64, W),
            vmem(3, 8, W),
            vmem(2, 8, W),
            vmem(4, 8, W),
            vmem(2, NY, 8, W),
            vmem(8, W),
            vmem(4, NX, E, 256),
            vmem(4, NX, E, 256, dtype=BF16),
            vmem(4, 2, 48, 256, dtype=BF16),
            vmem(4, 2, 96, 256, dtype=BF16),
            vmem(4, 2, 96, 256, dtype=BF16),
            vmem(96, B, dtype=BF16),
            vmem(3, 96, B),
            vmem(4, 96, B, dtype=BF16),
            vmem(2, 48, B, dtype=BF16),
            vmem(2, 96, B, dtype=BF16),
            vmem(2, 96, B, dtype=BF16),
            vmem(4, 96, B, dtype=BF16),
            vmem(2, 2, 32, B, dtype=BF16),
            vmem(2, NX, 32, B, dtype=BF16),
            vmem(3, NX, 32, B),
            vmem(2, NX, 32, B, dtype=BF16),
            vmem(4, NX, 32, B, dtype=BF16),
            vmem(NX, 32, B, dtype=BF16),
            vmem(NX, 32, B, dtype=BF16),
            vmem(NX, NZ, 96, E, dtype=BF16),
            vmem(NZ, NX, 32, E, dtype=BF16),
            pltpu.SemaphoreType.DMA((9,)),
            pltpu.SemaphoreType.DMA((N_COPIES,)),
            pltpu.SemaphoreType.DMA((N_COPIES,)),
        ],
        compiler_params=pltpu.CompilerParams(
            collective_id=0, has_side_effects=True, vmem_limit_bytes=40 * 1024 * 1024
        ),
    )(*[
        pltpu.with_memory_space_constraint(a, pltpu.HBM)
        for a in (
            q, it, pq, pi, wq, wi, pw.reshape(1, B), owner.reshape(B, 16).T, row.reshape(B, 16).T
        )
    ])
    return pl.pallas_call(
        finish,
        out_shape=(
            jax.ShapeDtypeStruct((4096, E), F32),
            jax.ShapeDtypeStruct((B, W), F32),
            jax.ShapeDtypeStruct((B, W), F32),
        ),
        in_specs=[pl.BlockSpec(memory_space=pltpu.VMEM)] * 2,
        out_specs=(pl.BlockSpec(memory_space=pltpu.HBM),) * 3,
        scratch_shapes=[vmem(8, 512, E), pltpu.SemaphoreType.DMA((10,))],
        compiler_params=pltpu.CompilerParams(vmem_limit_bytes=12 * 1024 * 1024),
    )(table, gw)


def solution(mesh):
    both = ("dp", "table")
    placed = (
        P(both, None),
        P(both, None),
        P(both, None),
        P(both, None),
        P(),
        P(),
        P(both),
        P(both, None, None),
        P(both, None, None),
    )
    return jax.shard_map(
        on_device,
        mesh=mesh,
        in_specs=placed,
        out_specs=(P("table", None), P(), P()),
        check_vma=False,
    )
```

```python
import math

import jax
import jax.numpy as jnp
from jax import lax
from jax.experimental import pallas as pl
from jax.experimental.pallas import tpu as pltpu
from jax.sharding import PartitionSpec as P

MESH = pl.DeviceIdType.MESH
F32, BF16, I32 = jnp.float32, jnp.bfloat16, jnp.int32
NX, NZ, NY = 4, 8, 8
B, W, E = 128, 256, 128
NT = 2 * NY
CAP = 256
SCALE = 1.0 / math.sqrt(W)
N_COPIES = 176

NN = (((1,), (0,)), ((), ()))
NT_DIMS = (((1,), (1,)), ((), ()))
TN = (((0,), (0,)), ((), ()))


def dot(a, b, dims=NN):
    return lax.dot_general(a, b, dims, preferred_element_type=F32)


def iota(shape, dim):
    return lax.broadcasted_iota(I32, shape, dim)


ARRIVE = (0, 2, 6, 1, 7, 3, 5, 4)
POS = {d: p for p, d in enumerate(ARRIVE)}
OWN = (0, 1, 2, 3, 4, 10, 11, 12)
SIB = (5, 6, 7, 8, 9, 13, 14, 15)
FIRST = 10 * CAP


def kernel(
    q_ref, it_ref, pq_ref, pi_ref, wq_ref, wi_ref, pw_ref, ow_ref, rw_ref,
    table_ref, gw_ref,
    pq, pi, wq, wi, pw, ow, rw,
    ibuf, qbuf, ebuf, gbuf, tops, totals, st_send, st_recv,
    gi_send, gi_relay, gi_half, gi_recv, gi_own, gq_send, gq_recv, gq_own,
    taken, slots_a, slots_b, lists, onehot, select, factor, pooled, values,
    w_part, wx_recv, wz_send, wz_relay, wz_pass, wz_recv, wy_recv, w_own,
    t_own, t_send, tx_half, tx_relay, tx_recv, tz_first, tz_own, tz_send, tz_half, tz_relay, tz_back, tz_recv,
    lz_half, lz_relay, lz_own, lz_send, lz_recv, lx_send, lx_recv, t_back, l_back,
    load_sem, send_sem, recv_sem,
):
    dp, tb = lax.axis_index("dp"), lax.axis_index("table")
    x, z = lax.div(dp, NZ), lax.rem(dp, NZ)
    y, core = lax.div(tb, 2), lax.rem(tb, 2)

    def at_x(d):
        return (lax.rem(x + d + NX, NX) * NZ + z, tb)

    def at_z(d):
        return (x * NZ + lax.rem(z + d + NZ, NZ), tb)

    def at_y(d):
        return (dp, lax.rem(y + d + NY, NY) * 2 + core)

    sibling = (dp, tb + 1 - 2 * core)
    partners = (
        [at_x(d) for d in range(1, NX)]
        + [at_z(d) for d in (1, 2, -1, -2)]
        + [at_y(d) for d in (1, 2, -1, -2)]
        + [sibling]
    )
    barrier = pltpu.get_barrier_semaphore()
    for partner in partners:
        pl.semaphore_signal(barrier, inc=1, device_id=partner, device_id_type=MESH)
    loads = [
        pltpu.make_async_copy(src, dst, load_sem.at[i])
        for i, (src, dst) in enumerate((
            (it_ref, ibuf.at[pl.ds(0, B), :]),
            (q_ref, qbuf.at[pl.ds(0, B), :]),
            (ow_ref, ow),
            (rw_ref, rw),
            (pw_ref, pw),
            (pq_ref, pq),
            (pi_ref, pi),
            (wq_ref, wq),
            (wi_ref, wi),
        ))
    ]
    for load in loads:
        load.start()
    pl.semaphore_wait(barrier, len(partners))

    copies, drained = [], [0]

    def remote(index, src, dst, device):
        return pltpu.make_async_remote_copy(
            src_ref=src,
            dst_ref=dst,
            send_sem=send_sem.at[index],
            recv_sem=recv_sem.at[index],
            device_id=device,
            device_id_type=MESH,
        )

    def send(src, dst, device):
        copy = remote(len(copies), src, dst, device)
        copy.start()
        copies.append(copy)
        return copy

    def drain():
        for copy in copies[drained[0]:]:
            copy.wait_send()
        drained[0] = len(copies)

    def gather_start(slot, at, source=None):
        source = slot(0, None) if source is None else source
        return {d: send(source, slot(d % 8, None), at(d)) for d in (2, -2, 1, -1)}

    def gather_pass(got, slot, at):
        got[2].wait_recv()
        got[3] = send(slot(2, None), slot(3, None), at(1))
        got[4] = send(slot(2, 0), slot(4, 0), at(2))
        got[-2].wait_recv()
        got[-3] = send(slot(6, None), slot(5, None), at(-1))
        got[-4] = send(slot(6, 1), slot(4, 1), at(-2))

    def wait_for(got, *names):
        for name in names:
            got[name].wait_recv()

    def item_slot(d, half):
        if half is None:
            return ibuf.at[pl.ds(POS[d] * B, B), :]
        return ibuf.at[pl.ds(POS[d] * B + half * 64, 64), :]

    item_in = gather_start(item_slot, at_z, it_ref)
    query_in = {}
    for d in (1, 3, 2):
        query_in[d] = send(q_ref, qbuf.at[pl.ds(d * B, B), :], at_x(d))

    for load in loads:
        load.wait()
    owner_row = iota((NT, B), 0)
    hits = jnp.concatenate([(ow[k:k + 1, :] == owner_row).astype(F32) for k in range(16)], axis=0)
    before = (iota((B, 2 * B), 0) < iota((B, 2 * B), 1)).astype(BF16)
    counts = dot(hits.astype(BF16), before)
    at_row, at_col = iota((256, 256), 0), iota((256, 256), 1)
    earlier = jnp.logical_and(
        lax.bitwise_and(at_row, 15) == lax.bitwise_and(at_col, 15),
        lax.shift_right_logical(at_col, 4) < lax.shift_right_logical(at_row, 4),
    ).astype(BF16)
    taken[...] = (counts[:, 0:B] + dot(earlier, counts[:, B:].astype(BF16))) * hits
    list_row = iota((64, B), 0)
    list_owner, piece = lax.bitwise_and(list_row, 15), lax.shift_right_logical(list_row, 4)
    pair = iota((1, B), 1)
    place = iota((CAP, B), 0)

    def list_slot(k, _):
        lanes = pl.ds(pl.multiple_of(k * B, B), B)
        ranks = taken[pl.ds(pl.multiple_of(k * NT, NT), NT), :]
        rank = jnp.sum(ranks, axis=0, keepdims=True).astype(I32)
        slots_b[:, lanes] = (place == rank).astype(BF16)
        owner, row = ow[pl.ds(k, 1), :], rw[pl.ds(k, 1), :]
        part = jnp.where(
            piece == 0,
            pair + lax.div(k, 8) * B,
            jnp.where(
                piece == 1,
                lax.shift_right_logical(row, 8) + 1,
                jnp.where(piece == 2, lax.bitwise_and(row, 255), 0),
            ),
        )
        slots_a[:, lanes] = jnp.where(list_owner == owner, part, 0).astype(F32).astype(BF16)
        return 0

    lax.fori_loop(0, 16, list_slot, 0, unroll=True)
    lists[0] = dot(slots_a[...], slots_b[...], NT_DIMS).astype(BF16)

    def list_slot_of(d, half):
        if half is None:
            return lists.at[OWN[POS[d]]]
        return lists.at[OWN[POS[d]], pl.ds(half * 32, 32), :]

    list_in = gather_start(list_slot_of, at_y)
    gather_pass(item_in, item_slot, at_z)

    wait_for(query_in, 1, 3, 2)

    def logits(p, _):
        rows = pl.ds(pl.multiple_of(p * B, B), B)
        block = SCALE * dot(ibuf[rows, :], qbuf[...], NT_DIMS)
        top = jnp.max(block, axis=0, keepdims=True)
        block = jnp.exp(block - top)
        ebuf[rows, :] = block
        tops[pl.ds(p, 1), :] = top
        totals[pl.ds(p, 1), :] = jnp.sum(block, axis=0, keepdims=True)
        return 0

    wait_for(item_in, 1, -1)
    lax.fori_loop(0, 5, logits, 0, unroll=True)
    wait_for(item_in, 3, -3)
    lax.fori_loop(5, 7, logits, 0, unroll=True)
    wait_for(item_in, 4, -4)
    logits(7, 0)

    top = jnp.max(tops[...], axis=0, keepdims=True)
    total = jnp.sum(totals[...] * jnp.exp(tops[...] - top), axis=0, keepdims=True)
    weight = pw[...]
    for k in range(NX):
        st_send[k:k + 1, :] = top[:, k * B:(k + 1) * B]
        st_send[NX + k:NX + k + 1, :] = total[:, k * B:(k + 1) * B]
    st_send[8:16, :] = jnp.broadcast_to(weight, (8, B))
    stat_in = {d: send(st_send, st_recv.at[d], at_x(d)) for d in (2, 1, 3)}
    gather_pass(list_in, list_slot_of, at_y)
    wait_for(stat_in, 1, 3, 2)
    maxima, factors = [], []
    for k in range(NX):
        part_tops, part_totals = [st_send[k:k + 1, :]], [st_send[NX + k:NX + k + 1, :]]
        for d in range(1, NX):
            j = (k - d) % NX
            part_tops.append(st_recv[d, j:j + 1, :])
            part_totals.append(st_recv[d, NX + j:NX + j + 1, :])
        row_max = part_tops[0]
        for t in part_tops[1:]:
            row_max = jnp.maximum(row_max, t)
        row_total = sum(s * jnp.exp(t - row_max) for t, s in zip(part_tops, part_totals))
        maxima.append(row_max)
        factors.append((weight if k == 0 else st_recv[k, 8:9, :]) / row_total)
    row_max, factors = jnp.concatenate(maxima, axis=1), jnp.concatenate(factors, axis=1)
    totals[...] = factors * jnp.exp(tops[...] - row_max)

    def item_terms(p):
        rows = pl.ds(pl.multiple_of(p * B, B), B)
        block = (ebuf[rows, :] * totals[pl.ds(p, 1), :]).astype(BF16)
        gbuf[rows, :] = block
        return SCALE * dot(block, qbuf[...])

    def far_terms(p, _):
        gi_send[p] = item_terms(p).astype(BF16)
        return 0

    def near_terms(p, _):
        gi_own[p] = item_terms(p)
        return 0

    far_terms(7, 0)
    half_in = [
        send(gi_send.at[7, pl.ds(0, 64), :], gi_half.at[0], at_z(2)),
        send(gi_send.at[7, pl.ds(64, 64), :], gi_half.at[1], at_z(-2)),
    ]
    lax.fori_loop(5, 7, far_terms, 0, unroll=True)
    relay_in = [
        send(gi_send.at[POS[5]], gi_relay.at[0], at_z(1)),
        send(gi_send.at[POS[3]], gi_relay.at[1], at_z(-1)),
    ]
    lax.fori_loop(3, 5, far_terms, 0, unroll=True)
    grad_in = {d: send(gi_send.at[POS[d]], gi_recv.at[POS[d]], at_z(-d)) for d in (7, 1)}
    lax.fori_loop(0, 3, near_terms, 0, unroll=True)
    same = iota((B, B), 0) == iota((B, B), 1)
    diagonal = ebuf[0:B, 0:B] * totals[0:1, 0:B] - jnp.where(same, weight, 0.0)
    gbuf[0:B, 0:B] = diagonal.astype(BF16)
    gi_own[0] = SCALE * dot(gbuf[0:B, :], qbuf[...])

    terms = SCALE * dot(gbuf[...], ibuf[...], TN)
    gq_own[...] = terms[0:B, :]
    for k in range(1, NX):
        gq_send[k] = terms[k * B:(k + 1) * B, :].astype(BF16)
    query_grad_in = {k: send(gq_send.at[k], gq_recv.at[k], at_x(-k)) for k in (2, 1, 3)}
    for side, (d, rows) in enumerate(((6, slice(0, 64)), (2, slice(64, 128)))):
        p = POS[d]
        relay_in[side].wait_recv()
        half_in[side].wait_recv()
        gi_own[p] += gi_relay[side].astype(F32)
        gi_own[p, rows, :] += gi_half[side].astype(F32)
        gi_send[p] = gi_own[p].astype(BF16)
        grad_in[d] = send(gi_send.at[p], gi_recv.at[p], at_z(-d))

    list_sib = []

    def lists_to_sibling(low, high):
        list_sib.append(send(
            lists.at[pl.ds(OWN[low], high - low)], lists.at[pl.ds(SIB[low], high - low)], sibling
        ))

    wait_for(list_in, 1, -1, 3, -3, 4, -4)
    lists_to_sibling(0, 5)
    lists_to_sibling(5, 8)
    source_row = iota((2 * B, CAP), 0)
    owner_row = iota((NT, CAP), 0)
    low_row = iota((1024, CAP), 0)

    def one_hots(s, _):
        entry = lists[s].astype(F32)
        source, high, low = [
            jnp.sum(jnp.where(owner_row == tb, entry[16 * k:16 * k + 16, :], 0.0), axis=0, keepdims=True).astype(I32)
            for k in range(3)
        ]
        row = (high - 1) * 256 + low
        select[s] = (source == source_row).astype(BF16)
        lanes = pl.ds(pl.multiple_of(s * CAP, CAP), CAP)
        onehot[:, lanes] = (lax.bitwise_and(row - z * B, 1023) == low_row).astype(BF16)
        block = jnp.broadcast_to(lax.shift_right_arithmetic(row, 10), (16, CAP))
        for j in range(NX):
            factor[s, j] = (block == j).astype(BF16)
        return 0

    lax.fori_loop(0, 5, one_hots, 0)
    lax.fori_loop(10, 13, one_hots, 0)

    query_grad = gq_own[...]
    for k in (1, 3, 2):
        query_grad_in[k].wait_recv()
        query_grad += gq_recv[k].astype(F32)
    query_grad = query_grad.astype(BF16)

    pooled_in, pooled_sib = {}, {}

    def pooled_slot(half):
        def slot(d, rows):
            if rows is None:
                return pooled.at[half, OWN[POS[d]]]
            return pooled.at[half, OWN[POS[d]], pl.ds(rows * 64, 64), :]

        return slot

    def to_sibling(half, low, high):
        pooled_sib[half, low] = send(
            pooled.at[half, pl.ds(OWN[low], high - low)], pooled.at[half, pl.ds(SIB[low], high - low)], sibling
        )

    pooled[0, 0] = dot(wq[...], query_grad, NT_DIMS).astype(BF16)
    pooled_in[0] = gather_start(pooled_slot(0), at_y)
    to_sibling(0, 0, 1)
    w_part[0:B, :] = dot(pq[...], query_grad, TN)

    for copy in list_sib:
        copy.wait_recv()
    lax.fori_loop(5, 10, one_hots, 0)
    lax.fori_loop(13, 16, one_hots, 0)
    drain()

    item_grad = gi_own[0]
    for d in (1, 7, 2, 6):
        grad_in[d].wait_recv()
        item_grad += gi_recv[POS[d]].astype(F32)
    item_grad = item_grad.astype(BF16)
    pooled[1, 0] = dot(wi[...], item_grad, NT_DIMS).astype(BF16)
    pooled_in[1] = gather_start(pooled_slot(1), at_y)
    to_sibling(1, 0, 1)
    gather_pass(pooled_in[0], pooled_slot(0), at_y)
    wait_for(pooled_in[0], 1, -1)
    to_sibling(0, 1, 3)
    to_sibling(0, 3, 5)
    w_part[B:, :] = dot(pi[...], item_grad, TN)
    w_in = {}
    for d in (2, 1, 3):
        to_x = lax.rem(x + d, NX)
        w_in[d] = send(w_part.at[pl.ds(pl.multiple_of(to_x * 64, 64), 64), :], wx_recv.at[d], at_x(d))

    def place_values(s, _):
        got = (dot(pooled[0, s], select[s, 0:B, :]) + dot(pooled[1, s], select[s, B:, :])).astype(BF16)
        lanes = pl.ds(pl.multiple_of(s * CAP, CAP), CAP)
        for j in range(NX):
            values[j * E:(j + 1) * E, lanes] = got * jnp.tile(factor[s, j], (8, 1))
        return 0

    def quarter_rows(p):
        return pl.ds(pl.multiple_of(lax.rem(4 + 3 * p * (p + 1), NZ) * B, B), 256)

    def first_part(p, _):
        part = dot(values[:, 0:FIRST], onehot[quarter_rows(p), 0:FIRST], NT_DIMS)
        t_own[p] = part.reshape(NX, E, 256)
        return 0

    gather_pass(pooled_in[1], pooled_slot(1), at_y)
    wait_for(pooled_in[1], 1, -1)
    to_sibling(1, 1, 3)
    to_sibling(1, 3, 5)
    lax.fori_loop(0, 5, place_values, 0, unroll=True)
    for low in (0, 1, 3):
        pooled_sib[0, low].wait_recv()
        pooled_sib[1, low].wait_recv()
    lax.fori_loop(5, 10, place_values, 0, unroll=True)

    w_sum = w_part[pl.ds(pl.multiple_of(x * 64, 64), 64), :]
    for d in (1, 3, 2):
        w_in[d].wait_recv()
        w_sum += wx_recv[d]
    wz_send[...] = w_sum

    def w_chunk(d):
        return pl.ds(pl.multiple_of(lax.rem(z + d + NZ, NZ) * 8, 8), 8)

    wz_in = {}
    for d, via, dst in (
        (4, 2, wz_relay.at[0]), (3, 1, wz_relay.at[1]), (-3, -1, wz_relay.at[2]),
        (1, 1, wz_recv.at[0]), (-1, -1, wz_recv.at[1]),
    ):
        wz_in[d] = send(wz_send.at[w_chunk(d), :], dst, at_z(via))

    lax.fori_loop(0, 2, first_part, 0, unroll=True)
    wait_for(pooled_in[0], 3, -3, 4, -4)
    to_sibling(0, 5, 8)
    wait_for(pooled_in[1], 3, -3, 4, -4)
    to_sibling(1, 5, 8)
    lax.fori_loop(10, 13, place_values, 0, unroll=True)
    lax.fori_loop(2, 4, first_part, 0, unroll=True)
    wait_for(wz_in, 4, 3, -3)
    wz_pass[0] = wz_send[w_chunk(2), :] + wz_relay[0] + wz_relay[1]
    wz_pass[1] = wz_send[w_chunk(-2), :] + wz_relay[2]
    for side, d in ((0, 2), (1, -2)):
        wz_in[d] = send(wz_pass.at[side], wz_recv.at[2 + side], at_z(d))
    pooled_sib[0, 5].wait_recv()
    pooled_sib[1, 5].wait_recv()
    lax.fori_loop(13, 16, place_values, 0, unroll=True)

    half_base = len(copies)
    copies.extend([None] * 8)

    def half_copy(p, side):
        return remote(
            half_base + 2 * p + side,
            t_send.at[p, lax.rem(x + 2, NX), pl.ds(side * 48, 48), :],
            tx_half.at[p, side],
            at_x(1 - 2 * side),
        )

    def send_part(p, part):
        part = t_own[p] + part.reshape(NX, E, 256)
        t_own[p] = part
        t_send[p] = part.astype(BF16)
        half_copy(p, 0).start()
        half_copy(p, 1).start()

    def last_part(p, _):
        send_part(p, dot(values[:, FIRST:], onehot[quarter_rows(p), FIRST:], NT_DIMS))
        return 0

    lax.fori_loop(0, 4, last_part, 0, unroll=True)
    for p in range(4):
        for side in (0, 1):
            copies[half_base + 2 * p + side] = half_copy(p, side)

    def low_columns(p, side):
        return t_send.at[p, :, pl.ds(96, 32), pl.ds(side * B, B)]

    low_half = [
        send(t_send.at[0, pl.ds(2 * side, 2), pl.ds(96, 32), pl.ds(0, B)], lz_half.at[side], at_z(2 - 4 * side))
        for side in (0, 1)
    ]
    low_relay = [
        send(low_columns(1, 1), lz_relay.at[0], at_z(1)),
        send(low_columns(0, 1), lz_relay.at[1], at_z(-1)),
    ]
    low_in = [
        send(low_columns(3, 1), lz_recv.at[0], at_z(1)),
        send(low_columns(2, 1), lz_recv.at[1], at_z(-1)),
    ]

    def low_pass():
        for side in (0, 1):
            low_relay[side].wait_recv()
            low_half[side].wait_recv()
            lz_own[side] = t_own[1 + side, :, 96:, 0:B] + lz_relay[side].astype(F32)
            pair_of = slice(2 * side, 2 * side + 2)
            lz_own[side, pair_of] += lz_half[side].astype(F32)
            lz_send[side] = lz_own[side].astype(BF16)
            low_in.append(send(lz_send.at[side], lz_recv.at[2 + side], at_z(2 - 4 * side)))

    low_x = {}

    def low_sum():
        part = t_own[3, :, 96:, 0:B]
        for k in range(4):
            low_in[k].wait_recv()
            part += lz_recv[k].astype(F32)
        lz_own[2] = part
        lx_send[...] = part.astype(BF16)
        for d in (2, 1, 3):
            low_x[d] = send(lx_send.at[lax.rem(x + d, NX)], lx_recv.at[d], at_x(d))

    relay_in, tz_half_in, tz_relay_in, tz_in = {}, {}, {}, {}

    def table_relay(p):
        for side, step in ((0, 1), (1, -1)):
            copies[half_base + 2 * p + side].wait_recv()
            near = lax.rem(x + step + NX, NX)
            for half in (0, 1):
                rows = slice(half * 48, half * 48 + 48)
                part = t_own[p, near, rows, :]
                if half == side:
                    part += tx_half[p, side].astype(F32)
                tx_relay[p, side, rows, :] = part.astype(BF16)
            relay_in[p, side] = send(tx_relay.at[p, side], tx_recv.at[p, side], at_x(step))

    def table_sum(p):
        part = t_own[p, x, 0:96, :]
        for side in (0, 1):
            relay_in[p, side].wait_recv()
            part += tx_recv[p, side].astype(F32)
        tz_send[p] = part[:, B:].astype(BF16)
        if p == 0:
            tz_first[...] = part[:, 0:B].astype(BF16)
            for side in (0, 1):
                tz_half_in[side] = send(
                    tz_first.at[pl.ds(side * 48, 48), :], tz_half.at[side], at_z(2 - 4 * side)
                )
        else:
            tz_own[p - 1] = part[:, 0:B]
        if p < 2:
            tz_relay_in[1 - p] = send(tz_send.at[p], tz_relay.at[1 - p], at_z(2 * p - 1))
        else:
            tz_in[3 - p] = send(tz_send.at[p], tz_recv.at[3 - p], at_z(2 * p - 5))

    def table_pass():
        for side in (0, 1):
            tz_relay_in[side].wait_recv()
            tz_half_in[side].wait_recv()
            rows = slice(side * 48, side * 48 + 48)
            tz_own[side] += tz_relay[side].astype(F32)
            tz_own[side, rows, :] += tz_half[side].astype(F32)
            tz_back[side] = tz_own[side].astype(BF16)
            tz_in[2 + side] = send(tz_back.at[side], tz_recv.at[2 + side], at_z(2 - 4 * side))

    def small_pass(got, slot, at, there):
        got[2].wait_recv()
        got[3] = send(slot(2), there(2, 3), at(1))
        got[4] = send(slot(2), there(2, 4), at(2))
        got[-2].wait_recv()
        got[5] = send(slot(-2), there(-2, 5), at(-1))

    def wy_slot(d):
        return wy_recv.at[0, d % 8]

    def w_rows(d):
        place = x * NZ + lax.rem(z - d + NZ, NZ)
        return gw_ref.at[pl.ds(pl.multiple_of(place * 8, 8), 8), pl.ds(pl.multiple_of(core * B, B), B)]

    table_relay(0)
    table_relay(1)
    w_sum = wz_send[w_chunk(0), :]
    wait_for(wz_in, 1, -1, 2, -2)
    for k in range(4):
        w_sum += wz_recv[k]
    wy_recv[0, 0] = w_sum
    wy_in = {d: send(wy_slot(0), wy_slot(d), at_y(d)) for d in (2, -2, 1, -1)}

    table_sum(0)
    low_pass()
    table_relay(2)
    small_pass(wy_in, wy_slot, at_y, lambda here, d: wy_slot(d))
    table_sum(1)
    table_relay(3)
    wait_for(wy_in, 1, -1, 3, 4, 5)
    wy_sib = send(wy_recv.at[0], wy_recv.at[1], sibling)
    table_sum(2)
    low_sum()
    table_pass()

    wy_sib.wait_recv()
    w_sum = wy_recv[0, 0]
    for d in range(1, NY):
        w_sum += wy_recv[0, d]
    for d in range(NY):
        w_sum += wy_recv[1, d]
    w_own[...] = w_sum
    own_lanes = pl.ds(pl.multiple_of(core * B, B), B)
    gw_ref[pl.ds(pl.multiple_of(dp * 8, 8), 8), own_lanes] = w_own[:, own_lanes]
    w_back = {d: send(w_rows(0), w_rows(0), at_z(d)) for d in (2, -2, 1, -1)}

    table_sum(3)
    drain()

    low = lz_own[2, x]
    for d in (1, 3, 2):
        low_x[d].wait_recv()
        low += lx_recv[d].astype(F32)
    part = tz_own[2]
    for k in (1, 0, 2, 3):
        tz_in[k].wait_recv()
        part += tz_recv[k].astype(F32)
    rows = jnp.concatenate([part, low], axis=0).T.astype(BF16)
    t_back[x, 0] = rows[0:96]
    l_back[0, x] = rows[96:]

    def back_slot(d, half):
        if half is None:
            return t_back.at[x, POS[d]]
        return t_back.at[x, POS[d], pl.ds(half * 48, 48), :]

    def low_slot(d, half):
        if half is None:
            return l_back.at[POS[d]]
        return l_back.at[POS[d], pl.ds(2 * half, 2)]

    back = gather_start(back_slot, at_z)
    low_back = [send(l_back.at[0, x], l_back.at[0, x], at_x(d)) for d in (2, 1, 3)]
    near_in, far_in = {}, []

    def to_near(low, high):
        rows = t_back.at[x, pl.ds(low, high - low)]
        for side, step in ((0, 1), (1, -1)):
            near_in[low, side] = send(rows, rows, at_x(step))

    def to_far(low, high):
        middle = {1: None, 2: low + 1, 3: None}[high - low]
        for side, step in ((0, 1), (1, -1)):
            near_in[low, side].wait_recv()
            held = lax.rem(x - step + NX, NX)
            if middle is None:
                rows = t_back.at[held, pl.ds(low, high - low), pl.ds(side * 48, 48), :]
            else:
                rows = t_back.at[held, low + side]
            far_in.append(send(rows, rows, at_x(step)))

    to_near(0, 1)

    small_pass(w_back, w_rows, at_z, lambda here, d: w_rows(here))
    gather_pass(back, back_slot, at_z)
    to_near(1, 3)
    for copy in low_back:
        copy.wait_recv()
    low_back = gather_start(low_slot, at_z)
    wait_for(w_back, 1, -1, 3, 4, 5)
    w_held = gw_ref.at[pl.ds(pl.multiple_of(x * 64, 64), 64), pl.ds(pl.multiple_of(core * B, B), B)]
    w_x = [send(w_held, w_held, at_x(step)) for step in (2, 1, 3)]
    to_far(0, 1)
    wait_for(back, 1, -1)
    to_near(3, 5)
    to_far(1, 3)
    wait_for(back, 3, -3, 4, -4)
    to_near(5, 8)
    gather_pass(low_back, low_slot, at_z)
    to_far(3, 5)

    def rows_of(far, p, d):
        place = (far * NZ + lax.rem(z - d + NZ, NZ)) * B
        table_ref[pl.ds(pl.multiple_of(place, B), 96), :] = t_back[far, p]

    def low_rows_of(p, d):
        for far in range(NX):
            place = (far * NZ + lax.rem(z - d + NZ, NZ)) * B + 96
            table_ref[pl.ds(pl.multiple_of(place, 32), 32), :] = l_back[p, far]

    to_far(5, 8)
    for copy in w_x:
        copy.wait_recv()
    w_half = gw_ref.at[:, pl.ds(pl.multiple_of(core * B, B), B)]
    far_in.append(send(w_half, w_half, sibling))
    for p, d in enumerate(ARRIVE):
        rows_of(x, p, d)
        rows_of(lax.rem(x + 1, NX), p, d)
        rows_of(lax.rem(x + 3, NX), p, d)
    wait_for(low_back, 1, -1, 3, -3, 4, -4)
    for p, d in enumerate(ARRIVE):
        low_rows_of(p, d)
    drain()
    for copy in far_in:
        copy.wait_recv()
    for p, d in enumerate(ARRIVE):
        rows_of(lax.rem(x + 2, NX), p, d)
    drain()


def finish(table_ref, gw_ref, out_ref, gwq_ref, gwi_ref, wide, sem):
    copies = [
        pltpu.make_async_copy(gw_ref.at[pl.ds(0, B), :], gwq_ref, sem.at[8]),
        pltpu.make_async_copy(gw_ref.at[pl.ds(B, B), :], gwi_ref, sem.at[9]),
    ]
    for copy in copies:
        copy.start()
    for i in range(8):
        wide[i] = table_ref[i * 512:(i + 1) * 512, :].astype(F32)
        copies.append(pltpu.make_async_copy(wide.at[i], out_ref.at[pl.ds(i * 512, 512), :], sem.at[i]))
        copies[-1].start()
    for copy in copies:
        copy.wait()


def on_device(q, it, pq, pi, wq, wi, pw, owner, row):
    def vmem(*shape, dtype=F32):
        return pltpu.VMEM(shape, dtype)

    table, gw = pl.pallas_call(
        kernel,
        out_shape=(
            jax.ShapeDtypeStruct((4096, E), BF16),
            jax.ShapeDtypeStruct((2 * B, W), F32),
        ),
        in_specs=[pl.BlockSpec(memory_space=pltpu.HBM)] * 9,
        out_specs=(pl.BlockSpec(memory_space=pltpu.VMEM),) * 2,
        scratch_shapes=[
            vmem(B, E, dtype=BF16),
            vmem(B, E, dtype=BF16),
            vmem(E, W, dtype=BF16),
            vmem(E, W, dtype=BF16),
            vmem(1, B),
            vmem(16, B, dtype=I32),
            vmem(16, B, dtype=I32),
            vmem(NZ * B, W, dtype=BF16),
            vmem(NX * B, W, dtype=BF16),
            vmem(NZ * B, NX * B),
            vmem(NZ * B, NX * B, dtype=BF16),
            vmem(NZ, NX * B),
            vmem(NZ, NX * B),
            vmem(16, B),
            vmem(NX, 16, B),
            vmem(NZ, B, W, dtype=BF16),
            vmem(2, B, W, dtype=BF16),
            vmem(2, 64, W, dtype=BF16),
            vmem(NZ, B, W, dtype=BF16),
            vmem(3, B, W),
            vmem(NX, B, W, dtype=BF16),
            vmem(NX, B, W, dtype=BF16),
            vmem(B, W),
            vmem(256, B),
            vmem(64, 16 * B, dtype=BF16),
            vmem(CAP, 16 * B, dtype=BF16),
            vmem(NT, 64, CAP, dtype=BF16),
            vmem(1024, NT * CAP, dtype=BF16),
            vmem(NT, 2 * B, CAP, dtype=BF16),
            vmem(NT, NX, 16, CAP, dtype=BF16),
            vmem(2, NT, E, B, dtype=BF16),
            vmem(NX * E, NT * CAP, dtype=BF16),
            vmem(2 * B, W),
            vmem(NX, 64, W),
            vmem(64, W),
            vmem(3, 8, W),
            vmem(2, 8, W),
            vmem(4, 8, W),
            vmem(2, NY, 8, W),
            vmem(8, W),
            vmem(4, NX, E, 256),
            vmem(4, NX, E, 256, dtype=BF16),
            vmem(4, 2, 48, 256, dtype=BF16),
            vmem(4, 2, 96, 256, dtype=BF16),
            vmem(4, 2, 96, 256, dtype=BF16),
            vmem(96, B, dtype=BF16),
            vmem(3, 96, B),
            vmem(4, 96, B, dtype=BF16),
            vmem(2, 48, B, dtype=BF16),
            vmem(2, 96, B, dtype=BF16),
            vmem(2, 96, B, dtype=BF16),
            vmem(4, 96, B, dtype=BF16),
            vmem(2, 2, 32, B, dtype=BF16),
            vmem(2, NX, 32, B, dtype=BF16),
            vmem(3, NX, 32, B),
            vmem(2, NX, 32, B, dtype=BF16),
            vmem(4, NX, 32, B, dtype=BF16),
            vmem(NX, 32, B, dtype=BF16),
            vmem(NX, 32, B, dtype=BF16),
            vmem(NX, NZ, 96, E, dtype=BF16),
            vmem(NZ, NX, 32, E, dtype=BF16),
            pltpu.SemaphoreType.DMA((9,)),
            pltpu.SemaphoreType.DMA((N_COPIES,)),
            pltpu.SemaphoreType.DMA((N_COPIES,)),
        ],
        compiler_params=pltpu.CompilerParams(
            collective_id=0, has_side_effects=True, vmem_limit_bytes=40 * 1024 * 1024
        ),
    )(*[
        pltpu.with_memory_space_constraint(a, pltpu.HBM)
        for a in (
            q, it, pq, pi, wq, wi, pw.reshape(1, B), owner.reshape(B, 16).T, row.reshape(B, 16).T
        )
    ])
    return pl.pallas_call(
        finish,
        out_shape=(
            jax.ShapeDtypeStruct((4096, E), F32),
            jax.ShapeDtypeStruct((B, W), F32),
            jax.ShapeDtypeStruct((B, W), F32),
        ),
        in_specs=[pl.BlockSpec(memory_space=pltpu.VMEM)] * 2,
        out_specs=(pl.BlockSpec(memory_space=pltpu.HBM),) * 3,
        scratch_shapes=[vmem(8, 512, E), pltpu.SemaphoreType.DMA((10,))],
        compiler_params=pltpu.CompilerParams(vmem_limit_bytes=12 * 1024 * 1024),
    )(table, gw)


def solution(mesh):
    both = ("dp", "table")
    placed = (
        P(both, None),
        P(both, None),
        P(both, None),
        P(both, None),
        P(),
        P(),
        P(both),
        P(both, None, None),
        P(both, None, None),
    )
    return jax.shard_map(
        on_device,
        mesh=mesh,
        in_specs=placed,
        out_specs=(P("table", None), P(), P()),
        check_vma=False,
    )
```

```python
import math

import jax
import jax.numpy as jnp
from jax import lax
from jax.experimental import pallas as pl
from jax.experimental.pallas import tpu as pltpu
from jax.sharding import PartitionSpec as P

MESH = pl.DeviceIdType.MESH
F32, BF16, I32 = jnp.float32, jnp.bfloat16, jnp.int32
NX, NZ, NY = 4, 8, 8
B, W, E = 128, 256, 128
NT = 2 * NY
CAP = 256
SCALE = 1.0 / math.sqrt(W)
N_COPIES = 176

NN = (((1,), (0,)), ((), ()))
NT_DIMS = (((1,), (1,)), ((), ()))
TN = (((0,), (0,)), ((), ()))


def dot(a, b, dims=NN):
    return lax.dot_general(a, b, dims, preferred_element_type=F32)


def iota(shape, dim):
    return lax.broadcasted_iota(I32, shape, dim)


ARRIVE = (0, 2, 6, 1, 7, 3, 5, 4)
POS = {d: p for p, d in enumerate(ARRIVE)}
OWN = (0, 1, 2, 3, 4, 10, 11, 12)
SIB = (5, 6, 7, 8, 9, 13, 14, 15)
FIRST = 10 * CAP


def kernel(
    q_ref, it_ref, pq_ref, pi_ref, wq_ref, wi_ref, pw_ref, ow_ref, rw_ref,
    table_ref, gw_ref,
    pq, pi, wq, wi, pw, ow, rw,
    ibuf, qbuf, ebuf, gbuf, tops, totals, st_send, st_recv,
    gi_send, gi_relay, gi_half, gi_recv, gi_own, gq_send, gq_recv, gq_own,
    taken, slots_a, slots_b, lists, onehot, select, factor, pooled, values,
    w_part, wx_recv, wz_send, wz_relay, wz_pass, wz_recv, wy_recv, w_own,
    t_own, t_send, tx_half, tx_relay, tx_recv, tz_first, tz_own, tz_send, tz_half, tz_relay, tz_back, tz_recv,
    lz_half, lz_relay, lz_own, lz_send, lz_recv, lx_send, lx_recv, t_back, l_back,
    load_sem, send_sem, recv_sem,
):
    dp, tb = lax.axis_index("dp"), lax.axis_index("table")
    x, z = lax.div(dp, NZ), lax.rem(dp, NZ)
    y, core = lax.div(tb, 2), lax.rem(tb, 2)

    def at_x(d):
        return (lax.rem(x + d + NX, NX) * NZ + z, tb)

    def at_z(d):
        return (x * NZ + lax.rem(z + d + NZ, NZ), tb)

    def at_y(d):
        return (dp, lax.rem(y + d + NY, NY) * 2 + core)

    sibling = (dp, tb + 1 - 2 * core)
    partners = (
        [at_x(d) for d in range(1, NX)]
        + [at_z(d) for d in (1, 2, -1, -2)]
        + [at_y(d) for d in (1, 2, -1, -2)]
        + [sibling]
    )
    barrier = pltpu.get_barrier_semaphore()
    for partner in partners:
        pl.semaphore_signal(barrier, inc=1, device_id=partner, device_id_type=MESH)
    loads = [
        pltpu.make_async_copy(src, dst, load_sem.at[i])
        for i, (src, dst) in enumerate((
            (it_ref, ibuf.at[pl.ds(0, B), :]),
            (q_ref, qbuf.at[pl.ds(0, B), :]),
            (ow_ref, ow),
            (rw_ref, rw),
            (pw_ref, pw),
            (pq_ref, pq),
            (pi_ref, pi),
            (wq_ref, wq),
            (wi_ref, wi),
        ))
    ]
    for load in loads:
        load.start()
    pl.semaphore_wait(barrier, len(partners))

    copies, drained = [], [0]

    def remote(index, src, dst, device):
        return pltpu.make_async_remote_copy(
            src_ref=src,
            dst_ref=dst,
            send_sem=send_sem.at[index],
            recv_sem=recv_sem.at[index],
            device_id=device,
            device_id_type=MESH,
        )

    def send(src, dst, device):
        copy = remote(len(copies), src, dst, device)
        copy.start()
        copies.append(copy)
        return copy

    def drain():
        for copy in copies[drained[0]:]:
            copy.wait_send()
        drained[0] = len(copies)

    def gather_start(slot, at, source=None):
        source = slot(0, None) if source is None else source
        return {d: send(source, slot(d % 8, None), at(d)) for d in (2, -2, 1, -1)}

    def gather_pass(got, slot, at):
        got[2].wait_recv()
        got[3] = send(slot(2, None), slot(3, None), at(1))
        got[4] = send(slot(2, 0), slot(4, 0), at(2))
        got[-2].wait_recv()
        got[-3] = send(slot(6, None), slot(5, None), at(-1))
        got[-4] = send(slot(6, 1), slot(4, 1), at(-2))

    def wait_for(got, *names):
        for name in names:
            got[name].wait_recv()

    def item_slot(d, half):
        if half is None:
            return ibuf.at[pl.ds(POS[d] * B, B), :]
        return ibuf.at[pl.ds(POS[d] * B + half * 64, 64), :]

    item_in = gather_start(item_slot, at_z, it_ref)
    query_in = {}
    for d in (1, 3, 2):
        query_in[d] = send(q_ref, qbuf.at[pl.ds(d * B, B), :], at_x(d))

    for load in loads:
        load.wait()
    owner_row = iota((NT, B), 0)
    hits = jnp.concatenate([(ow[k:k + 1, :] == owner_row).astype(F32) for k in range(16)], axis=0)
    before = (iota((B, 2 * B), 0) < iota((B, 2 * B), 1)).astype(BF16)
    counts = dot(hits.astype(BF16), before)
    at_row, at_col = iota((256, 256), 0), iota((256, 256), 1)
    earlier = jnp.logical_and(
        lax.bitwise_and(at_row, 15) == lax.bitwise_and(at_col, 15),
        lax.shift_right_logical(at_col, 4) < lax.shift_right_logical(at_row, 4),
    ).astype(BF16)
    taken[...] = (counts[:, 0:B] + dot(earlier, counts[:, B:].astype(BF16))) * hits
    list_row = iota((64, B), 0)
    list_owner, piece = lax.bitwise_and(list_row, 15), lax.shift_right_logical(list_row, 4)
    pair = iota((1, B), 1)
    place = iota((CAP, B), 0)

    def list_slot(k, _):
        lanes = pl.ds(pl.multiple_of(k * B, B), B)
        ranks = taken[pl.ds(pl.multiple_of(k * NT, NT), NT), :]
        rank = jnp.sum(ranks, axis=0, keepdims=True).astype(I32)
        slots_b[:, lanes] = (place == rank).astype(BF16)
        owner, row = ow[pl.ds(k, 1), :], rw[pl.ds(k, 1), :]
        part = jnp.where(
            piece == 0,
            pair + lax.div(k, 8) * B,
            jnp.where(
                piece == 1,
                lax.shift_right_logical(row, 8) + 1,
                jnp.where(piece == 2, lax.bitwise_and(row, 255), 0),
            ),
        )
        slots_a[:, lanes] = jnp.where(list_owner == owner, part, 0).astype(F32).astype(BF16)
        return 0

    lax.fori_loop(0, 16, list_slot, 0)
    lists[0] = dot(slots_a[...], slots_b[...], NT_DIMS).astype(BF16)

    def list_slot_of(d, half):
        if half is None:
            return lists.at[OWN[POS[d]]]
        return lists.at[OWN[POS[d]], pl.ds(half * 32, 32), :]

    list_in = gather_start(list_slot_of, at_y)
    gather_pass(item_in, item_slot, at_z)

    wait_for(query_in, 1, 3, 2)

    def logits(p, _):
        rows = pl.ds(pl.multiple_of(p * B, B), B)
        block = SCALE * dot(ibuf[rows, :], qbuf[...], NT_DIMS)
        top = jnp.max(block, axis=0, keepdims=True)
        block = jnp.exp(block - top)
        ebuf[rows, :] = block
        tops[pl.ds(p, 1), :] = top
        totals[pl.ds(p, 1), :] = jnp.sum(block, axis=0, keepdims=True)
        return 0

    wait_for(item_in, 1, -1)
    lax.fori_loop(0, 5, logits, 0, unroll=True)
    wait_for(item_in, 3, -3)
    lax.fori_loop(5, 7, logits, 0, unroll=True)
    wait_for(item_in, 4, -4)
    logits(7, 0)

    top = jnp.max(tops[...], axis=0, keepdims=True)
    total = jnp.sum(totals[...] * jnp.exp(tops[...] - top), axis=0, keepdims=True)
    weight = pw[...]
    for k in range(NX):
        st_send[k:k + 1, :] = top[:, k * B:(k + 1) * B]
        st_send[NX + k:NX + k + 1, :] = total[:, k * B:(k + 1) * B]
    st_send[8:16, :] = jnp.broadcast_to(weight, (8, B))
    stat_in = {d: send(st_send, st_recv.at[d], at_x(d)) for d in (2, 1, 3)}
    gather_pass(list_in, list_slot_of, at_y)
    wait_for(stat_in, 1, 3, 2)
    maxima, factors = [], []
    for k in range(NX):
        part_tops, part_totals = [st_send[k:k + 1, :]], [st_send[NX + k:NX + k + 1, :]]
        for d in range(1, NX):
            j = (k - d) % NX
            part_tops.append(st_recv[d, j:j + 1, :])
            part_totals.append(st_recv[d, NX + j:NX + j + 1, :])
        row_max = part_tops[0]
        for t in part_tops[1:]:
            row_max = jnp.maximum(row_max, t)
        row_total = sum(s * jnp.exp(t - row_max) for t, s in zip(part_tops, part_totals))
        maxima.append(row_max)
        factors.append((weight if k == 0 else st_recv[k, 8:9, :]) / row_total)
    row_max, factors = jnp.concatenate(maxima, axis=1), jnp.concatenate(factors, axis=1)
    totals[...] = factors * jnp.exp(tops[...] - row_max)

    def item_terms(p):
        rows = pl.ds(pl.multiple_of(p * B, B), B)
        block = (ebuf[rows, :] * totals[pl.ds(p, 1), :]).astype(BF16)
        gbuf[rows, :] = block
        return SCALE * dot(block, qbuf[...])

    def far_terms(p, _):
        gi_send[p] = item_terms(p).astype(BF16)
        return 0

    def near_terms(p, _):
        gi_own[p] = item_terms(p)
        return 0

    far_terms(7, 0)
    half_in = [
        send(gi_send.at[7, pl.ds(0, 64), :], gi_half.at[0], at_z(2)),
        send(gi_send.at[7, pl.ds(64, 64), :], gi_half.at[1], at_z(-2)),
    ]
    lax.fori_loop(5, 7, far_terms, 0, unroll=True)
    relay_in = [
        send(gi_send.at[POS[5]], gi_relay.at[0], at_z(1)),
        send(gi_send.at[POS[3]], gi_relay.at[1], at_z(-1)),
    ]
    lax.fori_loop(3, 5, far_terms, 0, unroll=True)
    grad_in = {d: send(gi_send.at[POS[d]], gi_recv.at[POS[d]], at_z(-d)) for d in (7, 1)}
    lax.fori_loop(0, 3, near_terms, 0, unroll=True)
    same = iota((B, B), 0) == iota((B, B), 1)
    diagonal = ebuf[0:B, 0:B] * totals[0:1, 0:B] - jnp.where(same, weight, 0.0)
    gbuf[0:B, 0:B] = diagonal.astype(BF16)
    gi_own[0] = SCALE * dot(gbuf[0:B, :], qbuf[...])

    terms = SCALE * dot(gbuf[...], ibuf[...], TN)
    gq_own[...] = terms[0:B, :]
    for k in range(1, NX):
        gq_send[k] = terms[k * B:(k + 1) * B, :].astype(BF16)
    query_grad_in = {k: send(gq_send.at[k], gq_recv.at[k], at_x(-k)) for k in (2, 1, 3)}
    for side, (d, rows) in enumerate(((6, slice(0, 64)), (2, slice(64, 128)))):
        p = POS[d]
        relay_in[side].wait_recv()
        half_in[side].wait_recv()
        gi_own[p] += gi_relay[side].astype(F32)
        gi_own[p, rows, :] += gi_half[side].astype(F32)
        gi_send[p] = gi_own[p].astype(BF16)
        grad_in[d] = send(gi_send.at[p], gi_recv.at[p], at_z(-d))

    list_sib = []

    def lists_to_sibling(low, high):
        list_sib.append(send(
            lists.at[pl.ds(OWN[low], high - low)], lists.at[pl.ds(SIB[low], high - low)], sibling
        ))

    wait_for(list_in, 1, -1, 3, -3, 4, -4)
    lists_to_sibling(0, 5)
    lists_to_sibling(5, 8)
    source_row = iota((2 * B, CAP), 0)
    owner_row = iota((NT, CAP), 0)
    low_row = lax.bitwise_and(iota((1152, CAP), 0), 1023)

    def one_hots(s, _):
        entry = lists[s].astype(F32)
        source, high, low = [
            jnp.sum(jnp.where(owner_row == tb, entry[16 * k:16 * k + 16, :], 0.0), axis=0, keepdims=True).astype(I32)
            for k in range(3)
        ]
        row = (high - 1) * 256 + low
        select[s] = (source == source_row).astype(BF16)
        lanes = pl.ds(pl.multiple_of(s * CAP, CAP), CAP)
        onehot[:, lanes] = (lax.bitwise_and(row, 1023) == low_row).astype(BF16)
        block = jnp.broadcast_to(lax.shift_right_arithmetic(row, 10), (16, CAP))
        for j in range(NX):
            factor[s, j] = (block == j).astype(BF16)
        return 0

    lax.fori_loop(0, 5, one_hots, 0)
    lax.fori_loop(10, 13, one_hots, 0)

    query_grad = gq_own[...]
    for k in (1, 3, 2):
        query_grad_in[k].wait_recv()
        query_grad += gq_recv[k].astype(F32)
    query_grad = query_grad.astype(BF16)

    pooled_in, pooled_sib = {}, {}

    def pooled_slot(half):
        def slot(d, rows):
            if rows is None:
                return pooled.at[half, OWN[POS[d]]]
            return pooled.at[half, OWN[POS[d]], pl.ds(rows * 64, 64), :]

        return slot

    def to_sibling(half, low, high):
        pooled_sib[half, low] = send(
            pooled.at[half, pl.ds(OWN[low], high - low)], pooled.at[half, pl.ds(SIB[low], high - low)], sibling
        )

    pooled[0, 0] = dot(wq[...], query_grad, NT_DIMS).astype(BF16)
    pooled_in[0] = gather_start(pooled_slot(0), at_y)
    to_sibling(0, 0, 1)
    w_part[0:B, :] = dot(pq[...], query_grad, TN)

    for copy in list_sib:
        copy.wait_recv()
    lax.fori_loop(5, 10, one_hots, 0)
    lax.fori_loop(13, 16, one_hots, 0)
    drain()

    item_grad = gi_own[0]
    for d in (1, 7, 2, 6):
        grad_in[d].wait_recv()
        item_grad += gi_recv[POS[d]].astype(F32)
    item_grad = item_grad.astype(BF16)
    pooled[1, 0] = dot(wi[...], item_grad, NT_DIMS).astype(BF16)
    pooled_in[1] = gather_start(pooled_slot(1), at_y)
    to_sibling(1, 0, 1)
    gather_pass(pooled_in[0], pooled_slot(0), at_y)
    wait_for(pooled_in[0], 1, -1)
    to_sibling(0, 1, 3)
    to_sibling(0, 3, 5)
    w_part[B:, :] = dot(pi[...], item_grad, TN)
    w_in = {}
    for d in (2, 1, 3):
        to_x = lax.rem(x + d, NX)
        w_in[d] = send(w_part.at[pl.ds(pl.multiple_of(to_x * 64, 64), 64), :], wx_recv.at[d], at_x(d))

    def place_values(s, _):
        got = (dot(pooled[0, s], select[s, 0:B, :]) + dot(pooled[1, s], select[s, B:, :])).astype(BF16)
        lanes = pl.ds(pl.multiple_of(s * CAP, CAP), CAP)
        for j in range(NX):
            values[j * E:(j + 1) * E, lanes] = got * jnp.tile(factor[s, j], (8, 1))
        return 0

    def quarter_rows(p):
        return pl.ds(pl.multiple_of(lax.rem(z + 4 + 3 * p * (p + 1), NZ) * B, B), 256)

    def first_part(p, _):
        part = dot(values[:, 0:FIRST], onehot[quarter_rows(p), 0:FIRST], NT_DIMS)
        t_own[p] = part.reshape(NX, E, 256)
        return 0

    gather_pass(pooled_in[1], pooled_slot(1), at_y)
    wait_for(pooled_in[1], 1, -1)
    to_sibling(1, 1, 3)
    to_sibling(1, 3, 5)
    lax.fori_loop(0, 5, place_values, 0, unroll=True)
    for low in (0, 1, 3):
        pooled_sib[0, low].wait_recv()
        pooled_sib[1, low].wait_recv()
    lax.fori_loop(5, 10, place_values, 0, unroll=True)

    lax.fori_loop(0, 2, first_part, 0)
    wait_for(pooled_in[0], 3, -3, 4, -4)
    to_sibling(0, 5, 8)
    wait_for(pooled_in[1], 3, -3, 4, -4)
    to_sibling(1, 5, 8)
    lax.fori_loop(10, 13, place_values, 0, unroll=True)
    w_sum = w_part[pl.ds(pl.multiple_of(x * 64, 64), 64), :]
    for d in (1, 3, 2):
        w_in[d].wait_recv()
        w_sum += wx_recv[d]
    wz_send[...] = w_sum

    def w_chunk(d):
        return pl.ds(pl.multiple_of(lax.rem(z + d + NZ, NZ) * 8, 8), 8)

    wz_in = {}
    for d, via, dst in (
        (4, 2, wz_relay.at[0]), (3, 1, wz_relay.at[1]), (-3, -1, wz_relay.at[2]),
        (1, 1, wz_recv.at[0]), (-1, -1, wz_recv.at[1]),
    ):
        wz_in[d] = send(wz_send.at[w_chunk(d), :], dst, at_z(via))

    lax.fori_loop(2, 4, first_part, 0)
    pooled_sib[0, 5].wait_recv()
    pooled_sib[1, 5].wait_recv()
    lax.fori_loop(13, 16, place_values, 0, unroll=True)

    half_base = len(copies)
    copies.extend([None] * 8)

    def half_copy(p, side):
        return remote(
            half_base + 2 * p + side,
            t_send.at[p, lax.rem(x + 2, NX), pl.ds(side * 48, 48), :],
            tx_half.at[p, side],
            at_x(1 - 2 * side),
        )

    def send_part(p, part):
        part = t_own[p] + part.reshape(NX, E, 256)
        t_own[p] = part
        t_send[p] = part.astype(BF16)
        half_copy(p, 0).start()
        half_copy(p, 1).start()

    def last_part(p, _):
        send_part(p, dot(values[:, FIRST:], onehot[quarter_rows(p), FIRST:], NT_DIMS))
        return 0

    lax.fori_loop(0, 4, last_part, 0)
    for p in range(4):
        for side in (0, 1):
            copies[half_base + 2 * p + side] = half_copy(p, side)

    def low_columns(p, side):
        return t_send.at[p, :, pl.ds(96, 32), pl.ds(side * B, B)]

    low_half = [
        send(t_send.at[0, pl.ds(2 * side, 2), pl.ds(96, 32), pl.ds(0, B)], lz_half.at[side], at_z(2 - 4 * side))
        for side in (0, 1)
    ]
    low_relay = [
        send(low_columns(1, 1), lz_relay.at[0], at_z(1)),
        send(low_columns(0, 1), lz_relay.at[1], at_z(-1)),
    ]
    low_in = [
        send(low_columns(3, 1), lz_recv.at[0], at_z(1)),
        send(low_columns(2, 1), lz_recv.at[1], at_z(-1)),
    ]

    def low_pass():
        for side in (0, 1):
            low_relay[side].wait_recv()
            low_half[side].wait_recv()
            lz_own[side] = t_own[1 + side, :, 96:, 0:B] + lz_relay[side].astype(F32)
            pair_of = slice(2 * side, 2 * side + 2)
            lz_own[side, pair_of] += lz_half[side].astype(F32)
            lz_send[side] = lz_own[side].astype(BF16)
            low_in.append(send(lz_send.at[side], lz_recv.at[2 + side], at_z(2 - 4 * side)))

    low_x = {}

    def low_sum():
        part = t_own[3, :, 96:, 0:B]
        for k in range(4):
            low_in[k].wait_recv()
            part += lz_recv[k].astype(F32)
        lz_own[2] = part
        lx_send[...] = part.astype(BF16)
        for d in (2, 1, 3):
            low_x[d] = send(lx_send.at[lax.rem(x + d, NX)], lx_recv.at[d], at_x(d))

    relay_in, tz_half_in, tz_relay_in, tz_in = {}, {}, {}, {}

    def table_relay(p):
        for side, step in ((0, 1), (1, -1)):
            copies[half_base + 2 * p + side].wait_recv()
            near = lax.rem(x + step + NX, NX)
            for half in (0, 1):
                rows = slice(half * 48, half * 48 + 48)
                part = t_own[p, near, rows, :]
                if half == side:
                    part += tx_half[p, side].astype(F32)
                tx_relay[p, side, rows, :] = part.astype(BF16)
            relay_in[p, side] = send(tx_relay.at[p, side], tx_recv.at[p, side], at_x(step))

    def table_sum(p):
        part = t_own[p, x, 0:96, :]
        for side in (0, 1):
            relay_in[p, side].wait_recv()
            part += tx_recv[p, side].astype(F32)
        tz_send[p] = part[:, B:].astype(BF16)
        if p == 0:
            tz_first[...] = part[:, 0:B].astype(BF16)
            for side in (0, 1):
                tz_half_in[side] = send(
                    tz_first.at[pl.ds(side * 48, 48), :], tz_half.at[side], at_z(2 - 4 * side)
                )
        else:
            tz_own[p - 1] = part[:, 0:B]
        if p < 2:
            tz_relay_in[1 - p] = send(tz_send.at[p], tz_relay.at[1 - p], at_z(2 * p - 1))
        else:
            tz_in[3 - p] = send(tz_send.at[p], tz_recv.at[3 - p], at_z(2 * p - 5))

    def table_pass():
        for side in (0, 1):
            tz_relay_in[side].wait_recv()
            tz_half_in[side].wait_recv()
            rows = slice(side * 48, side * 48 + 48)
            tz_own[side] += tz_relay[side].astype(F32)
            tz_own[side, rows, :] += tz_half[side].astype(F32)
            tz_back[side] = tz_own[side].astype(BF16)
            tz_in[2 + side] = send(tz_back.at[side], tz_recv.at[2 + side], at_z(2 - 4 * side))

    wait_for(wz_in, 4, 3, -3)
    wz_pass[0] = wz_send[w_chunk(2), :] + wz_relay[0] + wz_relay[1]
    wz_pass[1] = wz_send[w_chunk(-2), :] + wz_relay[2]
    for side, d in ((0, 2), (1, -2)):
        wz_in[d] = send(wz_pass.at[side], wz_recv.at[2 + side], at_z(d))

    def small_pass(got, slot, at, there):
        got[2].wait_recv()
        got[3] = send(slot(2), there(2, 3), at(1))
        got[4] = send(slot(2), there(2, 4), at(2))
        got[-2].wait_recv()
        got[5] = send(slot(-2), there(-2, 5), at(-1))

    def wy_slot(d):
        return wy_recv.at[0, d % 8]

    def w_rows(d):
        place = x * NZ + lax.rem(z - d + NZ, NZ)
        return gw_ref.at[pl.ds(pl.multiple_of(place * 8, 8), 8), pl.ds(pl.multiple_of(core * B, B), B)]

    table_relay(0)
    table_relay(1)
    w_sum = wz_send[w_chunk(0), :]
    wait_for(wz_in, 1, -1, 2, -2)
    for k in range(4):
        w_sum += wz_recv[k]
    wy_recv[0, 0] = w_sum
    wy_in = {d: send(wy_slot(0), wy_slot(d), at_y(d)) for d in (2, -2, 1, -1)}

    table_sum(0)
    low_pass()
    table_relay(2)
    small_pass(wy_in, wy_slot, at_y, lambda here, d: wy_slot(d))
    table_sum(1)
    table_relay(3)
    wait_for(wy_in, 1, -1, 3, 4, 5)
    wy_sib = send(wy_recv.at[0], wy_recv.at[1], sibling)
    table_sum(2)
    low_sum()
    table_pass()

    wy_sib.wait_recv()
    w_sum = wy_recv[0, 0]
    for d in range(1, NY):
        w_sum += wy_recv[0, d]
    for d in range(NY):
        w_sum += wy_recv[1, d]
    w_own[...] = w_sum
    own_lanes = pl.ds(pl.multiple_of(core * B, B), B)
    gw_ref[pl.ds(pl.multiple_of(dp * 8, 8), 8), own_lanes] = w_own[:, own_lanes]
    w_back = {d: send(w_rows(0), w_rows(0), at_z(d)) for d in (2, -2, 1, -1)}

    table_sum(3)
    drain()

    low = lz_own[2, x]
    for d in (1, 3, 2):
        low_x[d].wait_recv()
        low += lx_recv[d].astype(F32)
    part = tz_own[2]
    for k in (1, 0, 2, 3):
        tz_in[k].wait_recv()
        part += tz_recv[k].astype(F32)
    rows = jnp.concatenate([part, low], axis=0).T.astype(BF16)
    t_back[x, 0] = rows[0:96]
    l_back[0, x] = rows[96:]

    def back_slot(d, half):
        if half is None:
            return t_back.at[x, POS[d]]
        return t_back.at[x, POS[d], pl.ds(half * 48, 48), :]

    def low_slot(d, half):
        if half is None:
            return l_back.at[POS[d]]
        return l_back.at[POS[d], pl.ds(2 * half, 2)]

    back = gather_start(back_slot, at_z)
    low_back = [send(l_back.at[0, x], l_back.at[0, x], at_x(d)) for d in (2, 1, 3)]
    near_in, far_in = {}, []

    def to_near(low, high):
        rows = t_back.at[x, pl.ds(low, high - low)]
        for side, step in ((0, 1), (1, -1)):
            near_in[low, side] = send(rows, rows, at_x(step))

    def to_far(low, high):
        middle = {1: None, 2: low + 1, 3: None}[high - low]
        for side, step in ((0, 1), (1, -1)):
            near_in[low, side].wait_recv()
            held = lax.rem(x - step + NX, NX)
            if middle is None:
                rows = t_back.at[held, pl.ds(low, high - low), pl.ds(side * 48, 48), :]
            else:
                rows = t_back.at[held, low + side]
            far_in.append(send(rows, rows, at_x(step)))

    to_near(0, 1)

    small_pass(w_back, w_rows, at_z, lambda here, d: w_rows(here))
    gather_pass(back, back_slot, at_z)
    to_near(1, 3)
    for copy in low_back:
        copy.wait_recv()
    low_back = gather_start(low_slot, at_z)
    wait_for(w_back, 1, -1, 3, 4, 5)
    w_held = gw_ref.at[pl.ds(pl.multiple_of(x * 64, 64), 64), pl.ds(pl.multiple_of(core * B, B), B)]
    w_x = [send(w_held, w_held, at_x(step)) for step in (2, 1, 3)]
    to_far(0, 1)
    wait_for(back, 1, -1)
    to_near(3, 5)
    to_far(1, 3)
    wait_for(back, 3, -3, 4, -4)
    to_near(5, 8)
    gather_pass(low_back, low_slot, at_z)
    to_far(3, 5)

    def rows_of(far, p, d):
        place = (far * NZ + lax.rem(z - d + NZ, NZ)) * B
        table_ref[pl.ds(pl.multiple_of(place, B), 96), :] = t_back[far, p]

    def low_rows_of(p, d):
        for far in range(NX):
            place = (far * NZ + lax.rem(z - d + NZ, NZ)) * B + 96
            table_ref[pl.ds(pl.multiple_of(place, 32), 32), :] = l_back[p, far]

    to_far(5, 8)
    for copy in w_x:
        copy.wait_recv()
    w_half = gw_ref.at[:, pl.ds(pl.multiple_of(core * B, B), B)]
    far_in.append(send(w_half, w_half, sibling))
    for p, d in enumerate(ARRIVE):
        rows_of(x, p, d)
        rows_of(lax.rem(x + 1, NX), p, d)
        rows_of(lax.rem(x + 3, NX), p, d)
    wait_for(low_back, 1, -1, 3, -3, 4, -4)
    for p, d in enumerate(ARRIVE):
        low_rows_of(p, d)
    drain()
    for copy in far_in:
        copy.wait_recv()
    for p, d in enumerate(ARRIVE):
        rows_of(lax.rem(x + 2, NX), p, d)
    drain()


def finish(table_ref, gw_ref, out_ref, gwq_ref, gwi_ref, wide, sem):
    copies = [
        pltpu.make_async_copy(gw_ref.at[pl.ds(0, B), :], gwq_ref, sem.at[8]),
        pltpu.make_async_copy(gw_ref.at[pl.ds(B, B), :], gwi_ref, sem.at[9]),
    ]
    for copy in copies:
        copy.start()
    for i in range(8):
        wide[i] = table_ref[i * 512:(i + 1) * 512, :].astype(F32)
        copies.append(pltpu.make_async_copy(wide.at[i], out_ref.at[pl.ds(i * 512, 512), :], sem.at[i]))
        copies[-1].start()
    for copy in copies:
        copy.wait()


def on_device(q, it, pq, pi, wq, wi, pw, owner, row):
    def vmem(*shape, dtype=F32):
        return pltpu.VMEM(shape, dtype)

    table, gw = pl.pallas_call(
        kernel,
        out_shape=(
            jax.ShapeDtypeStruct((4096, E), BF16),
            jax.ShapeDtypeStruct((2 * B, W), F32),
        ),
        in_specs=[pl.BlockSpec(memory_space=pltpu.HBM)] * 9,
        out_specs=(pl.BlockSpec(memory_space=pltpu.VMEM),) * 2,
        scratch_shapes=[
            vmem(B, E, dtype=BF16),
            vmem(B, E, dtype=BF16),
            vmem(E, W, dtype=BF16),
            vmem(E, W, dtype=BF16),
            vmem(1, B),
            vmem(16, B, dtype=I32),
            vmem(16, B, dtype=I32),
            vmem(NZ * B, W, dtype=BF16),
            vmem(NX * B, W, dtype=BF16),
            vmem(NZ * B, NX * B),
            vmem(NZ * B, NX * B, dtype=BF16),
            vmem(NZ, NX * B),
            vmem(NZ, NX * B),
            vmem(16, B),
            vmem(NX, 16, B),
            vmem(NZ, B, W, dtype=BF16),
            vmem(2, B, W, dtype=BF16),
            vmem(2, 64, W, dtype=BF16),
            vmem(NZ, B, W, dtype=BF16),
            vmem(3, B, W),
            vmem(NX, B, W, dtype=BF16),
            vmem(NX, B, W, dtype=BF16),
            vmem(B, W),
            vmem(256, B),
            vmem(64, 16 * B, dtype=BF16),
            vmem(CAP, 16 * B, dtype=BF16),
            vmem(NT, 64, CAP, dtype=BF16),
            vmem(1152, NT * CAP, dtype=BF16),
            vmem(NT, 2 * B, CAP, dtype=BF16),
            vmem(NT, NX, 16, CAP, dtype=BF16),
            vmem(2, NT, E, B, dtype=BF16),
            vmem(NX * E, NT * CAP, dtype=BF16),
            vmem(2 * B, W),
            vmem(NX, 64, W),
            vmem(64, W),
            vmem(3, 8, W),
            vmem(2, 8, W),
            vmem(4, 8, W),
            vmem(2, NY, 8, W),
            vmem(8, W),
            vmem(4, NX, E, 256),
            vmem(4, NX, E, 256, dtype=BF16),
            vmem(4, 2, 48, 256, dtype=BF16),
            vmem(4, 2, 96, 256, dtype=BF16),
            vmem(4, 2, 96, 256, dtype=BF16),
            vmem(96, B, dtype=BF16),
            vmem(3, 96, B),
            vmem(4, 96, B, dtype=BF16),
            vmem(2, 48, B, dtype=BF16),
            vmem(2, 96, B, dtype=BF16),
            vmem(2, 96, B, dtype=BF16),
            vmem(4, 96, B, dtype=BF16),
            vmem(2, 2, 32, B, dtype=BF16),
            vmem(2, NX, 32, B, dtype=BF16),
            vmem(3, NX, 32, B),
            vmem(2, NX, 32, B, dtype=BF16),
            vmem(4, NX, 32, B, dtype=BF16),
            vmem(NX, 32, B, dtype=BF16),
            vmem(NX, 32, B, dtype=BF16),
            vmem(NX, NZ, 96, E, dtype=BF16),
            vmem(NZ, NX, 32, E, dtype=BF16),
            pltpu.SemaphoreType.DMA((9,)),
            pltpu.SemaphoreType.DMA((N_COPIES,)),
            pltpu.SemaphoreType.DMA((N_COPIES,)),
        ],
        compiler_params=pltpu.CompilerParams(
            collective_id=0, has_side_effects=True, vmem_limit_bytes=40 * 1024 * 1024
        ),
    )(*[
        pltpu.with_memory_space_constraint(a, pltpu.HBM)
        for a in (
            q, it, pq, pi, wq, wi, pw.reshape(1, B), owner.reshape(B, 16).T, row.reshape(B, 16).T
        )
    ])
    return pl.pallas_call(
        finish,
        out_shape=(
            jax.ShapeDtypeStruct((4096, E), F32),
            jax.ShapeDtypeStruct((B, W), F32),
            jax.ShapeDtypeStruct((B, W), F32),
        ),
        in_specs=[pl.BlockSpec(memory_space=pltpu.VMEM)] * 2,
        out_specs=(pl.BlockSpec(memory_space=pltpu.HBM),) * 3,
        scratch_shapes=[vmem(8, 512, E), pltpu.SemaphoreType.DMA((10,))],
        compiler_params=pltpu.CompilerParams(vmem_limit_bytes=12 * 1024 * 1024),
    )(table, gw)


def solution(mesh):
    both = ("dp", "table")
    placed = (
        P(both, None),
        P(both, None),
        P(both, None),
        P(both, None),
        P(),
        P(),
        P(both),
        P(both, None, None),
        P(both, None, None),
    )
    return jax.shard_map(
        on_device,
        mesh=mesh,
        in_specs=placed,
        out_specs=(P("table", None), P(), P()),
        check_vma=False,
    )
```
